128 devices in a mesh: chan: 8 (over z_hi, y), bl: 16 (over x, z_lo, core).
Axes of the slice: x: 4, y: 4, z: 4 (z_hi: 2, z_lo: 2; z = z_hi * 2 + z_lo), core: 2. Of those that a mesh axis runs over, the one named last changes fastest.
Arguments:
- coherency: bfloat16 [8, 32, 8, 16384], P('chan', None, None, 'bl'), may hold values from -1.5 to 1.5
- visibilities: float32 [8, 8, 16384], P('chan', None, 'bl'), may hold values from -6 to 6
- station_pairs: int32 [2, 16384], P(None, 'bl'), may hold values from 0 to 511, as said below
- gains: float32 [8, 32, 8, 512], P('chan', None, None, 'bl'), may hold values from -4 to 4
- duals: float32 [8, 32, 8, 512], P('chan', None, None, 'bl'), may hold values from -5 to 5
- poly: float32 [32, 8, 4, 512], P(None, None, None, 'bl'), may hold values from -4 to 4
- penalty: float32 [32], replicated, may hold values from 2 to 20
Outputs:
- gains_out: float32 [8, 32, 8, 512], P('chan', None, None, 'bl')
- duals_out: float32 [8, 32, 8, 512], P('chan', None, None, 'bl')
- poly_out: float32 [32, 8, 4, 512], P(None, None, None, 'bl')
The draws below stay inside these ranges and needn't reach their ends.
Inputs may be any that keep to these rules, and one draw needn't show every extreme that they name: `station_pairs`: each row names two different stations; station 0 and station 512 - 1 appear in every draw.
All inputs are finite; a program needn't handle non-finite values.
Results may differ from the reference program's by a relative error of at most 0.00045.
Values sent between devices are 32-bit elements; how exact they have to be, the bound alone decides.
No kernel may reach another device: no remote copies, remote signals or barrier semaphores. Data moves between devices by JAX's collectives and lax.ppermute only.
A program may use at most 64 MiB of HBM per device.

```python
import math
import jax
import jax.numpy as jnp
from jax import lax

N_ST = 512
DIRS = 32
TERMS = 4
GN_STEPS = 2
ADMM_ITERS = 2
CHANNELS = 8
ROWS = 16384


def draw_station_pairs(key, part):
    key = jax.random.fold_in(key, 7)
    key_first, key_offset = jax.random.split(key)
    first = jax.random.randint(key_first, (ROWS,), 0, N_ST)
    offset = jax.random.randint(key_offset, (ROWS,), 1, N_ST)
    second = (first + offset) % N_ST
    first = first.at[0].set(0)
    second = second.at[0].set(N_ST - 1)
    return jnp.stack([first, second]).astype(jnp.int32)


def levels(key, dims, cuts, least, high):
    level = 1.0
    for dim, shards_of in cuts:
        draws = jax.random.uniform(jax.random.fold_in(jax.random.fold_in(key, 6), dim), (shards_of,), jnp.float32, least / len(cuts), high / len(cuts))
        level = level * jnp.repeat(jnp.exp(draws), dims[dim] // shards_of).reshape((-1,) + (1,) * (len(dims) - 1 - dim))
    return level


def gaussian(rng, dims, width, limit, cuts=(), kind=jnp.bfloat16):
    gain = levels(rng, dims, cuts, -0.22, 0.18) if cuts else 1.0
    result = jax.random.normal(rng, dims, jnp.float32) * width * gain
    return jnp.minimum(jnp.maximum(result, -limit), limit).astype(kind)


def setup_inputs(seed: int = 0) -> dict:
    key_of = jax.random.split(jax.random.key(seed), 8)
    coherency = gaussian(key_of[0], (CHANNELS, DIRS, 8, ROWS), 0.25, 1.5, ((0, 8), (3, 16)))
    visibilities = gaussian(key_of[1], (CHANNELS, 8, ROWS), 1.0, 6.0, ((0, 8), (2, 16)), jnp.float32)
    station_pairs = draw_station_pairs(jax.random.fold_in(key_of[7], 71), 0)
    gains = gaussian(key_of[3], (CHANNELS, DIRS, 8, N_ST), 0.7, 4.0, ((0, 8), (3, 16)), jnp.float32)
    duals = gaussian(key_of[4], (CHANNELS, DIRS, 8, N_ST), 1.0, 5.0, ((0, 8), (3, 16)), jnp.float32)
    poly = gaussian(key_of[5], (DIRS, 8, TERMS, N_ST), 0.5, 4.0, ((3, 16),), jnp.float32)
    penalty = jnp.clip(jnp.exp(jax.random.uniform(key_of[6], (DIRS,), jnp.float32, math.log(2.0), math.log(20.0))), 2.0, 20.0)
    return {"coherency": coherency, "visibilities": visibilities, "station_pairs": station_pairs, "gains": gains, "duals": duals, "poly": poly, "penalty": penalty}


def complex_product(left, right):
    real_parts = []
    imag_parts = []
    for row in (0, 1):
        for col in (0, 1):
            lr0 = left[..., 2 * row, :]
            lr1 = left[..., 2 * row + 1, :]
            li0 = left[..., 4 + 2 * row, :]
            li1 = left[..., 5 + 2 * row, :]
            rr0 = right[..., col, :]
            rr1 = right[..., 2 + col, :]
            ri0 = right[..., 4 + col, :]
            ri1 = right[..., 6 + col, :]
            real_parts.append(lr0 * rr0 - li0 * ri0 + lr1 * rr1 - li1 * ri1)
            imag_parts.append(lr0 * ri0 + li0 * rr0 + lr1 * ri1 + li1 * rr1)
    return jnp.stack(real_parts + imag_parts, axis=-2)

def conj_transpose(matrix):
    order = [0, 2, 1, 3]
    real_parts = [matrix[..., i, :] for i in order]
    imag_parts = [-matrix[..., 4 + i, :] for i in order]
    return jnp.stack(real_parts + imag_parts, axis=-2)

def hermitian_square(matrix):
    full = complex_product(matrix, conj_transpose(matrix))
    return jnp.stack([full[..., 0, :], full[..., 3, :], full[..., 1, :], full[..., 5, :]], axis=-2)

def basis_table(count):
    place = (2.0 * jnp.arange(count, dtype=jnp.float32) + 1.0) / count - 1.0
    return jnp.stack([jnp.ones_like(place), place, 1.5 * place * place - 0.5, 2.5 * place * place * place - 1.5 * place], axis=1)

def channel_sums(gain_one, coh_one, vis_one, first, second, stations):
    gain_first = jnp.take(gain_one, first, axis=2)
    gain_second = jnp.take(gain_one, second, axis=2)
    z_first = complex_product(coh_one, conj_transpose(gain_second))
    model = complex_product(gain_first, z_first)
    resid = vis_one - jnp.sum(model, axis=0)
    per_dir = resid[None] + model
    z_second = complex_product(conj_transpose(coh_one), conj_transpose(gain_first))
    numer_first = complex_product(per_dir, conj_transpose(z_first))
    numer_second = complex_product(conj_transpose(per_dir), conj_transpose(z_second))
    side_first = jnp.concatenate([numer_first, hermitian_square(z_first)], axis=1)
    side_second = jnp.concatenate([numer_second, hermitian_square(z_second)], axis=1)
    stacked = jnp.concatenate([side_first, side_second], axis=2)
    index = jnp.concatenate([first, second]).astype(jnp.int32)
    summed = jax.ops.segment_sum(jnp.moveaxis(stacked, 2, 0), index, num_segments=stations)
    return jnp.moveaxis(summed, 0, 2)

def gain_update(gain_now, sums, target, penalty):
    half_rho = 0.5 * penalty[None, :, None]
    diag_first = sums[:, :, 8, :] + half_rho
    diag_second = sums[:, :, 9, :] + half_rho
    off_real = sums[:, :, 10, :]
    off_imag = sums[:, :, 11, :]
    determinant = diag_first * diag_second - off_real * off_real - off_imag * off_imag
    zeros = jnp.zeros_like(diag_first)
    inverse = jnp.stack([diag_second, -off_real, -off_real, diag_first, zeros, -off_imag, off_imag, zeros], axis=2) / determinant[:, :, None, :]
    solved = complex_product(sums[:, :, :8, :] + target, inverse)
    return 0.5 * (gain_now + solved)

def poly_solve(chol, total):
    shape = total.shape
    moved = jnp.moveaxis(total, 2, 0).reshape(shape[2], -1)
    half = lax.linalg.triangular_solve(chol, moved, left_side=True, lower=True)
    whole = lax.linalg.triangular_solve(chol, half, left_side=True, lower=True, transpose_a=True)
    return jnp.moveaxis(whole.reshape(shape[2], shape[0], shape[1], shape[3]), 0, 2)

def reference(coherency, visibilities, station_pairs, gains, duals, poly, penalty):
    table = basis_table(CHANNELS)
    gram = jnp.dot(table.T, table, precision=lax.Precision.HIGHEST)
    chol = jnp.linalg.cholesky(gram)
    rho_four = penalty[None, :, None, None]
    first = station_pairs[0]
    second = station_pairs[1]
    for outer in range(ADMM_ITERS):
        fitted = jnp.einsum('ft,kctn->fkcn', table, poly, precision=lax.Precision.HIGHEST)
        target = 0.5 * rho_four * fitted - 0.5 * duals
        for inner in range(GN_STEPS):

            def one_channel(items):
                gain_one, coh_one, vis_one = items
                return channel_sums(gain_one, coh_one.astype(jnp.float32), vis_one, first, second, N_ST)
            sums = lax.map(one_channel, (gains, coherency, visibilities))
            gains = gain_update(gains, sums, target, penalty)
        total = jnp.einsum('ft,fkcn->kctn', table, duals + rho_four * gains, precision=lax.Precision.HIGHEST)
        poly = poly_solve(chol, total)
        fitted = jnp.einsum('ft,kctn->fkcn', table, poly, precision=lax.Precision.HIGHEST)
        duals = duals + rho_four * (gains - fitted)
    return (gains, duals, poly)
```

```python
import functools

import jax
import jax.numpy as jnp
import numpy as np
from jax import lax
from jax.experimental import pallas as pl
from jax.experimental.pallas import tpu as pltpu
from jax.sharding import Mesh, PartitionSpec as P


CHANNELS = 8
TERMS = 4
ROWS = 1024
BLOCK = 256
STATIONS = 512
F32 = jnp.float32
BF16 = jnp.bfloat16
CORE_SWAP = [(0, 1), (1, 0)]
VMEM_BYTES = 24 * 1024 * 1024


def consensus_tables():
    place = (2.0 * np.arange(CHANNELS) + 1.0) / CHANNELS - 1.0
    basis = np.stack(
        [np.ones_like(place), place, 1.5 * place**2 - 0.5, 2.5 * place**3 - 1.5 * place], axis=1
    )
    solve = np.linalg.solve(basis.T @ basis, basis.T)
    return basis, solve, basis @ solve


def call(kernel, out_shapes, scratch=(), smem=(), n_in=0):
    in_specs = [
        pl.BlockSpec(memory_space=pltpu.SMEM if i in smem else pltpu.VMEM) for i in range(n_in)
    ]
    return pl.pallas_call(
        kernel,
        out_shape=[jax.ShapeDtypeStruct(s, d) for s, d in out_shapes],
        in_specs=in_specs,
        out_specs=[pl.BlockSpec(memory_space=pltpu.VMEM) for _ in out_shapes],
        scratch_shapes=list(scratch),
        compiler_params=pltpu.CompilerParams(vmem_limit_bytes=VMEM_BYTES),
    )


def lanes():
    return lax.broadcasted_iota(jnp.int32, (8, 128), 1)


def split_parts(x):
    high = x.astype(BF16)
    return high, (x - high.astype(F32)).astype(BF16)


def matrix(load):
    return [load(i) for i in range(4)], [load(4 + i) for i in range(4)]


def conj_t(m):
    re, im = m
    return [re[0], re[2], re[1], re[3]], [-im[0], -im[2], -im[1], -im[3]]


def product_nh(a, b):
    (ar, ai), (br, bi) = a, b
    re, im = [], []
    for i in (0, 1):
        for j in (0, 1):
            p, q, u, v = 2 * i, 2 * i + 1, 2 * j, 2 * j + 1
            re.append((ar[p] * br[u] + ai[p] * bi[u]) + (ar[q] * br[v] + ai[q] * bi[v]))
            im.append((ai[p] * br[u] - ar[p] * bi[u]) + (ai[q] * br[v] - ar[q] * bi[v]))
    return re, im


def product_hn(a, b):
    (ar, ai), (br, bi) = a, b
    re, im = [], []
    for i in (0, 1):
        for j in (0, 1):
            p, q, u, v = i, 2 + i, j, 2 + j
            re.append((ar[p] * br[u] + ai[p] * bi[u]) + (ar[q] * br[v] + ai[q] * bi[v]))
            im.append((ar[p] * bi[u] - ai[p] * br[u]) + (ar[q] * bi[v] - ai[q] * br[v]))
    return re, im


def product(a, b):
    (ar, ai), (br, bi) = a, b
    re, im = [], []
    for i in (0, 1):
        for j in (0, 1):
            p, q, u, v = 2 * i, 2 * i + 1, j, 2 + j
            re.append((ar[p] * br[u] - ai[p] * bi[u]) + (ar[q] * br[v] - ai[q] * bi[v]))
            im.append((ar[p] * bi[u] + ai[p] * br[u]) + (ar[q] * bi[v] + ai[q] * br[v]))
    return re, im


def square_nh(a):
    r, i = a
    return [
        (r[0] * r[0] + i[0] * i[0]) + (r[1] * r[1] + i[1] * i[1]),
        (r[2] * r[2] + i[2] * i[2]) + (r[3] * r[3] + i[3] * i[3]),
        (r[0] * r[2] + i[0] * i[2]) + (r[1] * r[3] + i[1] * i[3]),
        (i[0] * r[2] - r[0] * i[2]) + (i[1] * r[3] - r[1] * i[3]),
    ]


def square_hn(a):
    r, i = a
    return [
        (r[0] * r[0] + i[0] * i[0]) + (r[2] * r[2] + i[2] * i[2]),
        (r[1] * r[1] + i[1] * i[1]) + (r[3] * r[3] + i[3] * i[3]),
        (r[0] * r[1] + i[0] * i[1]) + (r[2] * r[3] + i[2] * i[3]),
        (r[0] * i[1] - i[0] * r[1]) + (r[2] * i[3] - i[2] * r[3]),
    ]


def prepare_kernel(
    coh, gains, duals, poly, penalty, tables,
    coh_keep, coh_send, state_keep, state_send, rho_a, rho_f,
    wide, thin,
):
    core = lax.axis_index("core")
    chan = lax.axis_index("chan")
    for t in range(ROWS // 128):
        cols = slice(t * 128, (t + 1) * 128)
        wide[t] = coh[:, :, cols].astype(F32).reshape(256, 128)
        for c in range(8):
            coh_keep[c * 16:(c + 1) * 16, cols] = wide[t, pl.ds(core * 128 + c, 16, stride=8), :]
            coh_send[c * 16:(c + 1) * 16, cols] = wide[t, pl.ds((1 - core) * 128 + c, 16, stride=8), :]
    row = lax.broadcasted_iota(jnp.int32, (8, 128), 0)
    lane = lanes()
    by_dir = jnp.zeros((8, 128), F32)
    half_dir = jnp.zeros((8, 128), F32)
    for q in range(4):
        for s in range(8):
            here = row == s
            by_dir = jnp.where(here & (lane // 32 == q), penalty[q * 8 + s], by_dir)
    for q in range(2):
        for s in range(8):
            here = row == s
            half_dir = jnp.where(here & (lane // 64 == q), penalty[core * 16 + q * 8 + s], half_dir)
    rho_a[...] = half_dir
    rho_f[...] = by_dir

    def pack(which):
        for c in range(8):
            for out, half in ((state_keep, core), (state_send, 1 - core)):
                total = None
                for h in range(2):
                    part = thin[pl.ds((half * 16 + h * 8) * 8 + c, 8, stride=8), :]
                    part = pltpu.roll(part, h * 64 + core * 32, 1)
                    total = part if total is None else total + part
                out[which * 64 + c * 8:which * 64 + (c + 1) * 8, :] = total

    thin[...] = jnp.zeros((256, 128), F32)
    thin[:, 0:32] = gains[...].reshape(256, 32)
    pack(0)
    thin[:, 0:32] = duals[...].reshape(256, 32)
    pack(1)
    fitted = poly[:, :, 0, :] * tables[chan, 0]
    for t in range(1, TERMS):
        fitted = fitted + poly[:, :, t, :] * tables[chan, t]
    thin[:, 0:32] = fitted.reshape(256, 32)
    pack(2)


def first_kernel(state_keep, state_recv, rho_a, gains, duals, target, spread):
    both = state_keep[...] + state_recv[...]
    gains[...] = both[0:64]
    duals[...] = both[64:128]
    for d in range(8):
        spread[d * 64:(d + 1) * 64, :] = both[0:64]
    half_rho = 0.5 * rho_a[...]
    for c in range(8):
        at = c * 8
        target[at:at + 8, :] = half_rho * both[128 + at:136 + at] - 0.5 * both[64 + at:72 + at]


def model_kernel(gathered, coh_own, coh_other, vis, pairs_own, pairs_other, z_ref, w_ref, s_ref, table, near, far):
    lane = lanes()
    low = lane < 64
    for c in range(8):
        for t in range(4):
            a = gathered[(2 * t) * 64 + c * 8:(2 * t) * 64 + c * 8 + 8, :]
            b = gathered[(2 * t + 1) * 64 + c * 8:(2 * t + 1) * 64 + c * 8 + 8, :]
            first = jnp.where(low, a, pltpu.roll(b, 64, 1))
            second = jnp.where(low, pltpu.roll(a, 64, 1), b)
            high, rest = split_parts(jnp.concatenate([first, second], axis=0))
            table[c * 16:(c + 1) * 16, t * 128:(t + 1) * 128] = high
            table[128 + c * 16:128 + (c + 1) * 16, t * 128:(t + 1) * 128] = rest
    station = lax.broadcasted_iota(jnp.int32, (STATIONS, BLOCK), 0)
    for j in range(2 * ROWS // BLOCK):
        own = j < ROWS // BLOCK
        coh = coh_own if own else coh_other
        pairs = pairs_own if own else pairs_other
        col = (j * BLOCK) % ROWS
        for side, dest in ((0, near), (1, far)):
            hot = (station == pairs[side:side + 1, col:col + BLOCK]).astype(F32).astype(BF16)
            both = jnp.dot(table[...], hot, preferred_element_type=F32)
            dest[j % 2] = both[:128] + both[128:]
        for l in range(BLOCK // 128):
            src = col + l * 128
            dst = j * BLOCK + l * 128
            gp = matrix(lambda i: near[j % 2, i * 16:(i + 1) * 16, l * 128:(l + 1) * 128])
            gq = matrix(lambda i: far[j % 2, i * 16:(i + 1) * 16, l * 128:(l + 1) * 128])
            cc = matrix(lambda i: coh[i * 16:(i + 1) * 16, src:src + 128])
            z = product_nh(cc, gq)
            w = product(gp, cc)
            m = product(gp, z)
            for i in range(8):
                z_ref[i * 16:(i + 1) * 16, dst:dst + 128] = z[i // 4][i % 4]
                w_ref[i * 16:(i + 1) * 16, dst:dst + 128] = w[i // 4][i % 4]
                total = -jnp.sum(m[i // 4][i % 4], axis=0, keepdims=True)
                if own:
                    total = total + vis[i:i + 1, src:src + 128]
                s_ref[i:i + 1, dst:dst + 128] = total


def sums_kernel(z_ref, w_ref, s_own, s_other, pairs_own, pairs_other, out, left, acc):
    station = lax.broadcasted_iota(jnp.int32, (STATIONS, BLOCK), 0)
    steps = 2 * ROWS // BLOCK
    for j in range(steps):
        own = j < steps // 2
        pairs = pairs_own if own else pairs_other
        col = (j * BLOCK) % ROWS
        slot = j % 2
        for l in range(BLOCK // 128):
            src = j * BLOCK + l * 128
            swapped = (src + ROWS) % (2 * ROWS)
            r = matrix(lambda i: s_own[i:i + 1, src:src + 128] + s_other[i:i + 1, swapped:swapped + 128])
            z = matrix(lambda i: z_ref[i * 16:(i + 1) * 16, src:src + 128])
            w = matrix(lambda i: w_ref[i * 16:(i + 1) * 16, src:src + 128])
            for side, (num, den) in enumerate(
                ((product_nh(r, z), square_nh(z)), (product_hn(r, w), square_hn(w)))
            ):
                at = side * BLOCK + l * 128
                for i, value in enumerate(num[0] + num[1] + den):
                    high, rest = split_parts(value)
                    left[slot, i * 16:(i + 1) * 16, at:at + 128] = high
                    left[slot, 192 + i * 16:192 + (i + 1) * 16, at:at + 128] = rest
        total = None
        for side in range(2):
            hot = (station == pairs[side:side + 1, col:col + BLOCK]).astype(F32).astype(BF16)
            part = lax.dot_general(
                left[slot, :, side * BLOCK:(side + 1) * BLOCK], hot,
                (((1,), (1,)), ((), ())), preferred_element_type=F32,
            )
            total = part if total is None else total + part
        if j == 0:
            acc[...] = total
        else:
            acc[...] += total
    low = lanes() < 64
    for c in range(12):
        for t in range(4):
            cols = slice(t * 128, (t + 1) * 128)
            at = c * 16
            v0 = acc[at:at + 8, cols] + acc[192 + at:192 + at + 8, cols]
            v1 = acc[at + 8:at + 16, cols] + acc[192 + at + 8:192 + at + 16, cols]
            out[(2 * t) * 96 + c * 8:(2 * t) * 96 + c * 8 + 8, :] = jnp.where(low, v0, pltpu.roll(v1, 64, 1))
            out[(2 * t + 1) * 96 + c * 8:(2 * t + 1) * 96 + c * 8 + 8, :] = jnp.where(low, pltpu.roll(v0, 64, 1), v1)


def updated(received, gains, target, rho):
    sums = []
    for c in range(12):
        parts = [received[d * 96 + c * 8:d * 96 + c * 8 + 8, :] for d in range(8)]
        while len(parts) > 1:
            parts = [parts[i] + parts[i + 1] for i in range(0, len(parts), 2)]
        sums.append(parts[0])
    half_rho = 0.5 * rho
    a, d, br, bi = sums[8] + half_rho, sums[9] + half_rho, sums[10], sums[11]
    scale = 0.5 / (a * d - br * br - bi * bi)
    n = [sums[i] + target[i] - half_rho * gains[i] for i in range(8)]
    result = [None] * 8
    for i in (0, 1):
        r0, r1, i0, i1 = n[2 * i], n[2 * i + 1], n[4 + 2 * i], n[5 + 2 * i]
        result[2 * i] = gains[2 * i] + scale * (r0 * d - (r1 * br + i1 * bi))
        result[4 + 2 * i] = gains[4 + 2 * i] + scale * (i0 * d - (i1 * br - r1 * bi))
        result[2 * i + 1] = gains[2 * i + 1] + scale * (r1 * a - (r0 * br - i0 * bi))
        result[5 + 2 * i] = gains[5 + 2 * i] + scale * (i1 * a - (i0 * br + r0 * bi))
    return result


def comps(ref):
    return [ref[c * 8:(c + 1) * 8, :] for c in range(8)]


def put(ref, values, base=0):
    for c in range(8):
        ref[base + c * 8:base + (c + 1) * 8, :] = values[c]


def update_kernel(received, gains, target, rho_a, gains_new, spread):
    new = updated(received, comps(gains), comps(target), rho_a[...])
    put(gains_new, new)
    for d in range(8):
        put(spread, new, d * 64)


def update_moment_kernel(received, gains, target, duals, rho_a, gains_new, spread, moment):
    rho = rho_a[...]
    new = updated(received, comps(gains), comps(target), rho)
    put(gains_new, new)
    old = comps(duals)
    whole = [old[c] + rho * new[c] for c in range(8)]
    for d in range(8):
        put(spread, new, d * 64)
        put(moment, whole, d * 64)


def fit(tables, row, moments, column):
    result = []
    for c in range(8):
        total = None
        for f in range(CHANNELS):
            part = tables[row, column + f] * moments[f * 64 + c * 8:f * 64 + c * 8 + 8, :]
            total = part if total is None else total + part
        result.append(total)
    return result


def update_consensus_kernel(received, gains, moments, duals, rho_a, tables, gains_new, spread, duals_new, target):
    rho = rho_a[...]
    chan = lax.axis_index("chan")
    old_gains = comps(gains)
    old_duals = comps(duals)
    fitted = fit(tables, chan, moments, 4)
    new_duals = [old_duals[c] + rho * (old_gains[c] - fitted[c]) for c in range(8)]
    aim = [0.5 * (rho * fitted[c] - new_duals[c]) for c in range(8)]
    put(duals_new, new_duals)
    put(target, aim)
    new = updated(received, old_gains, aim, rho)
    put(gains_new, new)
    for d in range(8):
        put(spread, new, d * 64)


def update_last_kernel(received, gains, target, duals, rho_a, keep, send):
    core = lax.axis_index("core")
    new = updated(received, comps(gains), comps(target), rho_a[...])
    old = comps(duals)
    lane = lanes()
    for out, stations in ((keep, core), (send, 1 - core)):
        for base, values in ((0, new), (64, old)):
            for c in range(8):
                total = jnp.zeros((8, 128), F32)
                for h in range(2):
                    here = jnp.where(lane // 32 == 2 * h + stations, values[c], 0.0)
                    total = total + pltpu.roll(here, (64 * core + 32 * stations * 3 + 96 * h) % 128, 1)
                out[base + c * 8:base + (c + 1) * 8, :] = total


def moment_kernel(keep, recv, rho_f, state, moment):
    both = keep[...] + recv[...]
    state[...] = both
    rho = rho_f[...]
    for c in range(8):
        value = both[64 + c * 8:72 + c * 8] + rho * both[c * 8:c * 8 + 8]
        for d in range(8):
            moment[d * 64 + c * 8:d * 64 + (c + 1) * 8, :] = value


def finish_kernel(moments, state, rho_f, tables, gains, duals, poly, thin, deep):
    chan = lax.axis_index("chan")
    rho = rho_f[...]
    fitted = fit(tables, chan, moments, 4)
    for c in range(8):
        value = state[c * 8:(c + 1) * 8, :]
        for q in range(4):
            thin[pl.ds(q * 64 + c, 8, stride=8), :] = pltpu.roll(value, (128 - 32 * q) % 128, 1)
    gains[...] = thin[:, 0:32].reshape(32, 8, 32)
    for c in range(8):
        value = state[64 + c * 8:72 + c * 8, :] + rho * (state[c * 8:(c + 1) * 8, :] - fitted[c])
        for q in range(4):
            thin[pl.ds(q * 64 + c, 8, stride=8), :] = pltpu.roll(value, (128 - 32 * q) % 128, 1)
    duals[...] = thin[:, 0:32].reshape(32, 8, 32)
    for t in range(TERMS):
        part = fit(tables, 8 + t, moments, 4)
        for c in range(8):
            for q in range(4):
                deep[pl.ds((q * 64 + c) * 4 + t, 8, stride=32), :] = pltpu.roll(part[c], (128 - 32 * q) % 128, 1)
    poly[...] = deep[:, 0:32].reshape(32, 8, 4, 32)


def local(coherency, visibilities, station_pairs, gains, duals, poly, penalty):
    basis, solve, hat = consensus_tables()
    constants = np.zeros((12, 12), np.float32)
    constants[:8, :4] = basis
    constants[:8, 4:] = hat
    constants[8:, 4:] = solve
    tables = jnp.asarray(constants)
    coh_keep, coh_send, state_keep, state_send, rho_a, rho_f = call(
        prepare_kernel,
        [((128, ROWS), F32), ((128, ROWS), F32), ((192, 128), F32), ((192, 128), F32), ((8, 128), F32), ((8, 128), F32)],
        [pltpu.VMEM((ROWS // 128, 256, 128), F32), pltpu.VMEM((256, 128), F32)],
        smem=(4, 5), n_in=6,
    )(coherency[0], gains[0], duals[0], poly, penalty, tables)

    def swap(x):
        return lax.ppermute(x, "core", CORE_SWAP)

    def exchange(x, axis):
        return lax.all_to_all(x, axis, 0, 0, tiled=True)

    state_recv = swap(state_send)
    coh_recv = swap(coh_send)
    pairs_recv = swap(station_pairs)
    vis = visibilities[0]
    packed = ((64, 128), F32)
    wide = ((512, 128), F32)
    gain, dual, target, spread = call(first_kernel, [packed, packed, packed, wide], n_in=3)(
        state_keep, state_recv, rho_a
    )

    def sums(spread):
        gathered = exchange(spread, "st")
        z, w, own = call(
            model_kernel,
            [((128, 2 * ROWS), F32), ((128, 2 * ROWS), F32), ((8, 2 * ROWS), F32)],
            [pltpu.VMEM((256, STATIONS), BF16), pltpu.VMEM((2, 128, BLOCK), F32), pltpu.VMEM((2, 128, BLOCK), F32)],
            n_in=6,
        )(gathered, coh_keep, coh_recv, vis, station_pairs, pairs_recv)
        other = swap(own)
        (parts,) = call(
            sums_kernel,
            [((768, 128), F32)],
            [pltpu.VMEM((2, 384, 2 * BLOCK), BF16), pltpu.VMEM((384, STATIONS), F32)],
            n_in=6,
        )(z, w, own, other, station_pairs, pairs_recv)
        return exchange(parts, "st")

    gain, spread = call(update_kernel, [packed, wide], n_in=4)(sums(spread), gain, target, rho_a)
    gain, spread, moment = call(update_moment_kernel, [packed, wide, wide], n_in=5)(
        sums(spread), gain, target, dual, rho_a
    )
    moments = exchange(moment, "chan")
    gain, spread, dual, target = call(
        update_consensus_kernel, [packed, wide, packed, packed], smem=(5,), n_in=6
    )(sums(spread), gain, moments, dual, rho_a, tables)
    keep, send = call(update_last_kernel, [((128, 128), F32), ((128, 128), F32)], n_in=5)(
        sums(spread), gain, target, dual, rho_a
    )
    state, moment = call(moment_kernel, [((128, 128), F32), wide], n_in=3)(keep, swap(send), rho_f)
    moments = exchange(moment, "chan")
    gains_out, duals_out, poly_out = call(
        finish_kernel,
        [((32, 8, 32), F32), ((32, 8, 32), F32), ((32, 8, 4, 32), F32)],
        [pltpu.VMEM((256, 128), F32), pltpu.VMEM((1024, 128), F32)],
        smem=(3,), n_in=4,
    )(moments, state, rho_f, tables)
    return gains_out[None], duals_out[None], poly_out


def solution(mesh):
    chan, bl = mesh.devices.shape
    finer = Mesh(mesh.devices.reshape(chan, bl // 2, 2), ("chan", "st", "core"))
    both = ("st", "core")
    in_specs = (
        P("chan", None, None, both),
        P("chan", None, both),
        P(None, both),
        P("chan", None, None, both),
        P("chan", None, None, both),
        P(None, None, None, both),
        P(),
    )
    out_specs = (
        P("chan", None, None, both),
        P("chan", None, None, both),
        P(None, None, None, both),
    )
    return jax.shard_map(local, mesh=finer, in_specs=in_specs, out_specs=out_specs, check_vma=False)
```

```python
import jax
import jax.numpy as jnp
import numpy as np
from jax import lax
from jax.experimental import pallas as pl
from jax.experimental.pallas import tpu as pltpu
from jax.sharding import Mesh, PartitionSpec as P


CHANNELS = 8
TERMS = 4
ROWS = 1024
BLOCK = 256
STATIONS = 512
F32 = jnp.float32
BF16 = jnp.bfloat16
CORE_SWAP = [(0, 1), (1, 0)]
VMEM_BYTES = 24 * 1024 * 1024
WHOLE_BYTES = 60 * 1024 * 1024


def consensus_tables():
    place = (2.0 * np.arange(CHANNELS) + 1.0) / CHANNELS - 1.0
    basis = np.stack(
        [np.ones_like(place), place, 1.5 * place**2 - 0.5, 2.5 * place**3 - 1.5 * place], axis=1
    )
    solve = np.linalg.solve(basis.T @ basis, basis.T)
    return basis, solve, basis @ solve


def call(kernel, out_shapes, scratch=(), smem=(), hbm=(), n_in=0, cost=0, room=VMEM_BYTES):
    spaces = [pltpu.SMEM if i in smem else pl.ANY if i in hbm else pltpu.VMEM for i in range(n_in)]
    in_specs = [pl.BlockSpec(memory_space=space) for space in spaces]
    return pl.pallas_call(
        kernel,
        out_shape=[jax.ShapeDtypeStruct(s, d) for s, d in out_shapes],
        in_specs=in_specs,
        out_specs=[pl.BlockSpec(memory_space=pltpu.VMEM) for _ in out_shapes],
        scratch_shapes=list(scratch),
        compiler_params=pltpu.CompilerParams(vmem_limit_bytes=room),
        cost_estimate=pl.CostEstimate(flops=0, bytes_accessed=cost * 3_000_000 + 1000, transcendentals=0),
    )


def lanes():
    return lax.broadcasted_iota(jnp.int32, (8, 128), 1)


def split_parts(x):
    high = x.astype(BF16)
    return high, (x - high.astype(F32)).astype(BF16)


def matrix(load):
    return [load(i) for i in range(4)], [load(4 + i) for i in range(4)]


def conj_t(m):
    re, im = m
    return [re[0], re[2], re[1], re[3]], [-im[0], -im[2], -im[1], -im[3]]


def product_nh(a, b):
    (ar, ai), (br, bi) = a, b
    re, im = [], []
    for i in (0, 1):
        for j in (0, 1):
            p, q, u, v = 2 * i, 2 * i + 1, 2 * j, 2 * j + 1
            re.append((ar[p] * br[u] + ai[p] * bi[u]) + (ar[q] * br[v] + ai[q] * bi[v]))
            im.append((ai[p] * br[u] - ar[p] * bi[u]) + (ai[q] * br[v] - ar[q] * bi[v]))
    return re, im


def product_hn(a, b):
    (ar, ai), (br, bi) = a, b
    re, im = [], []
    for i in (0, 1):
        for j in (0, 1):
            p, q, u, v = i, 2 + i, j, 2 + j
            re.append((ar[p] * br[u] + ai[p] * bi[u]) + (ar[q] * br[v] + ai[q] * bi[v]))
            im.append((ar[p] * bi[u] - ai[p] * br[u]) + (ar[q] * bi[v] - ai[q] * br[v]))
    return re, im


def product(a, b):
    (ar, ai), (br, bi) = a, b
    re, im = [], []
    for i in (0, 1):
        for j in (0, 1):
            p, q, u, v = 2 * i, 2 * i + 1, j, 2 + j
            re.append((ar[p] * br[u] - ai[p] * bi[u]) + (ar[q] * br[v] - ai[q] * bi[v]))
            im.append((ar[p] * bi[u] + ai[p] * br[u]) + (ar[q] * bi[v] + ai[q] * br[v]))
    return re, im


def square_nh(a):
    r, i = a
    return [
        (r[0] * r[0] + i[0] * i[0]) + (r[1] * r[1] + i[1] * i[1]),
        (r[2] * r[2] + i[2] * i[2]) + (r[3] * r[3] + i[3] * i[3]),
        (r[0] * r[2] + i[0] * i[2]) + (r[1] * r[3] + i[1] * i[3]),
        (i[0] * r[2] - r[0] * i[2]) + (i[1] * r[3] - r[1] * i[3]),
    ]


def square_hn(a):
    r, i = a
    return [
        (r[0] * r[0] + i[0] * i[0]) + (r[2] * r[2] + i[2] * i[2]),
        (r[1] * r[1] + i[1] * i[1]) + (r[3] * r[3] + i[3] * i[3]),
        (r[0] * r[1] + i[0] * i[1]) + (r[2] * r[3] + i[2] * i[3]),
        (r[0] * i[1] - i[0] * r[1]) + (r[2] * i[3] - i[2] * r[3]),
    ]


def spread_kernel(gains, spread, mark, thin):
    thin[...] = jnp.zeros((256, 128), F32)
    mark[...] = jnp.zeros((8, 128), F32)
    thin[:, 0:32] = gains[...].reshape(256, 32)
    for half in range(2):
        for c in range(4):
            total = None
            for im in range(2):
                for h in range(2):
                    part = thin[pl.ds((half * 16 + h * 8) * 8 + im * 4 + c, 8, stride=8), :]
                    if im or h:
                        part = pltpu.roll(part, im * 64 + h * 32, 1)
                    total = part if total is None else total + part
            for d in range(8):
                at = (2 * d + half) * 32 + c * 8
                spread[at:at + 8, :] = total


def prepare_kernel(
    mark, coh_hbm, gains_hbm, duals_hbm, poly_hbm, pairs, penalty, tables,
    coh_keep, state_keep, rho_a, rho_f, send_0, send_1, send_2, send_3,
    coh, gains, duals, poly, wide, thin, sems,
):
    send = (send_0, send_1, send_2, send_3)
    copies = [
        pltpu.make_async_copy(src, dst, sems.at[i])
        for i, (src, dst) in enumerate(((gains_hbm, gains), (duals_hbm, duals), (poly_hbm, poly), (coh_hbm, coh)))
    ]
    for copy in copies:
        copy.start()
    core = lax.axis_index("core")
    chan = lax.axis_index("chan")
    row = lax.broadcasted_iota(jnp.int32, (8, 128), 0)
    lane = lanes()
    by_dir = jnp.zeros((8, 128), F32)
    half_dir = jnp.zeros((8, 128), F32)
    for q in range(4):
        for s in range(8):
            here = row == s
            by_dir = jnp.where(here & (lane // 32 == q), penalty[q * 8 + s], by_dir)
    for q in range(2):
        for s in range(8):
            here = row == s
            half_dir = jnp.where(here & (lane // 64 == q), penalty[core * 16 + q * 8 + s], half_dir)
    rho_a[...] = half_dir
    rho_f[...] = by_dir
    send_3[32:40, :] = jnp.zeros((8, ROWS), F32)
    send_3[32:34, :] = pairs[...].astype(F32)

    def pack(which):
        for c in range(8):
            for keep, half in ((True, core), (False, 1 - core)):
                total = None
                for h in range(2):
                    part = thin[pl.ds((half * 16 + h * 8) * 8 + c, 8, stride=8), :]
                    part = pltpu.roll(part, h * 64 + core * 32, 1)
                    total = part if total is None else total + part
                if keep:
                    state_keep[which * 64 + c * 8:which * 64 + (c + 1) * 8, :] = total
                else:
                    send[which][32:40, c * 128:(c + 1) * 128] = total

    thin[...] = jnp.zeros((256, 128), F32)
    copies[0].wait()
    thin[:, 0:32] = gains[...].reshape(256, 32)
    pack(0)
    copies[1].wait()
    thin[:, 0:32] = duals[...].reshape(256, 32)
    pack(1)
    copies[2].wait()
    fitted = poly[:, :, 0, :] * tables[chan, 0]
    for t in range(1, TERMS):
        fitted = fitted + poly[:, :, t, :] * tables[chan, t]
    thin[:, 0:32] = fitted.reshape(256, 32)
    pack(2)
    copies[3].wait()
    for t in range(ROWS // 128):
        cols = slice(t * 128, (t + 1) * 128)
        wide[t] = coh[:, :, cols].astype(F32).reshape(256, 128)
        for c in range(8):
            coh_keep[c * 16:(c + 1) * 16, cols] = wide[t, pl.ds(core * 128 + c, 16, stride=8), :]
            send[c // 2][(c % 2) * 16:(c % 2) * 16 + 16, cols] = wide[t, pl.ds((1 - core) * 128 + c, 16, stride=8), :]


def one_hot(pairs, side, j):
    index = jnp.broadcast_to(pairs[side:side + 1, j * BLOCK:(j + 1) * BLOCK], (16, BLOCK)).astype(jnp.int16)
    index = jnp.concatenate([index] * (STATIONS // 16), axis=0)
    here = lax.broadcasted_iota(jnp.int16, (STATIONS, BLOCK), 0) == index
    return jnp.where(here, jnp.ones((STATIONS, BLOCK), BF16), jnp.zeros((STATIONS, BLOCK), BF16))


def put_table(table, c, t, first, second):
    high, rest = split_parts(jnp.concatenate([first, second], axis=0))
    table[c * 16:(c + 1) * 16, t * 128:(t + 1) * 128] = high
    table[128 + c * 16:128 + (c + 1) * 16, t * 128:(t + 1) * 128] = rest


def start_table(gathered, table):
    lane = lanes()
    for c in range(8):
        im, row = divmod(c, 4)
        for t in range(4):
            halves = []
            for h in range(2):
                total = None
                for b in range(4):
                    part = gathered[(4 * t + b) * 32 + row * 8:(4 * t + b) * 32 + row * 8 + 8, :]
                    shift = (b * 32 - im * 64 - h * 32) % 128
                    if shift:
                        part = pltpu.roll(part, shift, 1)
                    total = part if total is None else jnp.where(lane // 32 == b, part, total)
                halves.append(total)
            put_table(table, c, t, *halves)


def step_table(gathered, table):
    low = lanes() < 64
    for c in range(8):
        for t in range(4):
            a = gathered[(2 * t) * 64 + c * 8:(2 * t) * 64 + c * 8 + 8, :]
            b = gathered[(2 * t + 1) * 64 + c * 8:(2 * t + 1) * 64 + c * 8 + 8, :]
            first = jnp.where(low, a, pltpu.roll(b, 64, 1))
            second = jnp.where(low, pltpu.roll(a, 64, 1), b)
            put_table(table, c, t, first, second)


def first_model_kernel(
    gathered, coh_own, recv_0, recv_1, recv_2, recv_3, vis, pairs_own, state_keep, rho_a,
    z_ref, w_ref, s_ref, pairs, gains, duals, target, table, near, far,
):
    received = (recv_0, recv_1, recv_2, recv_3)
    pairs[0:2, 0:ROWS] = pairs_own[...]
    pairs[0:2, ROWS:] = recv_3[32:34, :].astype(jnp.int32)
    half_rho = 0.5 * rho_a[...]
    for c in range(8):
        at = c * 8
        state = [
            state_keep[which * 64 + at:which * 64 + at + 8, :]
            + received[which][32:40, c * 128:(c + 1) * 128]
            for which in range(3)
        ]
        gains[at:at + 8, :] = state[0]
        duals[at:at + 8, :] = state[1]
        target[at:at + 8, :] = half_rho * state[2] - 0.5 * state[1]
    start_table(gathered, table)
    model(coh_own, received, vis, pairs, z_ref, w_ref, s_ref, table, near, far)


def model_kernel(
    gathered, coh_own, recv_0, recv_1, recv_2, recv_3, vis, pairs, z_ref, w_ref, s_ref, table, near, far
):
    received = (recv_0, recv_1, recv_2, recv_3)
    step_table(gathered, table)
    model(coh_own, received, vis, pairs, z_ref, w_ref, s_ref, table, near, far)


def model(coh_own, received, vis, pairs, z_ref, w_ref, s_ref, table, near, far):
    for j in range(2 * ROWS // BLOCK):
        own = j < ROWS // BLOCK
        col = (j * BLOCK) % ROWS
        for side, dest in ((0, near), (1, far)):
            both = jnp.dot(table[...], one_hot(pairs, side, j), preferred_element_type=F32)
            dest[j % 2] = both[:128] + both[128:]
        for l in range(BLOCK // 128):
            src = col + l * 128
            dst = j * BLOCK + l * 128
            gp = matrix(lambda i: near[j % 2, i * 16:(i + 1) * 16, l * 128:(l + 1) * 128])
            gq = matrix(lambda i: far[j % 2, i * 16:(i + 1) * 16, l * 128:(l + 1) * 128])
            if own:
                cc = matrix(lambda i: coh_own[i * 16:(i + 1) * 16, src:src + 128])
            else:
                cc = matrix(lambda i: received[i // 2][(i % 2) * 16:(i % 2) * 16 + 16, src:src + 128])
            z = product_nh(cc, gq)
            w = product(gp, cc)
            m = product(gp, z)
            for i in range(8):
                z_ref[i * 16:(i + 1) * 16, dst:dst + 128] = z[i // 4][i % 4]
                w_ref[i * 16:(i + 1) * 16, dst:dst + 128] = w[i // 4][i % 4]
                total = -jnp.sum(m[i // 4][i % 4], axis=0, keepdims=True)
                if own:
                    total = total + vis[i:i + 1, src:src + 128]
                s_ref[i:i + 1, dst:dst + 128] = total


def sums_kernel(z_ref, w_ref, s_own, s_other, pairs, out, left, acc, hot):
    steps = 2 * ROWS // BLOCK
    for j in range(steps):
        for l in range(BLOCK // 128):
            src = j * BLOCK + l * 128
            swapped = (src + ROWS) % (2 * ROWS)
            r = matrix(lambda i: s_own[i:i + 1, src:src + 128] + s_other[i:i + 1, swapped:swapped + 128])
            z = matrix(lambda i: z_ref[i * 16:(i + 1) * 16, src:src + 128])
            w = matrix(lambda i: w_ref[i * 16:(i + 1) * 16, src:src + 128])
            for side, (num, den) in enumerate(
                ((product_nh(r, z), square_nh(z)), (product_hn(r, w), square_hn(w)))
            ):
                at = side * BLOCK + l * 128
                for i, value in enumerate(num[0] + num[1] + den):
                    high, rest = split_parts(value)
                    left[j, i * 16:(i + 1) * 16, at:at + 128] = high
                    left[j, 192 + i * 16:192 + (i + 1) * 16, at:at + 128] = rest
        for side in range(2):
            hot[j, :, side * BLOCK:(side + 1) * BLOCK] = one_hot(pairs, side, j)
        total = lax.dot_general(left[j], hot[j], (((1,), (1,)), ((), ())), preferred_element_type=F32)
        if j == 0:
            acc[...] = total
        else:
            acc[...] += total
    low = lanes() < 64
    for c in range(12):
        for t in range(4):
            cols = slice(t * 128, (t + 1) * 128)
            at = c * 16
            v0 = acc[at:at + 8, cols] + acc[192 + at:192 + at + 8, cols]
            v1 = acc[at + 8:at + 16, cols] + acc[192 + at + 8:192 + at + 16, cols]
            out[(2 * t) * 96 + c * 8:(2 * t) * 96 + c * 8 + 8, :] = jnp.where(low, v0, pltpu.roll(v1, 64, 1))
            out[(2 * t + 1) * 96 + c * 8:(2 * t + 1) * 96 + c * 8 + 8, :] = jnp.where(low, pltpu.roll(v0, 64, 1), v1)


def updated(received, gains, target, rho):
    sums = []
    for c in range(12):
        parts = [received[d * 96 + c * 8:d * 96 + c * 8 + 8, :] for d in range(8)]
        while len(parts) > 1:
            parts = [parts[i] + parts[i + 1] for i in range(0, len(parts), 2)]
        sums.append(parts[0])
    half_rho = 0.5 * rho
    a, d, br, bi = sums[8] + half_rho, sums[9] + half_rho, sums[10], sums[11]
    scale = 0.5 / (a * d - br * br - bi * bi)
    n = [sums[i] + target[i] - half_rho * gains[i] for i in range(8)]
    result = [None] * 8
    for i in (0, 1):
        r0, r1, i0, i1 = n[2 * i], n[2 * i + 1], n[4 + 2 * i], n[5 + 2 * i]
        result[2 * i] = gains[2 * i] + scale * (r0 * d - (r1 * br + i1 * bi))
        result[4 + 2 * i] = gains[4 + 2 * i] + scale * (i0 * d - (i1 * br - r1 * bi))
        result[2 * i + 1] = gains[2 * i + 1] + scale * (r1 * a - (r0 * br - i0 * bi))
        result[5 + 2 * i] = gains[5 + 2 * i] + scale * (i1 * a - (i0 * br + r0 * bi))
    return result


def comps(ref):
    return [ref[c * 8:(c + 1) * 8, :] for c in range(8)]


def put(ref, values, base=0):
    for c in range(8):
        ref[base + c * 8:base + (c + 1) * 8, :] = values[c]


def update_kernel(received, gains, target, rho_a, gains_new, spread):
    new = updated(received, comps(gains), comps(target), rho_a[...])
    put(gains_new, new)
    for d in range(8):
        put(spread, new, d * 64)


def update_moment_kernel(received, gains, target, duals, rho_a, gains_new, spread, moment):
    rho = rho_a[...]
    new = updated(received, comps(gains), comps(target), rho)
    put(gains_new, new)
    old = comps(duals)
    whole = [old[c] + rho * new[c] for c in range(8)]
    for d in range(8):
        put(spread, new, d * 64)
        put(moment, whole, d * 64)


def fit(tables, row, moments, first, stride, count):
    result = []
    for c in range(count):
        total = None
        for f in range(CHANNELS):
            at = f * stride + first + c * 8
            part = tables[row, 4 + f] * moments[at:at + 8, :]
            total = part if total is None else total + part
        result.append(total)
    return result


def update_consensus_kernel(received, gains, moments, duals, rho_a, tables, gains_new, spread, duals_new, target):
    rho = rho_a[...]
    chan = lax.axis_index("chan")
    old_gains = comps(gains)
    old_duals = comps(duals)
    fitted = fit(tables, chan, moments, 0, 64, 8)
    new_duals = [old_duals[c] + rho * (old_gains[c] - fitted[c]) for c in range(8)]
    aim = [0.5 * (rho * fitted[c] - new_duals[c]) for c in range(8)]
    put(duals_new, new_duals)
    put(target, aim)
    new = updated(received, old_gains, aim, rho)
    put(gains_new, new)
    for d in range(8):
        put(spread, new, d * 64)


def update_last_kernel(received, gains, target, duals, rho_a, keep, send, moment):
    core = lax.axis_index("core")
    rho = rho_a[...]
    new = updated(received, comps(gains), comps(target), rho)
    old = comps(duals)
    lane = lanes()
    quarter = lane // 32
    whole = [old[c] + rho * new[c] for c in range(8)]
    for half in range(2):
        for c in range(4):
            total = jnp.zeros((8, 128), F32)
            for im in range(2):
                for h in range(2):
                    here = jnp.where(quarter == 2 * h + half, whole[im * 4 + c], 0.0)
                    shift = (im * 64 - 32 * h - 32 * half) % 128
                    total = total + (pltpu.roll(here, shift, 1) if shift else here)
            for f in range(CHANNELS):
                at = (2 * f + half) * 32 + c * 8
                moment[at:at + 8, :] = total
    for out, stations in ((keep, core), (send, 1 - core)):
        for base, values in ((0, new), (64, old)):
            for c in range(8):
                total = jnp.zeros((8, 128), F32)
                for h in range(2):
                    here = jnp.where(quarter == 2 * h + stations, values[c], 0.0)
                    total = total + pltpu.roll(here, (64 * core + 96 * stations + 96 * h) % 128, 1)
                out[base + c * 8:base + (c + 1) * 8, :] = total


def finish_kernel(moments, keep, recv, rho_f, tables, gains, duals, poly, thin, deep):
    chan = lax.axis_index("chan")
    rho = rho_f[...]
    low = lanes() < 64

    def combine(row):
        parts = [fit(tables, row, moments, half * 32, 64, 4) for half in range(2)]
        real = [jnp.where(low, a, pltpu.roll(b, 64, 1)) for a, b in zip(*parts)]
        imag = [jnp.where(low, pltpu.roll(a, 64, 1), b) for a, b in zip(*parts)]
        return real + imag

    def place(ref, value, first, stride):
        for q in range(4):
            part = pltpu.roll(value, 128 - 32 * q, 1) if q else value
            ref[pl.ds(q * 8 * stride + first, 8, stride=stride), :] = part

    for t in range(TERMS):
        for c, value in enumerate(combine(8 + t)):
            place(deep, value, c * 4 + t, 32)
    poly[...] = deep[:, 0:32].reshape(32, 8, 4, 32)
    fitted = combine(chan)
    now = [keep[c * 8:(c + 1) * 8, :] + recv[c * 8:(c + 1) * 8, :] for c in range(16)]
    for c in range(8):
        place(thin, now[c], c, 8)
    gains[...] = thin[:, 0:32].reshape(32, 8, 32)
    for c in range(8):
        place(thin, now[8 + c] + rho * (now[c] - fitted[c]), c, 8)
    duals[...] = thin[:, 0:32].reshape(32, 8, 32)


def local(coherency, visibilities, station_pairs, gains, duals, poly, penalty):
    basis, solve, hat = consensus_tables()
    constants = np.zeros((12, 12), np.float32)
    constants[:8, :4] = basis
    constants[:8, 4:] = hat
    constants[8:, 4:] = solve
    tables = jnp.asarray(constants)

    def swap(x):
        return lax.ppermute(x, "core", CORE_SWAP)

    def exchange(x, axis):
        return lax.all_to_all(x, axis, 0, 0, tiled=True)

    packed = ((64, 128), F32)
    wide = ((512, 128), F32)
    small = ((8, 128), F32)
    state_in = pltpu.VMEM((32, 8, 32), F32)
    thin = pltpu.VMEM((256, 128), F32)
    spread, mark = call(
        spread_kernel, [wide, small], [thin], n_in=1
    )(gains[0])
    gathered = exchange(spread, ("st", "core"))
    coh_keep, state_keep, rho_a, rho_f, *send = call(
        prepare_kernel,
        [((128, ROWS), F32), ((192, 128), F32), small, small] + [((40, ROWS), F32)] * 4,
        [
            pltpu.VMEM((32, 8, ROWS), BF16), state_in, state_in, pltpu.VMEM((32, 8, TERMS, 32), F32),
            pltpu.VMEM((ROWS // 128, 256, 128), F32), thin, pltpu.SemaphoreType.DMA((4,)),
        ],
        smem=(6, 7), hbm=(0, 1, 2, 3, 4), n_in=8,
    )(mark, coherency[0], gains[0], duals[0], poly, station_pairs, penalty, tables)
    received = [swap(x) for x in send]
    vis = visibilities[0]

    model_outs = [((128, 2 * ROWS), F32), ((128, 2 * ROWS), F32), ((8, 2 * ROWS), F32)]
    model_scratch = [
        pltpu.VMEM((256, STATIONS), BF16), pltpu.VMEM((2, 128, BLOCK), F32), pltpu.VMEM((2, 128, BLOCK), F32)
    ]
    sums_out = ((768, 128), F32)
    blocks = 2 * ROWS // BLOCK
    sums_scratch = [
        pltpu.VMEM((blocks, 384, 2 * BLOCK), BF16),
        pltpu.VMEM((384, STATIONS), F32),
        pltpu.VMEM((blocks, STATIONS, 2 * BLOCK), BF16),
    ]
    z, w, own, pairs, gain, dual, target = call(
        first_model_kernel,
        model_outs + [((2, 2 * ROWS), jnp.int32), packed, packed, packed],
        model_scratch, n_in=10,
    )(gathered, coh_keep, *received, vis, station_pairs, state_keep, rho_a)

    def step_model(spread):
        gathered = exchange(spread, "st")
        return call(model_kernel, model_outs, model_scratch, n_in=8)(
            gathered, coh_keep, *received, vis, pairs
        )

    def step_sums(z, w, own):
        (parts,) = call(sums_kernel, [sums_out], sums_scratch, n_in=5)(z, w, own, swap(own), pairs)
        return exchange(parts, "st")

    gain, spread = call(update_kernel, [packed, wide], n_in=4)(step_sums(z, w, own), gain, target, rho_a)
    gain, spread, moment = call(update_moment_kernel, [packed, wide, wide], n_in=5)(
        step_sums(*step_model(spread)), gain, target, dual, rho_a
    )
    moments = exchange(moment, "chan")
    gain, spread, dual, target = call(
        update_consensus_kernel, [packed, wide, packed, packed], smem=(5,), n_in=6
    )(step_sums(*step_model(spread)), gain, moments, dual, rho_a, tables)
    keep, send, moment = call(update_last_kernel, [((128, 128), F32), ((128, 128), F32), wide], n_in=5)(
        step_sums(*step_model(spread)), gain, target, dual, rho_a
    )
    moments = exchange(moment, ("chan", "core"))
    gains_out, duals_out, poly_out = call(
        finish_kernel,
        [((32, 8, 32), F32), ((32, 8, 32), F32), ((32, 8, 4, 32), F32)],
        [pltpu.VMEM((256, 128), F32), pltpu.VMEM((1024, 128), F32)],
        smem=(4,), n_in=5,
    )(moments, keep, swap(send), rho_f, tables)
    return gains_out[None], duals_out[None], poly_out


def solution(mesh):
    chan, bl = mesh.devices.shape
    finer = Mesh(mesh.devices.reshape(chan, bl // 2, 2), ("chan", "st", "core"))
    both = ("st", "core")
    in_specs = (
        P("chan", None, None, both),
        P("chan", None, both),
        P(None, both),
        P("chan", None, None, both),
        P("chan", None, None, both),
        P(None, None, None, both),
        P(),
    )
    out_specs = (
        P("chan", None, None, both),
        P("chan", None, None, both),
        P(None, None, None, both),
    )
    return jax.shard_map(local, mesh=finer, in_specs=in_specs, out_specs=out_specs, check_vma=False)
```

```python
import jax
import jax.numpy as jnp
import numpy as np
from jax import lax
from jax.experimental import pallas as pl
from jax.experimental.pallas import tpu as pltpu
from jax.sharding import Mesh, PartitionSpec as P


CHANNELS = 8
TERMS = 4
ROWS = 1024
BLOCK = 256
STATIONS = 512
F32 = jnp.float32
BF16 = jnp.bfloat16
CORE_SWAP = [(0, 1), (1, 0)]
VMEM_BYTES = 24 * 1024 * 1024


def basis_of(place):
    square = place * place
    return [1.0 + 0.0 * place, place, 1.5 * square - 0.5, (2.5 * square - 1.5) * place]


def consensus_tables():
    basis = np.stack(basis_of((2.0 * np.arange(CHANNELS) + 1.0) / CHANNELS - 1.0), axis=1)
    inverse = np.linalg.inv(basis.T @ basis)
    return inverse, inverse @ basis.T


GRAM_INVERSE, SOLVE = consensus_tables()


def basis_at(channel):
    place = (2.0 * jnp.full((8, 128), channel, jnp.int32).astype(F32) + 1.0) / CHANNELS - 1.0
    return basis_of(place)


def dot_terms(a, b):
    total = a[0] * b[0]
    for t in range(1, TERMS):
        total = total + a[t] * b[t]
    return total


def weigh(values):
    return [
        sum(float(GRAM_INVERSE[t, u]) * values[u] for u in range(t % 2, TERMS, 2)) for t in range(TERMS)
    ]


def call(kernel, out_shapes, scratch=(), hbm=(), hbm_out=(), n_in=0):
    def specs(count, outside):
        return [pl.BlockSpec(memory_space=pl.ANY if i in outside else pltpu.VMEM) for i in range(count)]

    return pl.pallas_call(
        kernel,
        out_shape=[jax.ShapeDtypeStruct(s, d) for s, d in out_shapes],
        in_specs=specs(n_in, hbm),
        out_specs=specs(len(out_shapes), hbm_out),
        scratch_shapes=list(scratch),
        compiler_params=pltpu.CompilerParams(vmem_limit_bytes=VMEM_BYTES),
        cost_estimate=pl.CostEstimate(flops=0, bytes_accessed=1000, transcendentals=0),
    )


def lanes():
    return lax.broadcasted_iota(jnp.int32, (8, 128), 1)


def split_parts(x):
    high = x.astype(BF16)
    return high, (x - high.astype(F32)).astype(BF16)


def matrix(load):
    return [load(i) for i in range(4)], [load(4 + i) for i in range(4)]


def conj_t(m):
    re, im = m
    return [re[0], re[2], re[1], re[3]], [-im[0], -im[2], -im[1], -im[3]]


def product_nh(a, b):
    (ar, ai), (br, bi) = a, b
    re, im = [], []
    for i in (0, 1):
        for j in (0, 1):
            p, q, u, v = 2 * i, 2 * i + 1, 2 * j, 2 * j + 1
            re.append((ar[p] * br[u] + ai[p] * bi[u]) + (ar[q] * br[v] + ai[q] * bi[v]))
            im.append((ai[p] * br[u] - ar[p] * bi[u]) + (ai[q] * br[v] - ar[q] * bi[v]))
    return re, im


def product_hn(a, b):
    (ar, ai), (br, bi) = a, b
    re, im = [], []
    for i in (0, 1):
        for j in (0, 1):
            p, q, u, v = i, 2 + i, j, 2 + j
            re.append((ar[p] * br[u] + ai[p] * bi[u]) + (ar[q] * br[v] + ai[q] * bi[v]))
            im.append((ar[p] * bi[u] - ai[p] * br[u]) + (ar[q] * bi[v] - ai[q] * br[v]))
    return re, im


def product(a, b):
    (ar, ai), (br, bi) = a, b
    re, im = [], []
    for i in (0, 1):
        for j in (0, 1):
            p, q, u, v = 2 * i, 2 * i + 1, j, 2 + j
            re.append((ar[p] * br[u] - ai[p] * bi[u]) + (ar[q] * br[v] - ai[q] * bi[v]))
            im.append((ar[p] * bi[u] + ai[p] * br[u]) + (ar[q] * bi[v] + ai[q] * br[v]))
    return re, im


def square_nh(a):
    r, i = a
    return [
        (r[0] * r[0] + i[0] * i[0]) + (r[1] * r[1] + i[1] * i[1]),
        (r[2] * r[2] + i[2] * i[2]) + (r[3] * r[3] + i[3] * i[3]),
        (r[0] * r[2] + i[0] * i[2]) + (r[1] * r[3] + i[1] * i[3]),
        (i[0] * r[2] - r[0] * i[2]) + (i[1] * r[3] - r[1] * i[3]),
    ]


def square_hn(a):
    r, i = a
    return [
        (r[0] * r[0] + i[0] * i[0]) + (r[2] * r[2] + i[2] * i[2]),
        (r[1] * r[1] + i[1] * i[1]) + (r[3] * r[3] + i[3] * i[3]),
        (r[0] * r[1] + i[0] * i[1]) + (r[2] * r[3] + i[2] * i[3]),
        (r[0] * i[1] - i[0] * r[1]) + (r[2] * i[3] - i[2] * r[3]),
    ]


def spread_kernel(gains, spread, mark, thin):
    thin[...] = jnp.zeros((256, 128), F32)
    mark[...] = jnp.zeros((8, 128), F32)
    thin[:, 0:32] = gains[...].reshape(256, 32)
    for half in range(2):
        for c in range(4):
            total = None
            for im in range(2):
                for h in range(2):
                    part = thin[pl.ds((half * 16 + h * 8) * 8 + im * 4 + c, 8, stride=8), :]
                    if im or h:
                        part = pltpu.roll(part, im * 64 + h * 32, 1)
                    total = part if total is None else total + part
            for d in range(8):
                at = (2 * d + half) * 32 + c * 8
                spread[at:at + 8, :] = total


def prepare_kernel(
    mark, coh_hbm, gains_hbm, duals_hbm, poly_hbm, pairs, penalty,
    coh_keep, state_keep, rho_a, rho_f, send_0, send_1, send_2, send_3,
    coh, gains, duals, poly, wide, thin, sems,
):
    send = (send_0, send_1, send_2, send_3)
    copies = [
        pltpu.make_async_copy(src, dst, sems.at[i])
        for i, (src, dst) in enumerate(((gains_hbm, gains), (duals_hbm, duals), (poly_hbm, poly), (coh_hbm, coh)))
    ]
    for copy in copies:
        copy.start()
    core = lax.axis_index("core")
    chan = lax.axis_index("chan")
    row = lax.broadcasted_iota(jnp.int32, (8, 128), 0)
    lane = lanes()
    given = jnp.broadcast_to(penalty[...], (8, 128))
    column = [jnp.sum(jnp.where(lane == q * 8 + row, given, 0.0), axis=1, keepdims=True) for q in range(4)]
    by_dir = jnp.broadcast_to(column[0], (8, 128))
    for q in range(1, 4):
        by_dir = jnp.where(lane // 32 == q, column[q], by_dir)
    mine = jnp.full((8, 128), core, jnp.int32) == 0
    low = jnp.where(mine, column[0], column[2])
    high = jnp.where(mine, column[1], column[3])
    rho_a[...] = jnp.where(lane < 64, low, high)
    rho_f[...] = by_dir
    send_3[32:40, :] = jnp.zeros((8, ROWS), F32)
    send_3[32:34, :] = pairs[...].astype(F32)

    def pack(which):
        for c in range(8):
            for keep, half in ((True, core), (False, 1 - core)):
                total = None
                for h in range(2):
                    part = thin[pl.ds((half * 16 + h * 8) * 8 + c, 8, stride=8), :]
                    part = pltpu.roll(part, h * 64 + core * 32, 1)
                    total = part if total is None else total + part
                if keep:
                    state_keep[which * 64 + c * 8:which * 64 + (c + 1) * 8, :] = total
                else:
                    send[which][32:40, c * 128:(c + 1) * 128] = total

    thin[...] = jnp.zeros((256, 128), F32)
    copies[0].wait()
    thin[:, 0:32] = gains[...].reshape(256, 32)
    pack(0)
    copies[1].wait()
    thin[:, 0:32] = duals[...].reshape(256, 32)
    pack(1)
    copies[2].wait()
    place = (2.0 * chan.astype(F32) + 1.0) * (1.0 / CHANNELS) - 1.0
    basis = basis_of(place)
    fitted = poly[:, :, 0, :]
    for t in range(1, TERMS):
        fitted = fitted + poly[:, :, t, :] * basis[t]
    thin[:, 0:32] = fitted.reshape(256, 32)
    pack(2)
    copies[3].wait()
    for t in range(ROWS // 128):
        cols = slice(t * 128, (t + 1) * 128)
        wide[t] = coh[:, :, cols].astype(F32).reshape(256, 128)
        for c in range(8):
            coh_keep[c * 16:(c + 1) * 16, cols] = wide[t, pl.ds(core * 128 + c, 16, stride=8), :]
            send[c // 2][(c % 2) * 16:(c % 2) * 16 + 16, cols] = wide[t, pl.ds((1 - core) * 128 + c, 16, stride=8), :]


def one_hot(pairs, side, j):
    index = jnp.broadcast_to(pairs[side:side + 1, j * BLOCK:(j + 1) * BLOCK], (16, BLOCK)).astype(jnp.int16)
    index = jnp.concatenate([index] * (STATIONS // 16), axis=0)
    here = lax.broadcasted_iota(jnp.int16, (STATIONS, BLOCK), 0) == index
    return jnp.where(here, jnp.ones((STATIONS, BLOCK), BF16), jnp.zeros((STATIONS, BLOCK), BF16))


def put_table(table, c, t, first, second):
    high, rest = split_parts(jnp.concatenate([first, second], axis=0))
    table[c * 16:(c + 1) * 16, t * 128:(t + 1) * 128] = high
    table[128 + c * 16:128 + (c + 1) * 16, t * 128:(t + 1) * 128] = rest


def start_table(gathered, table):
    lane = lanes()
    for c in range(8):
        im, row = divmod(c, 4)
        for t in range(4):
            halves = []
            for h in range(2):
                total = None
                for b in range(4):
                    part = gathered[(4 * t + b) * 32 + row * 8:(4 * t + b) * 32 + row * 8 + 8, :]
                    shift = (b * 32 - im * 64 - h * 32) % 128
                    if shift:
                        part = pltpu.roll(part, shift, 1)
                    total = part if total is None else jnp.where(lane // 32 == b, part, total)
                halves.append(total)
            put_table(table, c, t, *halves)


def step_table(gathered, table):
    low = lanes() < 64
    for c in range(8):
        for t in range(4):
            a = gathered[(2 * t) * 64 + c * 8:(2 * t) * 64 + c * 8 + 8, :]
            b = gathered[(2 * t + 1) * 64 + c * 8:(2 * t + 1) * 64 + c * 8 + 8, :]
            first = jnp.where(low, a, pltpu.roll(b, 64, 1))
            second = jnp.where(low, pltpu.roll(a, 64, 1), b)
            put_table(table, c, t, first, second)


def first_model_kernel(
    gathered, coh_own, recv_0, recv_1, recv_2, recv_3, vis, pairs_own, state_keep, rho_a,
    z_ref, w_ref, s_ref, pairs, gains, duals, target, table, near, far,
):
    received = (recv_0, recv_1, recv_2, recv_3)
    pairs[0:2, 0:ROWS] = pairs_own[...]
    pairs[0:2, ROWS:] = recv_3[32:34, :].astype(jnp.int32)
    half_rho = 0.5 * rho_a[...]
    for c in range(8):
        at = c * 8
        state = [
            state_keep[which * 64 + at:which * 64 + at + 8, :]
            + received[which][32:40, c * 128:(c + 1) * 128]
            for which in range(3)
        ]
        gains[at:at + 8, :] = state[0]
        duals[at:at + 8, :] = state[1]
        target[at:at + 8, :] = half_rho * state[2] - 0.5 * state[1]
    start_table(gathered, table)
    model(coh_own, received, vis, pairs, z_ref, w_ref, s_ref, table, near, far)


def model_kernel(
    gathered, coh_own, recv_0, recv_1, recv_2, recv_3, vis, pairs, z_ref, w_ref, s_ref, table, near, far
):
    received = (recv_0, recv_1, recv_2, recv_3)
    step_table(gathered, table)
    model(coh_own, received, vis, pairs, z_ref, w_ref, s_ref, table, near, far)


def model_after_kernel(gathered, coh_own, recv_0, recv_1, recv_2, recv_3, vis, pairs, after, *rest):
    model_kernel(gathered, coh_own, recv_0, recv_1, recv_2, recv_3, vis, pairs, *rest)


def model(coh_own, received, vis, pairs, z_ref, w_ref, s_ref, table, near, far):
    for j in range(2 * ROWS // BLOCK):
        own = j < ROWS // BLOCK
        col = (j * BLOCK) % ROWS
        for side, dest in ((0, near), (1, far)):
            both = jnp.dot(table[...], one_hot(pairs, side, j), preferred_element_type=F32)
            dest[j % 2] = both[:128] + both[128:]
        for l in range(BLOCK // 128):
            src = col + l * 128
            dst = j * BLOCK + l * 128
            gp = matrix(lambda i: near[j % 2, i * 16:(i + 1) * 16, l * 128:(l + 1) * 128])
            gq = matrix(lambda i: far[j % 2, i * 16:(i + 1) * 16, l * 128:(l + 1) * 128])
            if own:
                cc = matrix(lambda i: coh_own[i * 16:(i + 1) * 16, src:src + 128])
            else:
                cc = matrix(lambda i: received[i // 2][(i % 2) * 16:(i % 2) * 16 + 16, src:src + 128])
            z = product_nh(cc, gq)
            w = product(gp, cc)
            m = product(gp, z)
            for i in range(8):
                z_ref[i * 16:(i + 1) * 16, dst:dst + 128] = z[i // 4][i % 4]
                w_ref[i * 16:(i + 1) * 16, dst:dst + 128] = w[i // 4][i % 4]
                total = -jnp.sum(m[i // 4][i % 4], axis=0, keepdims=True)
                if own:
                    total = total + vis[i:i + 1, src:src + 128]
                s_ref[i:i + 1, dst:dst + 128] = total


def message_sums_kernel(
    z_ref, w_ref, s_own, s_other, pairs, moment, moment_z, out, part_0, part_1, part_2, part_3, left, acc, hot
):
    chan = lax.axis_index("chan")
    near = weigh(basis_at(chan))
    far = weigh(basis_at(chan ^ 4))
    own = comps(moment)
    other = comps(moment_z)
    for d, part in enumerate((part_0, part_1, part_2, part_3)):
        at = basis_at(chan ^ d)
        near_weight = dot_terms(at, near)
        far_weight = dot_terms(at, far)
        put(part, [near_weight * own[c] + far_weight * other[c] for c in range(8)])
    sums_kernel(z_ref, w_ref, s_own, s_other, pairs, out, left, acc, hot)


def sums_kernel(z_ref, w_ref, s_own, s_other, pairs, out, left, acc, hot):
    steps = 2 * ROWS // BLOCK
    for j in range(steps):
        for l in range(BLOCK // 128):
            src = j * BLOCK + l * 128
            swapped = (src + ROWS) % (2 * ROWS)
            r = matrix(lambda i: s_own[i:i + 1, src:src + 128] + s_other[i:i + 1, swapped:swapped + 128])
            z = matrix(lambda i: z_ref[i * 16:(i + 1) * 16, src:src + 128])
            w = matrix(lambda i: w_ref[i * 16:(i + 1) * 16, src:src + 128])
            for side, (num, den) in enumerate(
                ((product_nh(r, z), square_nh(z)), (product_hn(r, w), square_hn(w)))
            ):
                at = side * BLOCK + l * 128
                for i, value in enumerate(num[0] + num[1] + den):
                    high, rest = split_parts(value)
                    left[j, i * 16:(i + 1) * 16, at:at + 128] = high
                    left[j, 192 + i * 16:192 + (i + 1) * 16, at:at + 128] = rest
        for side in range(2):
            hot[j, :, side * BLOCK:(side + 1) * BLOCK] = one_hot(pairs, side, j)
        total = lax.dot_general(left[j], hot[j], (((1,), (1,)), ((), ())), preferred_element_type=F32)
        if j == 0:
            acc[...] = total
        else:
            acc[...] += total
    low = lanes() < 64
    for c in range(12):
        for t in range(4):
            cols = slice(t * 128, (t + 1) * 128)
            at = c * 16
            v0 = acc[at:at + 8, cols] + acc[192 + at:192 + at + 8, cols]
            v1 = acc[at + 8:at + 16, cols] + acc[192 + at + 8:192 + at + 16, cols]
            out[(2 * t) * 96 + c * 8:(2 * t) * 96 + c * 8 + 8, :] = jnp.where(low, v0, pltpu.roll(v1, 64, 1))
            out[(2 * t + 1) * 96 + c * 8:(2 * t + 1) * 96 + c * 8 + 8, :] = jnp.where(low, pltpu.roll(v0, 64, 1), v1)


def updated(received, gains, target, rho):
    sums = []
    for c in range(12):
        parts = [received[d * 96 + c * 8:d * 96 + c * 8 + 8, :] for d in range(8)]
        while len(parts) > 1:
            parts = [parts[i] + parts[i + 1] for i in range(0, len(parts), 2)]
        sums.append(parts[0])
    half_rho = 0.5 * rho
    a, d, br, bi = sums[8] + half_rho, sums[9] + half_rho, sums[10], sums[11]
    scale = 0.5 / (a * d - br * br - bi * bi)
    n = [sums[i] + target[i] - half_rho * gains[i] for i in range(8)]
    result = [None] * 8
    for i in (0, 1):
        r0, r1, i0, i1 = n[2 * i], n[2 * i + 1], n[4 + 2 * i], n[5 + 2 * i]
        result[2 * i] = gains[2 * i] + scale * (r0 * d - (r1 * br + i1 * bi))
        result[4 + 2 * i] = gains[4 + 2 * i] + scale * (i0 * d - (i1 * br - r1 * bi))
        result[2 * i + 1] = gains[2 * i + 1] + scale * (r1 * a - (r0 * br - i0 * bi))
        result[5 + 2 * i] = gains[5 + 2 * i] + scale * (i1 * a - (i0 * br + r0 * bi))
    return result


def comps(ref):
    return [ref[c * 8:(c + 1) * 8, :] for c in range(8)]


def put(ref, values, base=0):
    for c in range(8):
        ref[base + c * 8:base + (c + 1) * 8, :] = values[c]


def update_kernel(received, gains, target, rho_a, gains_new, spread):
    new = updated(received, comps(gains), comps(target), rho_a[...])
    put(gains_new, new)
    for d in range(8):
        put(spread, new, d * 64)


def update_moment_kernel(received, gains, target, duals, rho_a, gains_new, spread, moment):
    rho = rho_a[...]
    new = updated(received, comps(gains), comps(target), rho)
    put(gains_new, new)
    for d in range(8):
        put(spread, new, d * 64)
    old = comps(duals)
    put(moment, [old[c] + rho * new[c] for c in range(8)])


def update_consensus_kernel(
    received, gains, part_0, part_1, part_2, part_3, duals, rho_a, gains_new, spread, duals_new, target
):
    rho = rho_a[...]
    old_gains = comps(gains)
    old_duals = comps(duals)
    parts = [comps(part) for part in (part_0, part_1, part_2, part_3)]
    fitted = [(parts[0][c] + parts[1][c]) + (parts[2][c] + parts[3][c]) for c in range(8)]
    new_duals = [old_duals[c] + rho * (old_gains[c] - fitted[c]) for c in range(8)]
    aim = [0.5 * (rho * fitted[c] - new_duals[c]) for c in range(8)]
    put(duals_new, new_duals)
    put(target, aim)
    new = updated(received, old_gains, aim, rho)
    put(gains_new, new)
    for d in range(8):
        put(spread, new, d * 64)


def update_last_kernel(received, gains, target, duals, rho_a, keep, send, moment):
    core = lax.axis_index("core")
    rho = rho_a[...]
    new = updated(received, comps(gains), comps(target), rho)
    old = comps(duals)
    lane = lanes()
    quarter = lane // 32
    whole = [old[c] + rho * new[c] for c in range(8)]
    for half in range(2):
        for c in range(4):
            total = jnp.zeros((8, 128), F32)
            for im in range(2):
                for h in range(2):
                    here = jnp.where(quarter == 2 * h + half, whole[im * 4 + c], 0.0)
                    shift = (im * 64 - 32 * h - 32 * half) % 128
                    total = total + (pltpu.roll(here, shift, 1) if shift else here)
            for f in range(CHANNELS):
                at = (2 * f + half) * 32 + c * 8
                moment[at:at + 8, :] = total
    for out, stations in ((keep, core), (send, 1 - core)):
        for base, values in ((0, new), (64, old)):
            for c in range(8):
                total = jnp.zeros((8, 128), F32)
                for h in range(2):
                    here = jnp.where(quarter == 2 * h + stations, values[c], 0.0)
                    total = total + pltpu.roll(here, (64 * core + 96 * stations + 96 * h) % 128, 1)
                out[base + c * 8:base + (c + 1) * 8, :] = total


def finish_kernel(
    moments_hbm, keep, recv, rho_f, gains_hbm, duals_hbm, poly_hbm,
    moments, gains, duals, poly, thin, deep, sems,
):
    load = pltpu.make_async_copy(moments_hbm, moments, sems.at[0])
    load.start()
    chan = lax.axis_index("chan")
    rho = rho_f[...]
    low = lanes() < 64

    def place(ref, value, first, stride):
        for q in range(4):
            part = pltpu.roll(value, 128 - 32 * q, 1) if q else value
            ref[pl.ds(q * 8 * stride + first, 8, stride=stride), :] = part

    now = [keep[c * 8:(c + 1) * 8, :] + recv[c * 8:(c + 1) * 8, :] for c in range(16)]
    for c in range(8):
        place(thin, now[c], c, 8)
    gains[...] = thin[:, 0:32].reshape(32, 8, 32)
    stores = [pltpu.make_async_copy(gains, gains_hbm, sems.at[1])]
    stores[0].start()
    load.wait()
    at = basis_at(chan)
    fitted = [None] * 8
    for t in range(TERMS):
        halves = []
        for half in range(2):
            for c in range(4):
                total = None
                for f in range(CHANNELS):
                    row = f * 64 + half * 32 + c * 8
                    part = float(SOLVE[t, f]) * moments[row:row + 8, :]
                    total = part if total is None else total + part
                halves.append(total)
        real = [jnp.where(low, halves[c], pltpu.roll(halves[4 + c], 64, 1)) for c in range(4)]
        imag = [jnp.where(low, pltpu.roll(halves[c], 64, 1), halves[4 + c]) for c in range(4)]
        for c, value in enumerate(real + imag):
            place(deep, value, c * 4 + t, 32)
            fitted[c] = value if t == 0 else fitted[c] + at[t] * value
    poly[...] = deep[:, 0:32].reshape(32, 8, 4, 32)
    stores.append(pltpu.make_async_copy(poly, poly_hbm, sems.at[2]))
    stores[1].start()
    for c in range(8):
        place(thin, now[8 + c] + rho * (now[c] - fitted[c]), c, 8)
    duals[...] = thin[:, 0:32].reshape(32, 8, 32)
    stores.append(pltpu.make_async_copy(duals, duals_hbm, sems.at[3]))
    stores[2].start()
    for store in stores:
        store.wait()


def local(coherency, visibilities, station_pairs, gains, duals, poly, penalty):
    def swap(x):
        return lax.ppermute(x, "core", CORE_SWAP)

    def exchange(x, axis):
        return lax.all_to_all(x, axis, 0, 0, tiled=True)

    packed = ((64, 128), F32)
    wide = ((512, 128), F32)
    small = ((8, 128), F32)
    state_in = pltpu.VMEM((32, 8, 32), F32)
    thin = pltpu.VMEM((256, 128), F32)
    spread, mark = call(
        spread_kernel, [wide, small], [thin], n_in=1
    )(gains[0])
    gathered = exchange(spread, ("st", "core"))
    coh_keep, state_keep, rho_a, rho_f, *send = call(
        prepare_kernel,
        [((128, ROWS), F32), ((192, 128), F32), small, small] + [((40, ROWS), F32)] * 4,
        [
            pltpu.VMEM((32, 8, ROWS), BF16), state_in, state_in, pltpu.VMEM((32, 8, TERMS, 32), F32),
            pltpu.VMEM((ROWS // 128, 256, 128), F32), thin, pltpu.SemaphoreType.DMA((4,)),
        ],
        hbm=(0, 1, 2, 3, 4), n_in=7,
    )(mark, coherency[0], gains[0], duals[0], poly, station_pairs, jnp.pad(penalty, (0, 96)).reshape(1, 128))
    received = [swap(x) for x in send]
    vis = visibilities[0]

    model_outs = [((128, 2 * ROWS), F32), ((128, 2 * ROWS), F32), ((8, 2 * ROWS), F32)]
    model_scratch = [
        pltpu.VMEM((256, STATIONS), BF16), pltpu.VMEM((2, 128, BLOCK), F32), pltpu.VMEM((2, 128, BLOCK), F32)
    ]
    sums_out = ((768, 128), F32)
    blocks = 2 * ROWS // BLOCK
    sums_scratch = [
        pltpu.VMEM((blocks, 384, 2 * BLOCK), BF16),
        pltpu.VMEM((384, STATIONS), F32),
        pltpu.VMEM((blocks, STATIONS, 2 * BLOCK), BF16),
    ]
    z, w, own, pairs, gain, dual, target = call(
        first_model_kernel,
        model_outs + [((2, 2 * ROWS), jnp.int32), packed, packed, packed],
        model_scratch, n_in=10,
    )(gathered, coh_keep, *received, vis, station_pairs, state_keep, rho_a)

    def step_model(spread, *after):
        gathered = exchange(spread, "st")
        kernel = model_after_kernel if after else model_kernel
        return call(kernel, model_outs, model_scratch, hbm=(8,), n_in=8 + len(after))(
            gathered, coh_keep, *received, vis, pairs, *after
        )

    def step_sums(z, w, own):
        (parts,) = call(sums_kernel, [sums_out], sums_scratch, n_in=5)(z, w, own, swap(own), pairs)
        return exchange(parts, "st")

    gain, spread = call(update_kernel, [packed, wide], n_in=4)(step_sums(z, w, own), gain, target, rho_a)
    gain, spread, moment = call(update_moment_kernel, [packed, wide, packed], n_in=5)(
        step_sums(*step_model(spread)), gain, target, dual, rho_a
    )

    def from_channel(x, distance):
        return lax.ppermute(x, "chan", [(f, f ^ distance) for f in range(CHANNELS)])

    moment_z = from_channel(moment, 4)
    z, w, own = step_model(spread, moment_z)
    parts, *messages = call(message_sums_kernel, [sums_out] + [packed] * 4, sums_scratch, n_in=7)(
        z, w, own, swap(own), pairs, moment, moment_z
    )
    shares = [messages[0]] + [from_channel(messages[d], d) for d in (1, 2, 3)]
    gain, spread, dual, target = call(update_consensus_kernel, [packed, wide, packed, packed], n_in=8)(
        exchange(parts, "st"), gain, *shares, dual, rho_a
    )
    keep, send, moment = call(update_last_kernel, [((128, 128), F32), ((128, 128), F32), wide], n_in=5)(
        step_sums(*step_model(spread)), gain, target, dual, rho_a
    )
    moments = exchange(moment, ("chan", "core"))
    gains_out, duals_out, poly_out = call(
        finish_kernel,
        [((32, 8, 32), F32), ((32, 8, 32), F32), ((32, 8, 4, 32), F32)],
        [
            pltpu.VMEM((512, 128), F32), state_in, state_in, pltpu.VMEM((32, 8, TERMS, 32), F32),
            thin, pltpu.VMEM((1024, 128), F32), pltpu.SemaphoreType.DMA((4,)),
        ],
        hbm=(0,), hbm_out=(0, 1, 2), n_in=4,
    )(moments, keep, swap(send), rho_f)
    return gains_out[None], duals_out[None], poly_out


def solution(mesh):
    chan, bl = mesh.devices.shape
    finer = Mesh(mesh.devices.reshape(chan, bl // 2, 2), ("chan", "st", "core"))
    both = ("st", "core")
    in_specs = (
        P("chan", None, None, both),
        P("chan", None, both),
        P(None, both),
        P("chan", None, None, both),
        P("chan", None, None, both),
        P(None, None, None, both),
        P(),
    )
    out_specs = (
        P("chan", None, None, both),
        P("chan", None, None, both),
        P(None, None, None, both),
    )
    return jax.shard_map(local, mesh=finer, in_specs=in_specs, out_specs=out_specs, check_vma=False)
```

```python
import jax
import jax.numpy as jnp
import numpy as np
from jax import lax
from jax.experimental import pallas as pl
from jax.experimental.pallas import tpu as pltpu
from jax.sharding import Mesh, PartitionSpec as P


CHANNELS = 8
TERMS = 4
ROWS = 1024
BLOCK = 256
STATIONS = 512
F32 = jnp.float32
BF16 = jnp.bfloat16
CORE_SWAP = [(0, 1), (1, 0)]
VMEM_BYTES = 24 * 1024 * 1024


def basis_of(place):
    square = place * place
    return [1.0 + 0.0 * place, place, 1.5 * square - 0.5, (2.5 * square - 1.5) * place]


def consensus_tables():
    basis = np.stack(basis_of((2.0 * np.arange(CHANNELS) + 1.0) / CHANNELS - 1.0), axis=1)
    inverse = np.linalg.inv(basis.T @ basis)
    return inverse, inverse @ basis.T


GRAM_INVERSE, SOLVE = consensus_tables()


def basis_at(channel):
    place = (2.0 * jnp.full((8, 128), channel, jnp.int32).astype(F32) + 1.0) / CHANNELS - 1.0
    return basis_of(place)


def dot_terms(a, b):
    total = a[0] * b[0]
    for t in range(1, TERMS):
        total = total + a[t] * b[t]
    return total


def weigh(values):
    return [
        sum(float(GRAM_INVERSE[t, u]) * values[u] for u in range(t % 2, TERMS, 2)) for t in range(TERMS)
    ]


def call(kernel, out_shapes, scratch=(), hbm=(), hbm_out=(), n_in=0):
    def specs(count, outside):
        return [pl.BlockSpec(memory_space=pl.ANY if i in outside else pltpu.VMEM) for i in range(count)]

    return pl.pallas_call(
        kernel,
        out_shape=[jax.ShapeDtypeStruct(s, d) for s, d in out_shapes],
        in_specs=specs(n_in, hbm),
        out_specs=specs(len(out_shapes), hbm_out),
        scratch_shapes=list(scratch),
        compiler_params=pltpu.CompilerParams(vmem_limit_bytes=VMEM_BYTES),
        cost_estimate=pl.CostEstimate(flops=0, bytes_accessed=1000, transcendentals=0),
    )


def lanes():
    return lax.broadcasted_iota(jnp.int32, (8, 128), 1)


def split_parts(x):
    high = x.astype(BF16)
    return high, (x - high.astype(F32)).astype(BF16)


def matrix(load):
    return [load(i) for i in range(4)], [load(4 + i) for i in range(4)]


def conj_t(m):
    re, im = m
    return [re[0], re[2], re[1], re[3]], [-im[0], -im[2], -im[1], -im[3]]


def product_nh(a, b):
    (ar, ai), (br, bi) = a, b
    re, im = [], []
    for i in (0, 1):
        for j in (0, 1):
            p, q, u, v = 2 * i, 2 * i + 1, 2 * j, 2 * j + 1
            re.append((ar[p] * br[u] + ai[p] * bi[u]) + (ar[q] * br[v] + ai[q] * bi[v]))
            im.append((ai[p] * br[u] - ar[p] * bi[u]) + (ai[q] * br[v] - ar[q] * bi[v]))
    return re, im


def product_hn(a, b):
    (ar, ai), (br, bi) = a, b
    re, im = [], []
    for i in (0, 1):
        for j in (0, 1):
            p, q, u, v = i, 2 + i, j, 2 + j
            re.append((ar[p] * br[u] + ai[p] * bi[u]) + (ar[q] * br[v] + ai[q] * bi[v]))
            im.append((ar[p] * bi[u] - ai[p] * br[u]) + (ar[q] * bi[v] - ai[q] * br[v]))
    return re, im


def product(a, b):
    (ar, ai), (br, bi) = a, b
    re, im = [], []
    for i in (0, 1):
        for j in (0, 1):
            p, q, u, v = 2 * i, 2 * i + 1, j, 2 + j
            re.append((ar[p] * br[u] - ai[p] * bi[u]) + (ar[q] * br[v] - ai[q] * bi[v]))
            im.append((ar[p] * bi[u] + ai[p] * br[u]) + (ar[q] * bi[v] + ai[q] * br[v]))
    return re, im


def square_nh(a):
    r, i = a
    return [
        (r[0] * r[0] + i[0] * i[0]) + (r[1] * r[1] + i[1] * i[1]),
        (r[2] * r[2] + i[2] * i[2]) + (r[3] * r[3] + i[3] * i[3]),
        (r[0] * r[2] + i[0] * i[2]) + (r[1] * r[3] + i[1] * i[3]),
        (i[0] * r[2] - r[0] * i[2]) + (i[1] * r[3] - r[1] * i[3]),
    ]


def square_hn(a):
    r, i = a
    return [
        (r[0] * r[0] + i[0] * i[0]) + (r[2] * r[2] + i[2] * i[2]),
        (r[1] * r[1] + i[1] * i[1]) + (r[3] * r[3] + i[3] * i[3]),
        (r[0] * r[1] + i[0] * i[1]) + (r[2] * r[3] + i[2] * i[3]),
        (r[0] * i[1] - i[0] * r[1]) + (r[2] * i[3] - i[2] * r[3]),
    ]


def spread_kernel(gains, spread, mark, thin):
    thin[...] = jnp.zeros((256, 128), F32)
    mark[...] = jnp.zeros((8, 128), F32)
    thin[:, 0:32] = gains[...].reshape(256, 32)
    for half in range(2):
        for c in range(4):
            total = None
            for im in range(2):
                for h in range(2):
                    part = thin[pl.ds((half * 16 + h * 8) * 8 + im * 4 + c, 8, stride=8), :]
                    if im or h:
                        part = pltpu.roll(part, im * 64 + h * 32, 1)
                    total = part if total is None else total + part
            for d in range(8):
                at = (2 * d + half) * 32 + c * 8
                spread[at:at + 8, :] = total


def prepare_kernel(
    mark, coh_hbm, gains_hbm, duals_hbm, poly_hbm, pairs, penalty,
    coh_keep, state_keep, rho_a, rho_f, send_0, send_1, send_2, send_3,
    coh, gains, duals, poly, wide, thin, sems,
):
    send = (send_0, send_1, send_2, send_3)
    copies = [
        pltpu.make_async_copy(src, dst, sems.at[i])
        for i, (src, dst) in enumerate(((gains_hbm, gains), (duals_hbm, duals), (poly_hbm, poly), (coh_hbm, coh)))
    ]
    for copy in copies:
        copy.start()
    core = lax.axis_index("core")
    chan = lax.axis_index("chan")
    row = lax.broadcasted_iota(jnp.int32, (8, 128), 0)
    lane = lanes()
    given = jnp.broadcast_to(penalty[...], (8, 128))
    column = [jnp.sum(jnp.where(lane == q * 8 + row, given, 0.0), axis=1, keepdims=True) for q in range(4)]
    by_dir = jnp.broadcast_to(column[0], (8, 128))
    for q in range(1, 4):
        by_dir = jnp.where(lane // 32 == q, column[q], by_dir)
    mine = jnp.full((8, 128), core, jnp.int32) == 0
    low = jnp.where(mine, column[0], column[2])
    high = jnp.where(mine, column[1], column[3])
    rho_a[...] = jnp.where(lane < 64, low, high)
    rho_f[...] = by_dir
    send_3[32:40, :] = jnp.zeros((8, ROWS), F32)
    send_3[32:34, :] = pairs[...].astype(F32)

    def pack(which):
        for c in range(8):
            for keep, half in ((True, core), (False, 1 - core)):
                total = None
                for h in range(2):
                    part = thin[pl.ds((half * 16 + h * 8) * 8 + c, 8, stride=8), :]
                    part = pltpu.roll(part, h * 64 + core * 32, 1)
                    total = part if total is None else total + part
                if keep:
                    state_keep[which * 64 + c * 8:which * 64 + (c + 1) * 8, :] = total
                else:
                    send[which][32:40, c * 128:(c + 1) * 128] = total

    thin[...] = jnp.zeros((256, 128), F32)
    copies[0].wait()
    thin[:, 0:32] = gains[...].reshape(256, 32)
    pack(0)
    copies[1].wait()
    thin[:, 0:32] = duals[...].reshape(256, 32)
    pack(1)
    copies[2].wait()
    place = (2.0 * chan.astype(F32) + 1.0) * (1.0 / CHANNELS) - 1.0
    basis = basis_of(place)
    fitted = poly[:, :, 0, :]
    for t in range(1, TERMS):
        fitted = fitted + poly[:, :, t, :] * basis[t]
    thin[:, 0:32] = fitted.reshape(256, 32)
    pack(2)
    copies[3].wait()
    for t in range(ROWS // 128):
        cols = slice(t * 128, (t + 1) * 128)
        wide[t] = coh[:, :, cols].astype(F32).reshape(256, 128)
        for c in range(8):
            coh_keep[c * 16:(c + 1) * 16, cols] = wide[t, pl.ds(core * 128 + c, 16, stride=8), :]
            send[c // 2][(c % 2) * 16:(c % 2) * 16 + 16, cols] = wide[t, pl.ds((1 - core) * 128 + c, 16, stride=8), :]


def one_hot(pairs, first, side, j):
    index = pairs[first + side:first + side + 1, j * BLOCK:(j + 1) * BLOCK].astype(jnp.int32)
    index = jnp.broadcast_to(index, (16, BLOCK)).astype(jnp.int16)
    index = jnp.concatenate([index] * (STATIONS // 16), axis=0)
    here = lax.broadcasted_iota(jnp.int16, (STATIONS, BLOCK), 0) == index
    return jnp.where(here, jnp.ones((STATIONS, BLOCK), BF16), jnp.zeros((STATIONS, BLOCK), BF16))


def put_table(table, c, t, first, second):
    high, rest = split_parts(jnp.concatenate([first, second], axis=0))
    table[c * 16:(c + 1) * 16, t * 128:(t + 1) * 128] = high
    table[128 + c * 16:128 + (c + 1) * 16, t * 128:(t + 1) * 128] = rest


def start_table(gathered, table):
    lane = lanes()
    for c in range(8):
        im, row = divmod(c, 4)
        for t in range(4):
            halves = []
            for h in range(2):
                total = None
                for b in range(4):
                    part = gathered[(4 * t + b) * 32 + row * 8:(4 * t + b) * 32 + row * 8 + 8, :]
                    shift = (b * 32 - im * 64 - h * 32) % 128
                    if shift:
                        part = pltpu.roll(part, shift, 1)
                    total = part if total is None else jnp.where(lane // 32 == b, part, total)
                halves.append(total)
            put_table(table, c, t, *halves)


def step_table(gathered, table):
    low = lanes() < 64
    for c in range(8):
        for t in range(4):
            a = gathered[(2 * t) * 64 + c * 8:(2 * t) * 64 + c * 8 + 8, :]
            b = gathered[(2 * t + 1) * 64 + c * 8:(2 * t + 1) * 64 + c * 8 + 8, :]
            first = jnp.where(low, a, pltpu.roll(b, 64, 1))
            second = jnp.where(low, pltpu.roll(a, 64, 1), b)
            put_table(table, c, t, first, second)


def first_own_kernel(gathered, coh, vis, pairs, z_ref, w_ref, s_ref, table, near, far):
    start_table(gathered, table)
    model(lambda i: (coh, i * 16), vis, pairs, 0, z_ref, w_ref, s_ref, table, near, far)


def own_kernel(gathered, coh, vis, pairs, z_ref, w_ref, s_ref, table, near, far):
    step_table(gathered, table)
    model(lambda i: (coh, i * 16), vis, pairs, 0, z_ref, w_ref, s_ref, table, near, far)


def own_after_kernel(gathered, coh, vis, pairs, after, *rest):
    own_kernel(gathered, coh, vis, pairs, *rest)


def other_kernel(table, recv_0, recv_1, recv_2, recv_3, z_ref, w_ref, s_ref, near, far):
    received = (recv_0, recv_1, recv_2, recv_3)
    model(lambda i: (received[i // 2], (i % 2) * 16), None, recv_3, 32, z_ref, w_ref, s_ref, table, near, far)


def first_other_kernel(
    table, recv_0, recv_1, recv_2, recv_3, state_keep, rho_a, z_ref, w_ref, s_ref, gains, duals, target, near, far
):
    received = (recv_0, recv_1, recv_2, recv_3)
    half_rho = 0.5 * rho_a[...]
    for c in range(8):
        at = c * 8
        state = [
            state_keep[which * 64 + at:which * 64 + at + 8, :]
            + received[which][32:40, c * 128:(c + 1) * 128]
            for which in range(3)
        ]
        gains[at:at + 8, :] = state[0]
        duals[at:at + 8, :] = state[1]
        target[at:at + 8, :] = half_rho * state[2] - 0.5 * state[1]
    other_kernel(table, *received, z_ref, w_ref, s_ref, near, far)


def model(coh_at, vis, pairs, first, z_ref, w_ref, s_ref, table, near, far):
    for j in range(ROWS // BLOCK):
        for side, dest in ((0, near), (1, far)):
            both = jnp.dot(table[...], one_hot(pairs, first, side, j), preferred_element_type=F32)
            dest[j % 2] = both[:128] + both[128:]
        for l in range(BLOCK // 128):
            at = j * BLOCK + l * 128

            def coherency(i):
                ref, row = coh_at(i)
                return ref[row:row + 16, at:at + 128]

            gp = matrix(lambda i: near[j % 2, i * 16:(i + 1) * 16, l * 128:(l + 1) * 128])
            gq = matrix(lambda i: far[j % 2, i * 16:(i + 1) * 16, l * 128:(l + 1) * 128])
            cc = matrix(coherency)
            z = product_nh(cc, gq)
            w = product(gp, cc)
            m = product(gp, z)
            for i in range(8):
                z_ref[i * 16:(i + 1) * 16, at:at + 128] = z[i // 4][i % 4]
                w_ref[i * 16:(i + 1) * 16, at:at + 128] = w[i // 4][i % 4]
                total = -jnp.sum(m[i // 4][i % 4], axis=0, keepdims=True)
                if vis is not None:
                    total = total + vis[i:i + 1, at:at + 128]
                s_ref[i:i + 1, at:at + 128] = total


def message_sums_kernel(
    z_ref, w_ref, s_here, s_there, pairs, before, moment, moment_z, out, part_0, part_1, part_2, part_3, left, acc, hot
):
    chan = lax.axis_index("chan")
    near = weigh(basis_at(chan))
    far = weigh(basis_at(chan ^ 4))
    own = comps(moment)
    other = comps(moment_z)
    for d, part in enumerate((part_0, part_1, part_2, part_3)):
        at = basis_at(chan ^ d)
        near_weight = dot_terms(at, near)
        far_weight = dot_terms(at, far)
        put(part, [near_weight * own[c] + far_weight * other[c] for c in range(8)])
    sums_own_kernel(z_ref, w_ref, s_here, s_there, pairs, before, out, left, acc, hot)


def half_sums(z_ref, w_ref, s_here, s_there, pairs, first, before, left, acc, hot):
    steps = ROWS // BLOCK
    for j in range(steps):
        for l in range(BLOCK // 128):
            src = j * BLOCK + l * 128
            r = matrix(lambda i: s_here[i:i + 1, src:src + 128] + s_there[i:i + 1, src:src + 128])
            z = matrix(lambda i: z_ref[i * 16:(i + 1) * 16, src:src + 128])
            w = matrix(lambda i: w_ref[i * 16:(i + 1) * 16, src:src + 128])
            for side, (num, den) in enumerate(
                ((product_nh(r, z), square_nh(z)), (product_hn(r, w), square_hn(w)))
            ):
                at = side * BLOCK + l * 128
                for i, value in enumerate(num[0] + num[1] + den):
                    high, rest = split_parts(value)
                    left[j, i * 16:(i + 1) * 16, at:at + 128] = high
                    left[j, 192 + i * 16:192 + (i + 1) * 16, at:at + 128] = rest
        for side in range(2):
            hot[j, :, side * BLOCK:(side + 1) * BLOCK] = one_hot(pairs, first, side, j)
        total = lax.dot_general(left[j], hot[j], (((1,), (1,)), ((), ())), preferred_element_type=F32)
        if j == 0:
            acc[...] = total if before is None else before[...] + total
        else:
            acc[...] += total


def sums_other_kernel(z_ref, w_ref, s_here, s_there, recv_3, acc, left, hot):
    half_sums(z_ref, w_ref, s_here, s_there, recv_3, 32, None, left, acc, hot)


def sums_own_kernel(z_ref, w_ref, s_here, s_there, pairs, before, out, left, acc, hot):
    half_sums(z_ref, w_ref, s_here, s_there, pairs, 0, before, left, acc, hot)
    low = lanes() < 64
    for c in range(12):
        for t in range(4):
            cols = slice(t * 128, (t + 1) * 128)
            at = c * 16
            v0 = acc[at:at + 8, cols] + acc[192 + at:192 + at + 8, cols]
            v1 = acc[at + 8:at + 16, cols] + acc[192 + at + 8:192 + at + 16, cols]
            out[(2 * t) * 96 + c * 8:(2 * t) * 96 + c * 8 + 8, :] = jnp.where(low, v0, pltpu.roll(v1, 64, 1))
            out[(2 * t + 1) * 96 + c * 8:(2 * t + 1) * 96 + c * 8 + 8, :] = jnp.where(low, pltpu.roll(v0, 64, 1), v1)


def updated(received, gains, target, rho):
    sums = []
    for c in range(12):
        parts = [received[d * 96 + c * 8:d * 96 + c * 8 + 8, :] for d in range(8)]
        while len(parts) > 1:
            parts = [parts[i] + parts[i + 1] for i in range(0, len(parts), 2)]
        sums.append(parts[0])
    half_rho = 0.5 * rho
    a, d, br, bi = sums[8] + half_rho, sums[9] + half_rho, sums[10], sums[11]
    scale = 0.5 / (a * d - br * br - bi * bi)
    n = [sums[i] + target[i] - half_rho * gains[i] for i in range(8)]
    result = [None] * 8
    for i in (0, 1):
        r0, r1, i0, i1 = n[2 * i], n[2 * i + 1], n[4 + 2 * i], n[5 + 2 * i]
        result[2 * i] = gains[2 * i] + scale * (r0 * d - (r1 * br + i1 * bi))
        result[4 + 2 * i] = gains[4 + 2 * i] + scale * (i0 * d - (i1 * br - r1 * bi))
        result[2 * i + 1] = gains[2 * i + 1] + scale * (r1 * a - (r0 * br - i0 * bi))
        result[5 + 2 * i] = gains[5 + 2 * i] + scale * (i1 * a - (i0 * br + r0 * bi))
    return result


def comps(ref):
    return [ref[c * 8:(c + 1) * 8, :] for c in range(8)]


def put(ref, values, base=0):
    for c in range(8):
        ref[base + c * 8:base + (c + 1) * 8, :] = values[c]


def update_kernel(received, gains, target, rho_a, gains_new, spread):
    new = updated(received, comps(gains), comps(target), rho_a[...])
    put(gains_new, new)
    for d in range(8):
        put(spread, new, d * 64)


def update_moment_kernel(received, gains, target, duals, rho_a, gains_new, spread, moment):
    rho = rho_a[...]
    new = updated(received, comps(gains), comps(target), rho)
    put(gains_new, new)
    for d in range(8):
        put(spread, new, d * 64)
    old = comps(duals)
    put(moment, [old[c] + rho * new[c] for c in range(8)])


def update_consensus_kernel(
    received, gains, part_0, part_1, part_2, part_3, duals, rho_a, gains_new, spread, duals_new, target
):
    rho = rho_a[...]
    old_gains = comps(gains)
    old_duals = comps(duals)
    parts = [comps(part) for part in (part_0, part_1, part_2, part_3)]
    fitted = [(parts[0][c] + parts[1][c]) + (parts[2][c] + parts[3][c]) for c in range(8)]
    new_duals = [old_duals[c] + rho * (old_gains[c] - fitted[c]) for c in range(8)]
    aim = [0.5 * (rho * fitted[c] - new_duals[c]) for c in range(8)]
    put(duals_new, new_duals)
    put(target, aim)
    new = updated(received, old_gains, aim, rho)
    put(gains_new, new)
    for d in range(8):
        put(spread, new, d * 64)


def update_last_kernel(received, gains, target, duals, rho_a, keep, send, moment):
    core = lax.axis_index("core")
    rho = rho_a[...]
    new = updated(received, comps(gains), comps(target), rho)
    old = comps(duals)
    lane = lanes()
    quarter = lane // 32
    whole = [old[c] + rho * new[c] for c in range(8)]
    for half in range(2):
        for c in range(4):
            total = jnp.zeros((8, 128), F32)
            for im in range(2):
                for h in range(2):
                    here = jnp.where(quarter == 2 * h + half, whole[im * 4 + c], 0.0)
                    shift = (im * 64 - 32 * h - 32 * half) % 128
                    total = total + (pltpu.roll(here, shift, 1) if shift else here)
            for f in range(CHANNELS):
                at = (2 * f + half) * 32 + c * 8
                moment[at:at + 8, :] = total
    for out, stations in ((keep, core), (send, 1 - core)):
        for base, values in ((0, new), (64, old)):
            for c in range(8):
                total = jnp.zeros((8, 128), F32)
                for h in range(2):
                    here = jnp.where(quarter == 2 * h + stations, values[c], 0.0)
                    total = total + pltpu.roll(here, (64 * core + 96 * stations + 96 * h) % 128, 1)
                out[base + c * 8:base + (c + 1) * 8, :] = total


def finish_kernel(
    moments_hbm, keep, recv, rho_f, gains_hbm, duals_hbm, poly_hbm,
    moments, gains, duals, poly, thin, deep, sems,
):
    load = pltpu.make_async_copy(moments_hbm, moments, sems.at[0])
    load.start()
    chan = lax.axis_index("chan")
    rho = rho_f[...]
    low = lanes() < 64

    def place(ref, value, first, stride):
        for q in range(4):
            part = pltpu.roll(value, 128 - 32 * q, 1) if q else value
            ref[pl.ds(q * 8 * stride + first, 8, stride=stride), :] = part

    now = [keep[c * 8:(c + 1) * 8, :] + recv[c * 8:(c + 1) * 8, :] for c in range(16)]
    for c in range(8):
        place(thin, now[c], c, 8)
    gains[...] = thin[:, 0:32].reshape(32, 8, 32)
    stores = [pltpu.make_async_copy(gains, gains_hbm, sems.at[1])]
    stores[0].start()
    load.wait()
    at = basis_at(chan)
    fitted = [None] * 8
    for t in range(TERMS):
        halves = []
        for half in range(2):
            for c in range(4):
                total = None
                for f in range(CHANNELS):
                    row = f * 64 + half * 32 + c * 8
                    part = float(SOLVE[t, f]) * moments[row:row + 8, :]
                    total = part if total is None else total + part
                halves.append(total)
        real = [jnp.where(low, halves[c], pltpu.roll(halves[4 + c], 64, 1)) for c in range(4)]
        imag = [jnp.where(low, pltpu.roll(halves[c], 64, 1), halves[4 + c]) for c in range(4)]
        for c, value in enumerate(real + imag):
            place(deep, value, c * 4 + t, 32)
            fitted[c] = value if t == 0 else fitted[c] + at[t] * value
    poly[...] = deep[:, 0:32].reshape(32, 8, 4, 32)
    stores.append(pltpu.make_async_copy(poly, poly_hbm, sems.at[2]))
    stores[1].start()
    for c in range(8):
        place(thin, now[8 + c] + rho * (now[c] - fitted[c]), c, 8)
    duals[...] = thin[:, 0:32].reshape(32, 8, 32)
    stores.append(pltpu.make_async_copy(duals, duals_hbm, sems.at[3]))
    stores[2].start()
    for store in stores:
        store.wait()


def local(coherency, visibilities, station_pairs, gains, duals, poly, penalty):
    def swap(x):
        return lax.ppermute(x, "core", CORE_SWAP)

    def exchange(x, axis):
        return lax.all_to_all(x, axis, 0, 0, tiled=True)

    packed = ((64, 128), F32)
    wide = ((512, 128), F32)
    small = ((8, 128), F32)
    state_in = pltpu.VMEM((32, 8, 32), F32)
    thin = pltpu.VMEM((256, 128), F32)
    spread, mark = call(
        spread_kernel, [wide, small], [thin], n_in=1
    )(gains[0])
    gathered = exchange(spread, ("st", "core"))
    coh_keep, state_keep, rho_a, rho_f, *send = call(
        prepare_kernel,
        [((128, ROWS), F32), ((192, 128), F32), small, small] + [((40, ROWS), F32)] * 4,
        [
            pltpu.VMEM((32, 8, ROWS), BF16), state_in, state_in, pltpu.VMEM((32, 8, TERMS, 32), F32),
            pltpu.VMEM((ROWS // 128, 256, 128), F32), thin, pltpu.SemaphoreType.DMA((4,)),
        ],
        hbm=(0, 1, 2, 3, 4), n_in=7,
    )(mark, coherency[0], gains[0], duals[0], poly, station_pairs, jnp.pad(penalty, (0, 96)).reshape(1, 128))
    received = [swap(x) for x in send]
    vis = visibilities[0]

    half_outs = [((128, ROWS), F32), ((128, ROWS), F32), ((8, ROWS), F32)]
    table_out = ((256, STATIONS), BF16)
    pair_scratch = [pltpu.VMEM((2, 128, BLOCK), F32)] * 2
    sums_out = ((768, 128), F32)
    blocks = ROWS // BLOCK
    left = pltpu.VMEM((blocks, 384, 2 * BLOCK), BF16)
    hot = pltpu.VMEM((blocks, STATIONS, 2 * BLOCK), BF16)
    total = pltpu.VMEM((384, STATIONS), F32)

    *own, table = call(first_own_kernel, half_outs + [table_out], pair_scratch, n_in=4)(
        gathered, coh_keep, vis, station_pairs
    )
    *other, gain, dual, target = call(
        first_other_kernel, half_outs + [packed, packed, packed], pair_scratch, n_in=7
    )(table, *received, state_keep, rho_a)

    def step_model(spread, *after):
        kernel = own_after_kernel if after else own_kernel
        *own, table = call(kernel, half_outs + [table_out], pair_scratch, hbm=(4,), n_in=4 + len(after))(
            exchange(spread, "st"), coh_keep, vis, station_pairs, *after
        )
        other = call(other_kernel, half_outs, pair_scratch, n_in=5)(table, *received)
        return own, other

    def step_sums(own, other, kernel=sums_own_kernel, outs=(), extra=()):
        from_own = swap(own[2])
        from_other = swap(other[2])
        (before,) = call(sums_other_kernel, [((384, STATIONS), F32)], [left, hot], n_in=5)(
            *other, from_own, received[3]
        )
        return call(kernel, [sums_out, *outs], [left, total, hot], n_in=6 + len(extra))(
            *own, from_other, station_pairs, before, *extra
        )

    def step(own, other):
        return exchange(step_sums(own, other)[0], "st")

    gain, spread = call(update_kernel, [packed, wide], n_in=4)(step(own, other), gain, target, rho_a)
    gain, spread, moment = call(update_moment_kernel, [packed, wide, packed], n_in=5)(
        step(*step_model(spread)), gain, target, dual, rho_a
    )

    def from_channel(x, distance):
        return lax.ppermute(x, "chan", [(f, f ^ distance) for f in range(CHANNELS)])

    moment_z = from_channel(moment, 4)
    parts, *messages = step_sums(
        *step_model(spread, moment_z), message_sums_kernel, [packed] * 4, (moment, moment_z)
    )
    shares = [messages[0]] + [from_channel(messages[d], d) for d in (1, 2, 3)]
    gain, spread, dual, target = call(update_consensus_kernel, [packed, wide, packed, packed], n_in=8)(
        exchange(parts, "st"), gain, *shares, dual, rho_a
    )
    keep, send, moment = call(update_last_kernel, [((128, 128), F32), ((1024, 128), F32), wide], n_in=5)(
        step(*step_model(spread)), gain, target, dual, rho_a
    )
    moments = exchange(moment, ("chan", "core"))
    gains_out, duals_out, poly_out = call(
        finish_kernel,
        [((32, 8, 32), F32), ((32, 8, 32), F32), ((32, 8, 4, 32), F32)],
        [
            pltpu.VMEM((512, 128), F32), state_in, state_in, pltpu.VMEM((32, 8, TERMS, 32), F32),
            thin, pltpu.VMEM((1024, 128), F32), pltpu.SemaphoreType.DMA((4,)),
        ],
        hbm=(0,), hbm_out=(0, 1, 2), n_in=4,
    )(moments, keep, swap(send), rho_f)
    return gains_out[None], duals_out[None], poly_out


def solution(mesh):
    chan, bl = mesh.devices.shape
    finer = Mesh(mesh.devices.reshape(chan, bl // 2, 2), ("chan", "st", "core"))
    both = ("st", "core")
    in_specs = (
        P("chan", None, None, both),
        P("chan", None, both),
        P(None, both),
        P("chan", None, None, both),
        P("chan", None, None, both),
        P(None, None, None, both),
        P(),
    )
    out_specs = (
        P("chan", None, None, both),
        P("chan", None, None, both),
        P(None, None, None, both),
    )
    return jax.shard_map(local, mesh=finer, in_specs=in_specs, out_specs=out_specs, check_vma=False)
```

```python
import jax
import jax.numpy as jnp
import numpy as np
from jax import lax
from jax.experimental import pallas as pl
from jax.experimental.pallas import tpu as pltpu
from jax.sharding import Mesh, PartitionSpec as P


CHANNELS = 8
TERMS = 4
ROWS = 1024
BLOCK = 256
STATIONS = 512
F32 = jnp.float32
BF16 = jnp.bfloat16
CORE_SWAP = [(0, 1), (1, 0)]
VMEM_BYTES = 24 * 1024 * 1024


def basis_of(place):
    square = place * place
    return [1.0 + 0.0 * place, place, 1.5 * square - 0.5, (2.5 * square - 1.5) * place]


def consensus_tables():
    basis = np.stack(basis_of((2.0 * np.arange(CHANNELS) + 1.0) / CHANNELS - 1.0), axis=1)
    inverse = np.linalg.inv(basis.T @ basis)
    return inverse, inverse @ basis.T


GRAM_INVERSE, SOLVE = consensus_tables()


def basis_at(channel):
    place = (2.0 * jnp.full((8, 128), channel, jnp.int32).astype(F32) + 1.0) / CHANNELS - 1.0
    return basis_of(place)


def dot_terms(a, b):
    total = a[0] * b[0]
    for t in range(1, TERMS):
        total = total + a[t] * b[t]
    return total


def weigh(values):
    return [
        sum(float(GRAM_INVERSE[t, u]) * values[u] for u in range(t % 2, TERMS, 2)) for t in range(TERMS)
    ]


def call(kernel, out_shapes, scratch=(), hbm=(), hbm_out=(), n_in=0):
    def specs(count, outside):
        return [pl.BlockSpec(memory_space=pl.ANY if i in outside else pltpu.VMEM) for i in range(count)]

    return pl.pallas_call(
        kernel,
        out_shape=[jax.ShapeDtypeStruct(s, d) for s, d in out_shapes],
        in_specs=specs(n_in, hbm),
        out_specs=specs(len(out_shapes), hbm_out),
        scratch_shapes=list(scratch),
        compiler_params=pltpu.CompilerParams(vmem_limit_bytes=VMEM_BYTES),
        cost_estimate=pl.CostEstimate(flops=0, bytes_accessed=1000, transcendentals=0),
    )


def lanes():
    return lax.broadcasted_iota(jnp.int32, (8, 128), 1)


def split_parts(x):
    high = x.astype(BF16)
    return high, (x - high.astype(F32)).astype(BF16)


def matrix(load):
    return [load(i) for i in range(4)], [load(4 + i) for i in range(4)]


def conj_t(m):
    re, im = m
    return [re[0], re[2], re[1], re[3]], [-im[0], -im[2], -im[1], -im[3]]


def product_nh(a, b):
    (ar, ai), (br, bi) = a, b
    re, im = [], []
    for i in (0, 1):
        for j in (0, 1):
            p, q, u, v = 2 * i, 2 * i + 1, 2 * j, 2 * j + 1
            re.append((ar[p] * br[u] + ai[p] * bi[u]) + (ar[q] * br[v] + ai[q] * bi[v]))
            im.append((ai[p] * br[u] - ar[p] * bi[u]) + (ai[q] * br[v] - ar[q] * bi[v]))
    return re, im


def product_hn(a, b):
    (ar, ai), (br, bi) = a, b
    re, im = [], []
    for i in (0, 1):
        for j in (0, 1):
            p, q, u, v = i, 2 + i, j, 2 + j
            re.append((ar[p] * br[u] + ai[p] * bi[u]) + (ar[q] * br[v] + ai[q] * bi[v]))
            im.append((ar[p] * bi[u] - ai[p] * br[u]) + (ar[q] * bi[v] - ai[q] * br[v]))
    return re, im


def product(a, b):
    (ar, ai), (br, bi) = a, b
    re, im = [], []
    for i in (0, 1):
        for j in (0, 1):
            p, q, u, v = 2 * i, 2 * i + 1, j, 2 + j
            re.append((ar[p] * br[u] - ai[p] * bi[u]) + (ar[q] * br[v] - ai[q] * bi[v]))
            im.append((ar[p] * bi[u] + ai[p] * br[u]) + (ar[q] * bi[v] + ai[q] * br[v]))
    return re, im


def square_nh(a):
    r, i = a
    return [
        (r[0] * r[0] + i[0] * i[0]) + (r[1] * r[1] + i[1] * i[1]),
        (r[2] * r[2] + i[2] * i[2]) + (r[3] * r[3] + i[3] * i[3]),
        (r[0] * r[2] + i[0] * i[2]) + (r[1] * r[3] + i[1] * i[3]),
        (i[0] * r[2] - r[0] * i[2]) + (i[1] * r[3] - r[1] * i[3]),
    ]


def square_hn(a):
    r, i = a
    return [
        (r[0] * r[0] + i[0] * i[0]) + (r[2] * r[2] + i[2] * i[2]),
        (r[1] * r[1] + i[1] * i[1]) + (r[3] * r[3] + i[3] * i[3]),
        (r[0] * r[1] + i[0] * i[1]) + (r[2] * r[3] + i[2] * i[3]),
        (r[0] * i[1] - i[0] * r[1]) + (r[2] * i[3] - i[2] * r[3]),
    ]


def spread_kernel(gains, spread, mark, thin):
    thin[...] = jnp.zeros((256, 128), F32)
    mark[...] = jnp.zeros((8, 128), F32)
    thin[:, 0:32] = gains[...].reshape(256, 32)
    for half in range(2):
        for c in range(4):
            total = None
            for im in range(2):
                for h in range(2):
                    part = thin[pl.ds((half * 16 + h * 8) * 8 + im * 4 + c, 8, stride=8), :]
                    if im or h:
                        part = pltpu.roll(part, im * 64 + h * 32, 1)
                    total = part if total is None else total + part
            for d in range(8):
                at = (2 * d + half) * 32 + c * 8
                spread[at:at + 8, :] = total


def prepare_kernel(
    mark, coh_hbm, gains_hbm, duals_hbm, poly_hbm, pairs, penalty,
    coh_keep, state_keep, rho_a, rho_f, send_0, send_1, send_2, send_3,
    coh, gains, duals, poly, wide, thin, sems,
):
    send = (send_0, send_1, send_2, send_3)
    copies = [
        pltpu.make_async_copy(src, dst, sems.at[i])
        for i, (src, dst) in enumerate(((gains_hbm, gains), (duals_hbm, duals), (poly_hbm, poly), (coh_hbm, coh)))
    ]
    for copy in copies:
        copy.start()
    core = lax.axis_index("core")
    chan = lax.axis_index("chan")
    row = lax.broadcasted_iota(jnp.int32, (8, 128), 0)
    lane = lanes()
    given = jnp.broadcast_to(penalty[...], (8, 128))
    column = [jnp.sum(jnp.where(lane == q * 8 + row, given, 0.0), axis=1, keepdims=True) for q in range(4)]
    by_dir = jnp.broadcast_to(column[0], (8, 128))
    for q in range(1, 4):
        by_dir = jnp.where(lane // 32 == q, column[q], by_dir)
    mine = jnp.full((8, 128), core, jnp.int32) == 0
    low = jnp.where(mine, column[0], column[2])
    high = jnp.where(mine, column[1], column[3])
    rho_a[...] = jnp.where(lane < 64, low, high)
    rho_f[...] = by_dir
    send_3[32:40, :] = jnp.zeros((8, ROWS), F32)
    send_3[32:34, :] = pairs[...].astype(F32)

    def pack(which):
        for c in range(8):
            for keep, half in ((True, core), (False, 1 - core)):
                total = None
                for h in range(2):
                    part = thin[pl.ds((half * 16 + h * 8) * 8 + c, 8, stride=8), :]
                    part = pltpu.roll(part, h * 64 + core * 32, 1)
                    total = part if total is None else total + part
                if keep:
                    state_keep[which * 64 + c * 8:which * 64 + (c + 1) * 8, :] = total
                else:
                    send[which][32:40, c * 128:(c + 1) * 128] = total

    thin[...] = jnp.zeros((256, 128), F32)
    copies[0].wait()
    thin[:, 0:32] = gains[...].reshape(256, 32)
    pack(0)
    copies[1].wait()
    thin[:, 0:32] = duals[...].reshape(256, 32)
    pack(1)
    copies[2].wait()
    place = (2.0 * chan.astype(F32) + 1.0) * (1.0 / CHANNELS) - 1.0
    basis = basis_of(place)
    fitted = poly[:, :, 0, :]
    for t in range(1, TERMS):
        fitted = fitted + poly[:, :, t, :] * basis[t]
    thin[:, 0:32] = fitted.reshape(256, 32)
    pack(2)
    copies[3].wait()
    for t in range(ROWS // 128):
        cols = slice(t * 128, (t + 1) * 128)
        wide[t] = coh[:, :, cols].astype(F32).reshape(256, 128)
        for c in range(8):
            coh_keep[c * 16:(c + 1) * 16, cols] = wide[t, pl.ds(core * 128 + c, 16, stride=8), :]
            send[c // 2][(c % 2) * 16:(c % 2) * 16 + 16, cols] = wide[t, pl.ds((1 - core) * 128 + c, 16, stride=8), :]


def one_hot(pairs, first, side, j):
    index = pairs[first + side:first + side + 1, j * BLOCK:(j + 1) * BLOCK].astype(jnp.int32)
    index = jnp.broadcast_to(index, (16, BLOCK)).astype(jnp.int16)
    index = jnp.concatenate([index] * (STATIONS // 16), axis=0)
    here = lax.broadcasted_iota(jnp.int16, (STATIONS, BLOCK), 0) == index
    return jnp.where(here, jnp.ones((STATIONS, BLOCK), BF16), jnp.zeros((STATIONS, BLOCK), BF16))


def put_table(table, c, t, first, second):
    high, rest = split_parts(jnp.concatenate([first, second], axis=0))
    table[c * 16:(c + 1) * 16, t * 128:(t + 1) * 128] = high
    table[128 + c * 16:128 + (c + 1) * 16, t * 128:(t + 1) * 128] = rest


def start_table(gathered, table):
    lane = lanes()
    for c in range(8):
        im, row = divmod(c, 4)
        for t in range(4):
            halves = []
            for h in range(2):
                total = None
                for b in range(4):
                    part = gathered[(4 * t + b) * 32 + row * 8:(4 * t + b) * 32 + row * 8 + 8, :]
                    shift = (b * 32 - im * 64 - h * 32) % 128
                    if shift:
                        part = pltpu.roll(part, shift, 1)
                    total = part if total is None else jnp.where(lane // 32 == b, part, total)
                halves.append(total)
            put_table(table, c, t, *halves)


def step_table(gathered, table):
    low = lanes() < 64
    for c in range(8):
        for t in range(4):
            a = gathered[(2 * t) * 64 + c * 8:(2 * t) * 64 + c * 8 + 8, :]
            b = gathered[(2 * t + 1) * 64 + c * 8:(2 * t + 1) * 64 + c * 8 + 8, :]
            first = jnp.where(low, a, pltpu.roll(b, 64, 1))
            second = jnp.where(low, pltpu.roll(a, 64, 1), b)
            put_table(table, c, t, first, second)


def first_own_kernel(gathered, coh, vis, pairs, z_ref, w_ref, s_ref, table, near, far):
    start_table(gathered, table)
    model(lambda i: (coh, i * 16), vis, pairs, 0, z_ref, w_ref, s_ref, table, near, far)


def own_kernel(gathered, coh, vis, pairs, z_ref, w_ref, s_ref, table, near, far):
    step_table(gathered, table)
    model(lambda i: (coh, i * 16), vis, pairs, 0, z_ref, w_ref, s_ref, table, near, far)


def other_kernel(table, recv_0, recv_1, recv_2, recv_3, z_ref, w_ref, s_ref, near, far):
    received = (recv_0, recv_1, recv_2, recv_3)
    model(lambda i: (received[i // 2], (i % 2) * 16), None, recv_3, 32, z_ref, w_ref, s_ref, table, near, far)


def other_after_kernel(table, recv_0, recv_1, recv_2, recv_3, after, *rest):
    other_kernel(table, recv_0, recv_1, recv_2, recv_3, *rest)


def first_other_kernel(
    table, recv_0, recv_1, recv_2, recv_3, state_keep, rho_a, z_ref, w_ref, s_ref, gains, duals, target, near, far
):
    received = (recv_0, recv_1, recv_2, recv_3)
    half_rho = 0.5 * rho_a[...]
    for c in range(8):
        at = c * 8
        state = [
            state_keep[which * 64 + at:which * 64 + at + 8, :]
            + received[which][32:40, c * 128:(c + 1) * 128]
            for which in range(3)
        ]
        gains[at:at + 8, :] = state[0]
        duals[at:at + 8, :] = state[1]
        target[at:at + 8, :] = half_rho * state[2] - 0.5 * state[1]
    other_kernel(table, *received, z_ref, w_ref, s_ref, near, far)


def model(coh_at, vis, pairs, first, z_ref, w_ref, s_ref, table, near, far):
    for j in range(ROWS // BLOCK):
        for side, dest in ((0, near), (1, far)):
            both = jnp.dot(table[...], one_hot(pairs, first, side, j), preferred_element_type=F32)
            dest[j % 2] = both[:128] + both[128:]
        for l in range(BLOCK // 128):
            at = j * BLOCK + l * 128

            def coherency(i):
                ref, row = coh_at(i)
                return ref[row:row + 16, at:at + 128]

            gp = matrix(lambda i: near[j % 2, i * 16:(i + 1) * 16, l * 128:(l + 1) * 128])
            gq = matrix(lambda i: far[j % 2, i * 16:(i + 1) * 16, l * 128:(l + 1) * 128])
            cc = matrix(coherency)
            z = product_nh(cc, gq)
            w = product(gp, cc)
            m = product(gp, z)
            for i in range(8):
                z_ref[i * 16:(i + 1) * 16, at:at + 128] = z[i // 4][i % 4]
                w_ref[i * 16:(i + 1) * 16, at:at + 128] = w[i // 4][i % 4]
                total = -jnp.sum(m[i // 4][i % 4], axis=0, keepdims=True)
                if vis is not None:
                    total = total + vis[i:i + 1, at:at + 128]
                s_ref[i:i + 1, at:at + 128] = total


def message_sums_kernel(
    z_ref, w_ref, s_here, s_there, pairs, before, moment, moment_z, out, part_0, part_1, part_2, part_3, left, acc, hot
):
    chan = lax.axis_index("chan")
    near = weigh(basis_at(chan))
    far = weigh(basis_at(chan ^ 4))
    own = comps(moment)
    other = comps(moment_z)
    for d, part in enumerate((part_0, part_1, part_2, part_3)):
        at = basis_at(chan ^ d)
        near_weight = dot_terms(at, near)
        far_weight = dot_terms(at, far)
        put(part, [near_weight * own[c] + far_weight * other[c] for c in range(8)])
    sums_own_kernel(z_ref, w_ref, s_here, s_there, pairs, before, out, left, acc, hot)


def half_sums(z_ref, w_ref, s_here, s_there, pairs, first, before, left, acc, hot):
    steps = ROWS // BLOCK
    for j in range(steps):
        for l in range(BLOCK // 128):
            src = j * BLOCK + l * 128
            r = matrix(lambda i: s_here[i:i + 1, src:src + 128] + s_there[i:i + 1, src:src + 128])
            z = matrix(lambda i: z_ref[i * 16:(i + 1) * 16, src:src + 128])
            w = matrix(lambda i: w_ref[i * 16:(i + 1) * 16, src:src + 128])
            for side, (num, den) in enumerate(
                ((product_nh(r, z), square_nh(z)), (product_hn(r, w), square_hn(w)))
            ):
                at = side * BLOCK + l * 128
                for i, value in enumerate(num[0] + num[1] + den):
                    high, rest = split_parts(value)
                    left[j, i * 16:(i + 1) * 16, at:at + 128] = high
                    left[j, 192 + i * 16:192 + (i + 1) * 16, at:at + 128] = rest
        for side in range(2):
            hot[j, :, side * BLOCK:(side + 1) * BLOCK] = one_hot(pairs, first, side, j)
        total = lax.dot_general(left[j], hot[j], (((1,), (1,)), ((), ())), preferred_element_type=F32)
        if j == 0:
            acc[...] = total if before is None else before[...] + total
        else:
            acc[...] += total


def sums_other_kernel(z_ref, w_ref, s_here, s_there, recv_3, acc, left, hot):
    half_sums(z_ref, w_ref, s_here, s_there, recv_3, 32, None, left, acc, hot)


def sums_own_kernel(z_ref, w_ref, s_here, s_there, pairs, before, out, left, acc, hot):
    half_sums(z_ref, w_ref, s_here, s_there, pairs, 0, before, left, acc, hot)
    low = lanes() < 64
    for c in range(12):
        for t in range(4):
            cols = slice(t * 128, (t + 1) * 128)
            at = c * 16
            v0 = acc[at:at + 8, cols] + acc[192 + at:192 + at + 8, cols]
            v1 = acc[at + 8:at + 16, cols] + acc[192 + at + 8:192 + at + 16, cols]
            out[(2 * t) * 96 + c * 8:(2 * t) * 96 + c * 8 + 8, :] = jnp.where(low, v0, pltpu.roll(v1, 64, 1))
            out[(2 * t + 1) * 96 + c * 8:(2 * t + 1) * 96 + c * 8 + 8, :] = jnp.where(low, pltpu.roll(v0, 64, 1), v1)


def updated(received, gains, target, rho):
    sums = []
    for c in range(12):
        parts = [received[d * 96 + c * 8:d * 96 + c * 8 + 8, :] for d in range(8)]
        while len(parts) > 1:
            parts = [parts[i] + parts[i + 1] for i in range(0, len(parts), 2)]
        sums.append(parts[0])
    half_rho = 0.5 * rho
    a, d, br, bi = sums[8] + half_rho, sums[9] + half_rho, sums[10], sums[11]
    scale = 0.5 / (a * d - br * br - bi * bi)
    n = [sums[i] + target[i] - half_rho * gains[i] for i in range(8)]
    result = [None] * 8
    for i in (0, 1):
        r0, r1, i0, i1 = n[2 * i], n[2 * i + 1], n[4 + 2 * i], n[5 + 2 * i]
        result[2 * i] = gains[2 * i] + scale * (r0 * d - (r1 * br + i1 * bi))
        result[4 + 2 * i] = gains[4 + 2 * i] + scale * (i0 * d - (i1 * br - r1 * bi))
        result[2 * i + 1] = gains[2 * i + 1] + scale * (r1 * a - (r0 * br - i0 * bi))
        result[5 + 2 * i] = gains[5 + 2 * i] + scale * (i1 * a - (i0 * br + r0 * bi))
    return result


def comps(ref):
    return [ref[c * 8:(c + 1) * 8, :] for c in range(8)]


def put(ref, values, base=0):
    for c in range(8):
        ref[base + c * 8:base + (c + 1) * 8, :] = values[c]


def update_kernel(received, gains, target, rho_a, gains_new, spread):
    new = updated(received, comps(gains), comps(target), rho_a[...])
    put(gains_new, new)
    for d in range(8):
        put(spread, new, d * 64)


def update_moment_kernel(received, gains, target, duals, rho_a, gains_new, spread, moment):
    rho = rho_a[...]
    new = updated(received, comps(gains), comps(target), rho)
    put(gains_new, new)
    for d in range(8):
        put(spread, new, d * 64)
    old = comps(duals)
    put(moment, [old[c] + rho * new[c] for c in range(8)])


def update_consensus_kernel(
    received, gains, part_0, part_1, part_2, part_3, duals, rho_a, gains_new, spread, duals_new, target
):
    rho = rho_a[...]
    old_gains = comps(gains)
    old_duals = comps(duals)
    parts = [comps(part) for part in (part_0, part_1, part_2, part_3)]
    fitted = [(parts[0][c] + parts[1][c]) + (parts[2][c] + parts[3][c]) for c in range(8)]
    new_duals = [old_duals[c] + rho * (old_gains[c] - fitted[c]) for c in range(8)]
    aim = [0.5 * (rho * fitted[c] - new_duals[c]) for c in range(8)]
    put(duals_new, new_duals)
    put(target, aim)
    new = updated(received, old_gains, aim, rho)
    put(gains_new, new)
    for d in range(8):
        put(spread, new, d * 64)


def update_last_kernel(received, gains, target, duals, rho_a, keep, send, moment):
    core = lax.axis_index("core")
    rho = rho_a[...]
    new = updated(received, comps(gains), comps(target), rho)
    old = comps(duals)
    lane = lanes()
    quarter = lane // 32
    whole = [old[c] + rho * new[c] for c in range(8)]
    for half in range(2):
        for c in range(4):
            total = jnp.zeros((8, 128), F32)
            for im in range(2):
                for h in range(2):
                    here = jnp.where(quarter == 2 * h + half, whole[im * 4 + c], 0.0)
                    shift = (im * 64 - 32 * h - 32 * half) % 128
                    total = total + (pltpu.roll(here, shift, 1) if shift else here)
            for f in range(CHANNELS):
                at = (2 * f + half) * 32 + c * 8
                moment[at:at + 8, :] = total
    for out, stations in ((keep, core), (send, 1 - core)):
        for base, values in ((0, new), (64, old)):
            for c in range(8):
                total = jnp.zeros((8, 128), F32)
                for h in range(2):
                    here = jnp.where(quarter == 2 * h + stations, values[c], 0.0)
                    total = total + pltpu.roll(here, (64 * core + 96 * stations + 96 * h) % 128, 1)
                out[base + c * 8:base + (c + 1) * 8, :] = total


def finish_kernel(
    moments, keep, recv, rho_f, gains_hbm, duals_hbm, poly_hbm, gains, duals, poly, thin, deep, sems
):
    chan = lax.axis_index("chan")
    rho = rho_f[...]
    low = lanes() < 64

    def place(ref, value, first, stride):
        for q in range(4):
            part = pltpu.roll(value, 128 - 32 * q, 1) if q else value
            ref[pl.ds(q * 8 * stride + first, 8, stride=stride), :] = part

    now = [keep[c * 8:(c + 1) * 8, :] + recv[c * 8:(c + 1) * 8, :] for c in range(16)]
    for c in range(8):
        place(thin, now[c], c, 8)
    gains[...] = thin[:, 0:32].reshape(32, 8, 32)
    stores = [pltpu.make_async_copy(gains, gains_hbm, sems.at[0])]
    stores[0].start()
    at = basis_at(chan)
    fitted = [None] * 8
    for t in range(TERMS):
        halves = []
        for half in range(2):
            for c in range(4):
                total = None
                for f in range(CHANNELS):
                    row = f * 64 + half * 32 + c * 8
                    part = float(SOLVE[t, f]) * moments[row:row + 8, :]
                    total = part if total is None else total + part
                halves.append(total)
        real = [jnp.where(low, halves[c], pltpu.roll(halves[4 + c], 64, 1)) for c in range(4)]
        imag = [jnp.where(low, pltpu.roll(halves[c], 64, 1), halves[4 + c]) for c in range(4)]
        for c, value in enumerate(real + imag):
            place(deep, value, c * 4 + t, 32)
            fitted[c] = value if t == 0 else fitted[c] + at[t] * value
    poly[...] = deep[:, 0:32].reshape(32, 8, 4, 32)
    stores.append(pltpu.make_async_copy(poly, poly_hbm, sems.at[1]))
    stores[1].start()
    for c in range(8):
        place(thin, now[8 + c] + rho * (now[c] - fitted[c]), c, 8)
    duals[...] = thin[:, 0:32].reshape(32, 8, 32)
    stores.append(pltpu.make_async_copy(duals, duals_hbm, sems.at[2]))
    stores[2].start()
    for store in stores:
        store.wait()


def local(coherency, visibilities, station_pairs, gains, duals, poly, penalty):
    def swap(x):
        return lax.ppermute(x, "core", CORE_SWAP)

    def exchange(x, axis):
        return lax.all_to_all(x, axis, 0, 0, tiled=True)

    packed = ((64, 128), F32)
    wide = ((512, 128), F32)
    small = ((8, 128), F32)
    state_in = pltpu.VMEM((32, 8, 32), F32)
    thin = pltpu.VMEM((256, 128), F32)
    spread, mark = call(
        spread_kernel, [wide, small], [thin], n_in=1
    )(gains[0])
    gathered = exchange(spread, ("st", "core"))
    coh_keep, state_keep, rho_a, rho_f, *send = call(
        prepare_kernel,
        [((128, ROWS), F32), ((192, 128), F32), small, small] + [((40, ROWS), F32)] * 4,
        [
            pltpu.VMEM((32, 8, ROWS), BF16), state_in, state_in, pltpu.VMEM((32, 8, TERMS, 32), F32),
            pltpu.VMEM((ROWS // 128, 256, 128), F32), thin, pltpu.SemaphoreType.DMA((4,)),
        ],
        hbm=(0, 1, 2, 3, 4), n_in=7,
    )(mark, coherency[0], gains[0], duals[0], poly, station_pairs, jnp.pad(penalty, (0, 96)).reshape(1, 128))
    received = [swap(x) for x in send]
    vis = visibilities[0]

    half_outs = [((128, ROWS), F32), ((128, ROWS), F32), ((8, ROWS), F32)]
    table_out = ((256, STATIONS), BF16)
    pair_scratch = [pltpu.VMEM((2, 128, BLOCK), F32)] * 2
    sums_out = ((768, 128), F32)
    blocks = ROWS // BLOCK
    left = pltpu.VMEM((blocks, 384, 2 * BLOCK), BF16)
    hot = pltpu.VMEM((blocks, STATIONS, 2 * BLOCK), BF16)
    total = pltpu.VMEM((384, STATIONS), F32)

    *own, table = call(first_own_kernel, half_outs + [table_out], pair_scratch, n_in=4)(
        gathered, coh_keep, vis, station_pairs
    )
    *other, gain, dual, target = call(
        first_other_kernel, half_outs + [packed, packed, packed], pair_scratch, n_in=7
    )(table, *received, state_keep, rho_a)

    def step_model(spread, *after):
        *own, table = call(own_kernel, half_outs + [table_out], pair_scratch, n_in=4)(
            exchange(spread, "st"), coh_keep, vis, station_pairs
        )
        kernel = other_after_kernel if after else other_kernel
        other = call(kernel, half_outs, pair_scratch, hbm=(5,), n_in=5 + len(after))(table, *received, *after)
        return own, other

    def step_sums(own, other, kernel=sums_own_kernel, outs=(), extra=()):
        from_own = swap(own[2])
        from_other = swap(other[2])
        (before,) = call(sums_other_kernel, [((384, STATIONS), F32)], [left, hot], n_in=5)(
            *other, from_own, received[3]
        )
        return call(kernel, [sums_out, *outs], [left, total, hot], n_in=6 + len(extra))(
            *own, from_other, station_pairs, before, *extra
        )

    def step(own, other):
        return exchange(step_sums(own, other)[0], "st")

    gain, spread = call(update_kernel, [packed, wide], n_in=4)(step(own, other), gain, target, rho_a)
    gain, spread, moment = call(update_moment_kernel, [packed, wide, packed], n_in=5)(
        step(*step_model(spread)), gain, target, dual, rho_a
    )

    def from_channel(x, distance):
        return lax.ppermute(x, "chan", [(f, f ^ distance) for f in range(CHANNELS)])

    moment_z = from_channel(moment, 4)
    parts, *messages = step_sums(
        *step_model(spread, moment_z), message_sums_kernel, [packed] * 4, (moment, moment_z)
    )
    shares = [messages[0]] + [from_channel(messages[d], d) for d in (1, 2, 3)]
    gain, spread, dual, target = call(update_consensus_kernel, [packed, wide, packed, packed], n_in=8)(
        exchange(parts, "st"), gain, *shares, dual, rho_a
    )
    keep, send, moment = call(update_last_kernel, [((128, 128), F32), ((1024, 128), F32), wide], n_in=5)(
        step(*step_model(spread)), gain, target, dual, rho_a
    )
    moments = exchange(moment, ("chan", "core"))
    gains_out, duals_out, poly_out = call(
        finish_kernel,
        [((32, 8, 32), F32), ((32, 8, 32), F32), ((32, 8, 4, 32), F32)],
        [
            state_in, state_in, pltpu.VMEM((32, 8, TERMS, 32), F32),
            thin, pltpu.VMEM((1024, 128), F32), pltpu.SemaphoreType.DMA((3,)),
        ],
        hbm_out=(0, 1, 2), n_in=4,
    )(moments, keep, swap(send), rho_f)
    return gains_out[None], duals_out[None], poly_out


def solution(mesh):
    chan, bl = mesh.devices.shape
    finer = Mesh(mesh.devices.reshape(chan, bl // 2, 2), ("chan", "st", "core"))
    both = ("st", "core")
    in_specs = (
        P("chan", None, None, both),
        P("chan", None, both),
        P(None, both),
        P("chan", None, None, both),
        P("chan", None, None, both),
        P(None, None, None, both),
        P(),
    )
    out_specs = (
        P("chan", None, None, both),
        P("chan", None, None, both),
        P(None, None, None, both),
    )
    return jax.shard_map(local, mesh=finer, in_specs=in_specs, out_specs=out_specs, check_vma=False)
```

```python
import jax
import jax.numpy as jnp
import numpy as np
from jax import lax
from jax.experimental import pallas as pl
from jax.experimental.pallas import tpu as pltpu
from jax.sharding import Mesh, PartitionSpec as P


CHANNELS = 8
TERMS = 4
ROWS = 1024
BLOCK = 256
STATIONS = 512
F32 = jnp.float32
BF16 = jnp.bfloat16
CORE_SWAP = [(0, 1), (1, 0)]
VMEM_BYTES = 24 * 1024 * 1024


def basis_of(place):
    square = place * place
    return [1.0 + 0.0 * place, place, 1.5 * square - 0.5, (2.5 * square - 1.5) * place]


def consensus_tables():
    basis = np.stack(basis_of((2.0 * np.arange(CHANNELS) + 1.0) / CHANNELS - 1.0), axis=1)
    inverse = np.linalg.inv(basis.T @ basis)
    return inverse, inverse @ basis.T


GRAM_INVERSE, SOLVE = consensus_tables()


def basis_at(channel):
    place = (2.0 * jnp.full((8, 128), channel, jnp.int32).astype(F32) + 1.0) / CHANNELS - 1.0
    return basis_of(place)


def dot_terms(a, b):
    total = a[0] * b[0]
    for t in range(1, TERMS):
        total = total + a[t] * b[t]
    return total


def weigh(values):
    return [
        sum(float(GRAM_INVERSE[t, u]) * values[u] for u in range(t % 2, TERMS, 2)) for t in range(TERMS)
    ]


def call(kernel, out_shapes, scratch=(), hbm=(), hbm_out=(), n_in=0):
    def specs(count, outside):
        return [pl.BlockSpec(memory_space=pl.ANY if i in outside else pltpu.VMEM) for i in range(count)]

    return pl.pallas_call(
        kernel,
        out_shape=[jax.ShapeDtypeStruct(s, d) for s, d in out_shapes],
        in_specs=specs(n_in, hbm),
        out_specs=specs(len(out_shapes), hbm_out),
        scratch_shapes=list(scratch),
        compiler_params=pltpu.CompilerParams(vmem_limit_bytes=VMEM_BYTES),
        cost_estimate=pl.CostEstimate(flops=0, bytes_accessed=1000, transcendentals=0),
    )


def lanes():
    return lax.broadcasted_iota(jnp.int32, (8, 128), 1)


def split_parts(x):
    high = x.astype(BF16)
    return high, (x - high.astype(F32)).astype(BF16)


def matrix(load):
    return [load(i) for i in range(4)], [load(4 + i) for i in range(4)]


def conj_t(m):
    re, im = m
    return [re[0], re[2], re[1], re[3]], [-im[0], -im[2], -im[1], -im[3]]


def product_nh(a, b):
    (ar, ai), (br, bi) = a, b
    re, im = [], []
    for i in (0, 1):
        for j in (0, 1):
            p, q, u, v = 2 * i, 2 * i + 1, 2 * j, 2 * j + 1
            re.append((ar[p] * br[u] + ai[p] * bi[u]) + (ar[q] * br[v] + ai[q] * bi[v]))
            im.append((ai[p] * br[u] - ar[p] * bi[u]) + (ai[q] * br[v] - ar[q] * bi[v]))
    return re, im


def product_hn(a, b):
    (ar, ai), (br, bi) = a, b
    re, im = [], []
    for i in (0, 1):
        for j in (0, 1):
            p, q, u, v = i, 2 + i, j, 2 + j
            re.append((ar[p] * br[u] + ai[p] * bi[u]) + (ar[q] * br[v] + ai[q] * bi[v]))
            im.append((ar[p] * bi[u] - ai[p] * br[u]) + (ar[q] * bi[v] - ai[q] * br[v]))
    return re, im


def product(a, b):
    (ar, ai), (br, bi) = a, b
    re, im = [], []
    for i in (0, 1):
        for j in (0, 1):
            p, q, u, v = 2 * i, 2 * i + 1, j, 2 + j
            re.append((ar[p] * br[u] - ai[p] * bi[u]) + (ar[q] * br[v] - ai[q] * bi[v]))
            im.append((ar[p] * bi[u] + ai[p] * br[u]) + (ar[q] * bi[v] + ai[q] * br[v]))
    return re, im


def square_nh(a):
    r, i = a
    return [
        (r[0] * r[0] + i[0] * i[0]) + (r[1] * r[1] + i[1] * i[1]),
        (r[2] * r[2] + i[2] * i[2]) + (r[3] * r[3] + i[3] * i[3]),
        (r[0] * r[2] + i[0] * i[2]) + (r[1] * r[3] + i[1] * i[3]),
        (i[0] * r[2] - r[0] * i[2]) + (i[1] * r[3] - r[1] * i[3]),
    ]


def square_hn(a):
    r, i = a
    return [
        (r[0] * r[0] + i[0] * i[0]) + (r[2] * r[2] + i[2] * i[2]),
        (r[1] * r[1] + i[1] * i[1]) + (r[3] * r[3] + i[3] * i[3]),
        (r[0] * r[1] + i[0] * i[1]) + (r[2] * r[3] + i[2] * i[3]),
        (r[0] * i[1] - i[0] * r[1]) + (r[2] * i[3] - i[2] * r[3]),
    ]


def spread_kernel(gains, spread, mark, thin):
    thin[...] = jnp.zeros((256, 128), F32)
    mark[...] = jnp.zeros((8, 128), F32)
    thin[:, 0:32] = gains[...].reshape(256, 32)
    for half in range(2):
        for c in range(4):
            total = None
            for im in range(2):
                for h in range(2):
                    part = thin[pl.ds((half * 16 + h * 8) * 8 + im * 4 + c, 8, stride=8), :]
                    if im or h:
                        part = pltpu.roll(part, im * 64 + h * 32, 1)
                    total = part if total is None else total + part
            for d in range(8):
                at = (2 * d + half) * 32 + c * 8
                spread[at:at + 8, :] = total


def prepare_kernel(
    mark, coh_hbm, gains_hbm, duals_hbm, poly_hbm, pairs, penalty,
    coh_keep, state_keep, rho_a, rho_f, send_0, send_1, send_2, send_3,
    coh, gains, duals, poly, wide, thin, sems,
):
    send = (send_0, send_1, send_2, send_3)
    copies = [
        pltpu.make_async_copy(src, dst, sems.at[i])
        for i, (src, dst) in enumerate(((gains_hbm, gains), (duals_hbm, duals), (poly_hbm, poly), (coh_hbm, coh)))
    ]
    for copy in copies:
        copy.start()
    core = lax.axis_index("core")
    chan = lax.axis_index("chan")
    row = lax.broadcasted_iota(jnp.int32, (8, 128), 0)
    lane = lanes()
    given = jnp.broadcast_to(penalty[...], (8, 128))
    column = [jnp.sum(jnp.where(lane == q * 8 + row, given, 0.0), axis=1, keepdims=True) for q in range(4)]
    by_dir = jnp.broadcast_to(column[0], (8, 128))
    for q in range(1, 4):
        by_dir = jnp.where(lane // 32 == q, column[q], by_dir)
    mine = jnp.full((8, 128), core, jnp.int32) == 0
    low = jnp.where(mine, column[0], column[2])
    high = jnp.where(mine, column[1], column[3])
    rho_a[...] = jnp.where(lane < 64, low, high)
    rho_f[...] = by_dir
    send_3[32:40, :] = jnp.zeros((8, ROWS), F32)
    send_3[32:34, :] = pairs[...].astype(F32)

    def pack(which):
        for c in range(8):
            for keep, half in ((True, core), (False, 1 - core)):
                total = None
                for h in range(2):
                    part = thin[pl.ds((half * 16 + h * 8) * 8 + c, 8, stride=8), :]
                    part = pltpu.roll(part, h * 64 + core * 32, 1)
                    total = part if total is None else total + part
                if keep:
                    state_keep[which * 64 + c * 8:which * 64 + (c + 1) * 8, :] = total
                else:
                    send[which][32:40, c * 128:(c + 1) * 128] = total

    thin[...] = jnp.zeros((256, 128), F32)
    copies[0].wait()
    thin[:, 0:32] = gains[...].reshape(256, 32)
    pack(0)
    copies[1].wait()
    thin[:, 0:32] = duals[...].reshape(256, 32)
    pack(1)
    copies[2].wait()
    place = (2.0 * chan.astype(F32) + 1.0) * (1.0 / CHANNELS) - 1.0
    basis = basis_of(place)
    fitted = poly[:, :, 0, :]
    for t in range(1, TERMS):
        fitted = fitted + poly[:, :, t, :] * basis[t]
    thin[:, 0:32] = fitted.reshape(256, 32)
    pack(2)
    copies[3].wait()
    for t in range(ROWS // 128):
        cols = slice(t * 128, (t + 1) * 128)
        wide[t] = coh[:, :, cols].astype(F32).reshape(256, 128)
        for c in range(8):
            coh_keep[c * 16:(c + 1) * 16, cols] = wide[t, pl.ds(core * 128 + c, 16, stride=8), :]
            send[c // 2][(c % 2) * 16:(c % 2) * 16 + 16, cols] = wide[t, pl.ds((1 - core) * 128 + c, 16, stride=8), :]


def one_hot(pairs, first, side, j):
    index = pairs[first + side:first + side + 1, j * BLOCK:(j + 1) * BLOCK].astype(jnp.int32)
    index = jnp.broadcast_to(index, (16, BLOCK)).astype(jnp.int16)
    index = jnp.concatenate([index] * (STATIONS // 16), axis=0)
    here = lax.broadcasted_iota(jnp.int16, (STATIONS, BLOCK), 0) == index
    return jnp.where(here, jnp.ones((STATIONS, BLOCK), BF16), jnp.zeros((STATIONS, BLOCK), BF16))


def put_table(table, c, t, first, second):
    high, rest = split_parts(jnp.concatenate([first, second], axis=0))
    table[c * 16:(c + 1) * 16, t * 128:(t + 1) * 128] = high
    table[128 + c * 16:128 + (c + 1) * 16, t * 128:(t + 1) * 128] = rest


def start_table(gathered, table):
    lane = lanes()
    for c in range(8):
        im, row = divmod(c, 4)
        for t in range(4):
            halves = []
            for h in range(2):
                total = None
                for b in range(4):
                    part = gathered[(4 * t + b) * 32 + row * 8:(4 * t + b) * 32 + row * 8 + 8, :]
                    shift = (b * 32 - im * 64 - h * 32) % 128
                    if shift:
                        part = pltpu.roll(part, shift, 1)
                    total = part if total is None else jnp.where(lane // 32 == b, part, total)
                halves.append(total)
            put_table(table, c, t, *halves)


def step_table(gathered, table):
    low = lanes() < 64
    for c in range(8):
        for t in range(4):
            a = gathered[(2 * t) * 64 + c * 8:(2 * t) * 64 + c * 8 + 8, :]
            b = gathered[(2 * t + 1) * 64 + c * 8:(2 * t + 1) * 64 + c * 8 + 8, :]
            first = jnp.where(low, a, pltpu.roll(b, 64, 1))
            second = jnp.where(low, pltpu.roll(a, 64, 1), b)
            put_table(table, c, t, first, second)


def first_own_kernel(gathered, coh, vis, pairs, z_ref, w_ref, s_ref, table, near, far):
    start_table(gathered, table)
    model(lambda i: (coh, i * 16), vis, pairs, 0, z_ref, w_ref, s_ref, table, near, far)


def own_kernel(gathered, coh, vis, pairs, z_ref, w_ref, s_ref, table, near, far):
    step_table(gathered, table)
    model(lambda i: (coh, i * 16), vis, pairs, 0, z_ref, w_ref, s_ref, table, near, far)


def other_kernel(table, recv_0, recv_1, recv_2, recv_3, z_ref, w_ref, s_ref, near, far):
    received = (recv_0, recv_1, recv_2, recv_3)
    model(lambda i: (received[i // 2], (i % 2) * 16), None, recv_3, 32, z_ref, w_ref, s_ref, table, near, far)


def other_after_kernel(table, recv_0, recv_1, recv_2, recv_3, after, *rest):
    other_kernel(table, recv_0, recv_1, recv_2, recv_3, *rest)


def first_other_kernel(
    table, recv_0, recv_1, recv_2, recv_3, state_keep, rho_a, z_ref, w_ref, s_ref, gains, duals, target, near, far
):
    received = (recv_0, recv_1, recv_2, recv_3)
    half_rho = 0.5 * rho_a[...]
    for c in range(8):
        at = c * 8
        state = [
            state_keep[which * 64 + at:which * 64 + at + 8, :]
            + received[which][32:40, c * 128:(c + 1) * 128]
            for which in range(3)
        ]
        gains[at:at + 8, :] = state[0]
        duals[at:at + 8, :] = state[1]
        target[at:at + 8, :] = half_rho * state[2] - 0.5 * state[1]
    other_kernel(table, *received, z_ref, w_ref, s_ref, near, far)


def model(coh_at, vis, pairs, first, z_ref, w_ref, s_ref, table, near, far):
    for j in range(ROWS // BLOCK):
        for side, dest in ((0, near), (1, far)):
            both = jnp.dot(table[...], one_hot(pairs, first, side, j), preferred_element_type=F32)
            dest[j % 2] = both[:128] + both[128:]
        for l in range(BLOCK // 128):
            at = j * BLOCK + l * 128

            def coherency(i):
                ref, row = coh_at(i)
                return ref[row:row + 16, at:at + 128]

            gp = matrix(lambda i: near[j % 2, i * 16:(i + 1) * 16, l * 128:(l + 1) * 128])
            gq = matrix(lambda i: far[j % 2, i * 16:(i + 1) * 16, l * 128:(l + 1) * 128])
            cc = matrix(coherency)
            z = product_nh(cc, gq)
            w = product(gp, cc)
            m = product(gp, z)
            for i in range(8):
                z_ref[i * 16:(i + 1) * 16, at:at + 128] = z[i // 4][i % 4]
                w_ref[i * 16:(i + 1) * 16, at:at + 128] = w[i // 4][i % 4]
                total = -jnp.sum(m[i // 4][i % 4], axis=0, keepdims=True)
                if vis is not None:
                    total = total + vis[i:i + 1, at:at + 128]
                s_ref[i:i + 1, at:at + 128] = total


def message_sums_kernel(
    z_ref, w_ref, s_here, s_there, pairs, before, moment, moment_z, out, part_0, part_1, part_2, part_3, left, acc, hot
):
    chan = lax.axis_index("chan")
    near = weigh(basis_at(chan))
    far = weigh(basis_at(chan ^ 4))
    own = comps(moment)
    other = comps(moment_z)
    for d, part in enumerate((part_0, part_1, part_2, part_3)):
        at = basis_at(chan ^ d)
        near_weight = dot_terms(at, near)
        far_weight = dot_terms(at, far)
        put(part, [near_weight * own[c] + far_weight * other[c] for c in range(8)])
    sums_own_kernel(z_ref, w_ref, s_here, s_there, pairs, before, out, left, acc, hot)


def half_sums(z_ref, w_ref, s_here, s_there, pairs, first, before, left, acc, hot):
    steps = ROWS // BLOCK
    for j in range(steps):
        for l in range(BLOCK // 128):
            src = j * BLOCK + l * 128
            r = matrix(lambda i: s_here[i:i + 1, src:src + 128] + s_there[i:i + 1, src:src + 128])
            z = matrix(lambda i: z_ref[i * 16:(i + 1) * 16, src:src + 128])
            w = matrix(lambda i: w_ref[i * 16:(i + 1) * 16, src:src + 128])
            for side, (num, den) in enumerate(
                ((product_nh(r, z), square_nh(z)), (product_hn(r, w), square_hn(w)))
            ):
                at = side * BLOCK + l * 128
                for i, value in enumerate(num[0] + num[1] + den):
                    high, rest = split_parts(value)
                    left[j, i * 16:(i + 1) * 16, at:at + 128] = high
                    left[j, 192 + i * 16:192 + (i + 1) * 16, at:at + 128] = rest
        for side in range(2):
            hot[j, :, side * BLOCK:(side + 1) * BLOCK] = one_hot(pairs, first, side, j)
        total = lax.dot_general(left[j], hot[j], (((1,), (1,)), ((), ())), preferred_element_type=F32)
        if j == 0:
            acc[...] = total if before is None else before[...] + total
        else:
            acc[...] += total


def sums_other_kernel(z_ref, w_ref, s_here, s_there, recv_3, acc, left, hot):
    half_sums(z_ref, w_ref, s_here, s_there, recv_3, 32, None, left, acc, hot)


def sums_own_kernel(z_ref, w_ref, s_here, s_there, pairs, before, out, left, acc, hot):
    half_sums(z_ref, w_ref, s_here, s_there, pairs, 0, before, left, acc, hot)
    low = lanes() < 64
    for c in range(12):
        for t in range(4):
            cols = slice(t * 128, (t + 1) * 128)
            at = c * 16
            v0 = acc[at:at + 8, cols] + acc[192 + at:192 + at + 8, cols]
            v1 = acc[at + 8:at + 16, cols] + acc[192 + at + 8:192 + at + 16, cols]
            out[(2 * t) * 96 + c * 8:(2 * t) * 96 + c * 8 + 8, :] = jnp.where(low, v0, pltpu.roll(v1, 64, 1))
            out[(2 * t + 1) * 96 + c * 8:(2 * t + 1) * 96 + c * 8 + 8, :] = jnp.where(low, pltpu.roll(v0, 64, 1), v1)


def updated(received, gains, target, rho):
    sums = []
    for c in range(12):
        parts = [received[d * 96 + c * 8:d * 96 + c * 8 + 8, :] for d in range(8)]
        while len(parts) > 1:
            parts = [parts[i] + parts[i + 1] for i in range(0, len(parts), 2)]
        sums.append(parts[0])
    half_rho = 0.5 * rho
    a, d, br, bi = sums[8] + half_rho, sums[9] + half_rho, sums[10], sums[11]
    scale = 0.5 / (a * d - br * br - bi * bi)
    n = [sums[i] + target[i] - half_rho * gains[i] for i in range(8)]
    result = [None] * 8
    for i in (0, 1):
        r0, r1, i0, i1 = n[2 * i], n[2 * i + 1], n[4 + 2 * i], n[5 + 2 * i]
        result[2 * i] = gains[2 * i] + scale * (r0 * d - (r1 * br + i1 * bi))
        result[4 + 2 * i] = gains[4 + 2 * i] + scale * (i0 * d - (i1 * br - r1 * bi))
        result[2 * i + 1] = gains[2 * i + 1] + scale * (r1 * a - (r0 * br - i0 * bi))
        result[5 + 2 * i] = gains[5 + 2 * i] + scale * (i1 * a - (i0 * br + r0 * bi))
    return result


def comps(ref):
    return [ref[c * 8:(c + 1) * 8, :] for c in range(8)]


def put(ref, values, base=0):
    for c in range(8):
        ref[base + c * 8:base + (c + 1) * 8, :] = values[c]


def update_kernel(received, gains, target, rho_a, gains_new, spread):
    new = updated(received, comps(gains), comps(target), rho_a[...])
    put(gains_new, new)
    for d in range(8):
        put(spread, new, d * 64)


def update_moment_kernel(received, gains, target, duals, rho_a, gains_new, spread, moment):
    rho = rho_a[...]
    new = updated(received, comps(gains), comps(target), rho)
    put(gains_new, new)
    for d in range(8):
        put(spread, new, d * 64)
    old = comps(duals)
    put(moment, [old[c] + rho * new[c] for c in range(8)])


def update_consensus_kernel(
    received, gains, part_0, part_1, part_2, part_3, duals, rho_a, gains_new, spread, duals_new, target
):
    rho = rho_a[...]
    old_gains = comps(gains)
    old_duals = comps(duals)
    parts = [comps(part) for part in (part_0, part_1, part_2, part_3)]
    fitted = [(parts[0][c] + parts[1][c]) + (parts[2][c] + parts[3][c]) for c in range(8)]
    new_duals = [old_duals[c] + rho * (old_gains[c] - fitted[c]) for c in range(8)]
    aim = [0.5 * (rho * fitted[c] - new_duals[c]) for c in range(8)]
    put(duals_new, new_duals)
    put(target, aim)
    new = updated(received, old_gains, aim, rho)
    put(gains_new, new)
    for d in range(8):
        put(spread, new, d * 64)


def update_last_kernel(received, gains, target, duals, rho_a, keep, send, moment):
    core = lax.axis_index("core")
    rho = rho_a[...]
    new = updated(received, comps(gains), comps(target), rho)
    old = comps(duals)
    lane = lanes()
    quarter = lane // 32
    whole = [old[c] + rho * new[c] for c in range(8)]
    for half in range(2):
        for c in range(4):
            total = jnp.zeros((8, 128), F32)
            for im in range(2):
                for h in range(2):
                    here = jnp.where(quarter == 2 * h + half, whole[im * 4 + c], 0.0)
                    shift = (im * 64 - 32 * h - 32 * half) % 128
                    total = total + (pltpu.roll(here, shift, 1) if shift else here)
            for f in range(CHANNELS):
                at = (2 * f + half) * 32 + c * 8
                moment[at:at + 8, :] = total
    for out, stations in ((keep, core), (send, 1 - core)):
        for base, values in ((0, new), (64, old)):
            for c in range(8):
                total = jnp.zeros((8, 128), F32)
                for h in range(2):
                    here = jnp.where(quarter == 2 * h + stations, values[c], 0.0)
                    total = total + pltpu.roll(here, (64 * core + 96 * stations + 96 * h) % 128, 1)
                out[base + c * 8:base + (c + 1) * 8, :] = total


def finish_kernel(
    moments, keep, recv, rho_f, gains_hbm, duals_hbm, poly_hbm, gains, duals, poly, thin, deep, sems
):
    chan = lax.axis_index("chan")
    rho = rho_f[...]
    low = lanes() < 64

    def place(ref, value, first, stride):
        for q in range(4):
            part = pltpu.roll(value, 128 - 32 * q, 1) if q else value
            ref[pl.ds(q * 8 * stride + first, 8, stride=stride), :] = part

    now = [keep[c * 8:(c + 1) * 8, :] + recv[c * 8:(c + 1) * 8, :] for c in range(16)]
    for c in range(8):
        place(thin, now[c], c, 8)
    gains[...] = thin[:, 0:32].reshape(32, 8, 32)
    stores = [pltpu.make_async_copy(gains, gains_hbm, sems.at[0])]
    stores[0].start()
    at = basis_at(chan)
    fitted = [None] * 8
    terms = []
    for t in range(TERMS):
        halves = []
        for half in range(2):
            for c in range(4):
                total = None
                for f in range(CHANNELS):
                    row = f * 64 + half * 32 + c * 8
                    part = float(SOLVE[t, f]) * moments[row:row + 8, :]
                    total = part if total is None else total + part
                halves.append(total)
        real = [jnp.where(low, halves[c], pltpu.roll(halves[4 + c], 64, 1)) for c in range(4)]
        imag = [jnp.where(low, pltpu.roll(halves[c], 64, 1), halves[4 + c]) for c in range(4)]
        terms.append(real + imag)
        for c, value in enumerate(real + imag):
            fitted[c] = value if t == 0 else fitted[c] + at[t] * value
    for c in range(8):
        place(thin, now[8 + c] + rho * (now[c] - fitted[c]), c, 8)
    duals[...] = thin[:, 0:32].reshape(32, 8, 32)
    stores.append(pltpu.make_async_copy(duals, duals_hbm, sems.at[1]))
    stores[1].start()
    for q in range(4):
        for t in range(TERMS):
            for c in range(8):
                part = pltpu.roll(terms[t][c], 128 - 32 * q, 1) if q else terms[t][c]
                deep[pl.ds(q * 256 + c * 4 + t, 8, stride=32), :] = part
        dirs = pl.ds(q * 8, 8)
        poly[dirs] = deep[q * 256:(q + 1) * 256, 0:32].reshape(8, 8, TERMS, 32)
        stores.append(pltpu.make_async_copy(poly.at[dirs], poly_hbm.at[dirs], sems.at[2 + q]))
        stores[-1].start()
    for store in stores:
        store.wait()


def local(coherency, visibilities, station_pairs, gains, duals, poly, penalty):
    def swap(x):
        return lax.ppermute(x, "core", CORE_SWAP)

    def exchange(x, axis):
        return lax.all_to_all(x, axis, 0, 0, tiled=True)

    packed = ((64, 128), F32)
    wide = ((512, 128), F32)
    small = ((8, 128), F32)
    state_in = pltpu.VMEM((32, 8, 32), F32)
    thin = pltpu.VMEM((256, 128), F32)
    spread, mark = call(
        spread_kernel, [wide, small], [thin], n_in=1
    )(gains[0])
    gathered = exchange(spread, ("st", "core"))
    coh_keep, state_keep, rho_a, rho_f, *send = call(
        prepare_kernel,
        [((128, ROWS), F32), ((192, 128), F32), small, small] + [((40, ROWS), F32)] * 4,
        [
            pltpu.VMEM((32, 8, ROWS), BF16), state_in, state_in, pltpu.VMEM((32, 8, TERMS, 32), F32),
            pltpu.VMEM((ROWS // 128, 256, 128), F32), thin, pltpu.SemaphoreType.DMA((4,)),
        ],
        hbm=(0, 1, 2, 3, 4), n_in=7,
    )(mark, coherency[0], gains[0], duals[0], poly, station_pairs, jnp.pad(penalty, (0, 96)).reshape(1, 128))
    received = [swap(x) for x in send]
    vis = visibilities[0]

    half_outs = [((128, ROWS), F32), ((128, ROWS), F32), ((8, ROWS), F32)]
    table_out = ((256, STATIONS), BF16)
    pair_scratch = [pltpu.VMEM((2, 128, BLOCK), F32)] * 2
    sums_out = ((768, 128), F32)
    blocks = ROWS // BLOCK
    left = pltpu.VMEM((blocks, 384, 2 * BLOCK), BF16)
    hot = pltpu.VMEM((blocks, STATIONS, 2 * BLOCK), BF16)
    total = pltpu.VMEM((384, STATIONS), F32)

    *own, table = call(first_own_kernel, half_outs + [table_out], pair_scratch, n_in=4)(
        gathered, coh_keep, vis, station_pairs
    )
    *other, gain, dual, target = call(
        first_other_kernel, half_outs + [packed, packed, packed], pair_scratch, n_in=7
    )(table, *received, state_keep, rho_a)

    def step_model(spread, *after):
        *own, table = call(own_kernel, half_outs + [table_out], pair_scratch, n_in=4)(
            exchange(spread, "st"), coh_keep, vis, station_pairs
        )
        kernel = other_after_kernel if after else other_kernel
        other = call(kernel, half_outs, pair_scratch, hbm=(5,), n_in=5 + len(after))(table, *received, *after)
        return own, other

    def step_sums(own, other, kernel=sums_own_kernel, outs=(), extra=()):
        from_own = swap(own[2])
        from_other = swap(other[2])
        (before,) = call(sums_other_kernel, [((384, STATIONS), F32)], [left, hot], n_in=5)(
            *other, from_own, received[3]
        )
        return call(kernel, [sums_out, *outs], [left, total, hot], n_in=6 + len(extra))(
            *own, from_other, station_pairs, before, *extra
        )

    def step(own, other):
        return exchange(step_sums(own, other)[0], "st")

    gain, spread = call(update_kernel, [packed, wide], n_in=4)(step(own, other), gain, target, rho_a)
    gain, spread, moment = call(update_moment_kernel, [packed, wide, packed], n_in=5)(
        step(*step_model(spread)), gain, target, dual, rho_a
    )

    def from_channel(x, distance):
        return lax.ppermute(x, "chan", [(f, f ^ distance) for f in range(CHANNELS)])

    moment_z = from_channel(moment, 4)
    parts, *messages = step_sums(
        *step_model(spread, moment_z), message_sums_kernel, [packed] * 4, (moment, moment_z)
    )
    shares = [messages[0]] + [from_channel(messages[d], d) for d in (1, 2, 3)]
    gain, spread, dual, target = call(update_consensus_kernel, [packed, wide, packed, packed], n_in=8)(
        exchange(parts, "st"), gain, *shares, dual, rho_a
    )
    keep, send, moment = call(update_last_kernel, [((128, 128), F32), ((1024, 128), F32), wide], n_in=5)(
        step(*step_model(spread)), gain, target, dual, rho_a
    )
    moments = exchange(moment, ("chan", "core"))
    gains_out, duals_out, poly_out = call(
        finish_kernel,
        [((32, 8, 32), F32), ((32, 8, 32), F32), ((32, 8, 4, 32), F32)],
        [
            state_in, state_in, pltpu.VMEM((32, 8, TERMS, 32), F32),
            thin, pltpu.VMEM((1024, 128), F32), pltpu.SemaphoreType.DMA((6,)),
        ],
        hbm_out=(0, 1, 2), n_in=4,
    )(moments, keep, swap(send), rho_f)
    return gains_out[None], duals_out[None], poly_out


def solution(mesh):
    chan, bl = mesh.devices.shape
    finer = Mesh(mesh.devices.reshape(chan, bl // 2, 2), ("chan", "st", "core"))
    both = ("st", "core")
    in_specs = (
        P("chan", None, None, both),
        P("chan", None, both),
        P(None, both),
        P("chan", None, None, both),
        P("chan", None, None, both),
        P(None, None, None, both),
        P(),
    )
    out_specs = (
        P("chan", None, None, both),
        P("chan", None, None, both),
        P(None, None, None, both),
    )
    return jax.shard_map(local, mesh=finer, in_specs=in_specs, out_specs=out_specs, check_vma=False)
```

```python
import jax
import jax.numpy as jnp
import numpy as np
from jax import lax
from jax.experimental import pallas as pl
from jax.experimental.pallas import tpu as pltpu
from jax.sharding import Mesh, PartitionSpec as P


CHANNELS = 8
TERMS = 4
ROWS = 1024
BLOCK = 256
STATIONS = 512
F32 = jnp.float32
BF16 = jnp.bfloat16
CORE_SWAP = [(0, 1), (1, 0)]
VMEM_BYTES = 24 * 1024 * 1024


def basis_of(place):
    square = place * place
    return [1.0 + 0.0 * place, place, 1.5 * square - 0.5, (2.5 * square - 1.5) * place]


def consensus_tables():
    basis = np.stack(basis_of((2.0 * np.arange(CHANNELS) + 1.0) / CHANNELS - 1.0), axis=1)
    inverse = np.linalg.inv(basis.T @ basis)
    return inverse, inverse @ basis.T


GRAM_INVERSE, SOLVE = consensus_tables()


def basis_at(channel):
    place = (2.0 * jnp.full((8, 128), channel, jnp.int32).astype(F32) + 1.0) / CHANNELS - 1.0
    return basis_of(place)


def dot_terms(a, b):
    total = a[0] * b[0]
    for t in range(1, TERMS):
        total = total + a[t] * b[t]
    return total


def weigh(values):
    return [
        sum(float(GRAM_INVERSE[t, u]) * values[u] for u in range(t % 2, TERMS, 2)) for t in range(TERMS)
    ]


def call(kernel, out_shapes, scratch=(), hbm=(), hbm_out=(), n_in=0):
    def specs(count, outside):
        return [pl.BlockSpec(memory_space=pl.ANY if i in outside else pltpu.VMEM) for i in range(count)]

    return pl.pallas_call(
        kernel,
        out_shape=[jax.ShapeDtypeStruct(s, d) for s, d in out_shapes],
        in_specs=specs(n_in, hbm),
        out_specs=specs(len(out_shapes), hbm_out),
        scratch_shapes=list(scratch),
        compiler_params=pltpu.CompilerParams(vmem_limit_bytes=VMEM_BYTES),
        cost_estimate=pl.CostEstimate(flops=0, bytes_accessed=1000, transcendentals=0),
    )


def lanes():
    return lax.broadcasted_iota(jnp.int32, (8, 128), 1)


def split_parts(x):
    high = x.astype(BF16)
    return high, (x - high.astype(F32)).astype(BF16)


def matrix(load):
    return [load(i) for i in range(4)], [load(4 + i) for i in range(4)]


def conj_t(m):
    re, im = m
    return [re[0], re[2], re[1], re[3]], [-im[0], -im[2], -im[1], -im[3]]


def product_nh(a, b):
    (ar, ai), (br, bi) = a, b
    re, im = [], []
    for i in (0, 1):
        for j in (0, 1):
            p, q, u, v = 2 * i, 2 * i + 1, 2 * j, 2 * j + 1
            re.append((ar[p] * br[u] + ai[p] * bi[u]) + (ar[q] * br[v] + ai[q] * bi[v]))
            im.append((ai[p] * br[u] - ar[p] * bi[u]) + (ai[q] * br[v] - ar[q] * bi[v]))
    return re, im


def product_hn(a, b):
    (ar, ai), (br, bi) = a, b
    re, im = [], []
    for i in (0, 1):
        for j in (0, 1):
            p, q, u, v = i, 2 + i, j, 2 + j
            re.append((ar[p] * br[u] + ai[p] * bi[u]) + (ar[q] * br[v] + ai[q] * bi[v]))
            im.append((ar[p] * bi[u] - ai[p] * br[u]) + (ar[q] * bi[v] - ai[q] * br[v]))
    return re, im


def product(a, b):
    (ar, ai), (br, bi) = a, b
    re, im = [], []
    for i in (0, 1):
        for j in (0, 1):
            p, q, u, v = 2 * i, 2 * i + 1, j, 2 + j
            re.append((ar[p] * br[u] - ai[p] * bi[u]) + (ar[q] * br[v] - ai[q] * bi[v]))
            im.append((ar[p] * bi[u] + ai[p] * br[u]) + (ar[q] * bi[v] + ai[q] * br[v]))
    return re, im


def square_nh(a):
    r, i = a
    return [
        (r[0] * r[0] + i[0] * i[0]) + (r[1] * r[1] + i[1] * i[1]),
        (r[2] * r[2] + i[2] * i[2]) + (r[3] * r[3] + i[3] * i[3]),
        (r[0] * r[2] + i[0] * i[2]) + (r[1] * r[3] + i[1] * i[3]),
        (i[0] * r[2] - r[0] * i[2]) + (i[1] * r[3] - r[1] * i[3]),
    ]


def square_hn(a):
    r, i = a
    return [
        (r[0] * r[0] + i[0] * i[0]) + (r[2] * r[2] + i[2] * i[2]),
        (r[1] * r[1] + i[1] * i[1]) + (r[3] * r[3] + i[3] * i[3]),
        (r[0] * r[1] + i[0] * i[1]) + (r[2] * r[3] + i[2] * i[3]),
        (r[0] * i[1] - i[0] * r[1]) + (r[2] * i[3] - i[2] * r[3]),
    ]


def spread_kernel(gains, spread, mark, thin):
    thin[...] = jnp.zeros((264, 128), F32)
    mark[...] = jnp.zeros((8, 128), F32)
    thin[0:256, 0:32] = gains[...].reshape(256, 32)
    for half in range(2):
        for c in range(4):
            total = None
            for im in range(2):
                for h in range(2):
                    part = thin[pl.ds((half * 16 + h * 8) * 8 + im * 4 + c, 8, stride=8), :]
                    if im or h:
                        part = pltpu.roll(part, im * 64 + h * 32, 1)
                    total = part if total is None else total + part
            for d in range(8):
                at = (2 * d + half) * 32 + c * 8
                spread[at:at + 8, :] = total


def prepare_kernel(
    mark, coh_hbm, gains_hbm, duals_hbm, poly_hbm, pairs, penalty,
    coh_keep, state_keep, rho_a, rho_f, send_0, send_1, send_2, send_3,
    coh, gains, duals, poly, wide, thin, sems,
):
    send = (send_0, send_1, send_2, send_3)
    copies = [
        pltpu.make_async_copy(src, dst, sems.at[i])
        for i, (src, dst) in enumerate(((gains_hbm, gains), (duals_hbm, duals), (poly_hbm, poly), (coh_hbm, coh)))
    ]
    for copy in copies:
        copy.start()
    core = lax.axis_index("core")
    chan = lax.axis_index("chan")
    row = lax.broadcasted_iota(jnp.int32, (8, 128), 0)
    lane = lanes()
    given = jnp.broadcast_to(penalty[...], (8, 128))
    column = [jnp.sum(jnp.where(lane == q * 8 + row, given, 0.0), axis=1, keepdims=True) for q in range(4)]
    by_dir = jnp.broadcast_to(column[0], (8, 128))
    for q in range(1, 4):
        by_dir = jnp.where(lane // 32 == q, column[q], by_dir)
    mine = jnp.full((8, 128), core, jnp.int32) == 0
    low = jnp.where(mine, column[0], column[2])
    high = jnp.where(mine, column[1], column[3])
    rho_a[...] = jnp.where(lane < 64, low, high)
    rho_f[...] = by_dir
    send_3[32:40, :] = jnp.zeros((8, ROWS), F32)
    send_3[32:34, :] = pairs[...].astype(F32)

    def pack(which):
        for c in range(8):
            for keep, half in ((True, core), (False, 1 - core)):
                total = None
                for h in range(2):
                    part = thin[pl.ds((half * 16 + h * 8) * 8 + c, 8, stride=8), :]
                    part = pltpu.roll(part, h * 64 + core * 32, 1)
                    total = part if total is None else total + part
                if keep:
                    state_keep[which * 64 + c * 8:which * 64 + (c + 1) * 8, :] = total
                else:
                    send[which][32:40, c * 128:(c + 1) * 128] = total

    thin[...] = jnp.zeros((264, 128), F32)
    copies[0].wait()
    thin[0:256, 0:32] = gains[...].reshape(256, 32)
    pack(0)
    copies[1].wait()
    thin[0:256, 0:32] = duals[...].reshape(256, 32)
    pack(1)
    copies[2].wait()
    place = (2.0 * chan.astype(F32) + 1.0) * (1.0 / CHANNELS) - 1.0
    basis = basis_of(place)
    fitted = poly[:, :, 0, :]
    for t in range(1, TERMS):
        fitted = fitted + poly[:, :, t, :] * basis[t]
    thin[0:256, 0:32] = fitted.reshape(256, 32)
    pack(2)
    copies[3].wait()
    for t in range(ROWS // 128):
        cols = slice(t * 128, (t + 1) * 128)
        wide[t, 0:256, :] = coh[:, :, cols].astype(F32).reshape(256, 128)
        for c in range(8):
            coh_keep[c * 16:(c + 1) * 16, cols] = wide[t, pl.ds(core * 128 + c, 16, stride=8), :]
            send[c // 2][(c % 2) * 16:(c % 2) * 16 + 16, cols] = wide[t, pl.ds((1 - core) * 128 + c, 16, stride=8), :]


def one_hot(pairs, first, side, j):
    index = pairs[first + side:first + side + 1, j * BLOCK:(j + 1) * BLOCK].astype(jnp.int32)
    index = jnp.broadcast_to(index, (16, BLOCK)).astype(jnp.int16)
    index = jnp.concatenate([index] * (STATIONS // 16), axis=0)
    here = lax.broadcasted_iota(jnp.int16, (STATIONS, BLOCK), 0) == index
    return jnp.where(here, jnp.ones((STATIONS, BLOCK), BF16), jnp.zeros((STATIONS, BLOCK), BF16))


def put_table(table, c, t, first, second):
    high, rest = split_parts(jnp.concatenate([first, second], axis=0))
    table[c * 16:(c + 1) * 16, t * 128:(t + 1) * 128] = high
    table[128 + c * 16:128 + (c + 1) * 16, t * 128:(t + 1) * 128] = rest


def start_table(gathered, table):
    lane = lanes()
    for c in range(8):
        im, row = divmod(c, 4)
        for t in range(4):
            halves = []
            for h in range(2):
                total = None
                for b in range(4):
                    part = gathered[(4 * t + b) * 32 + row * 8:(4 * t + b) * 32 + row * 8 + 8, :]
                    shift = (b * 32 - im * 64 - h * 32) % 128
                    if shift:
                        part = pltpu.roll(part, shift, 1)
                    total = part if total is None else jnp.where(lane // 32 == b, part, total)
                halves.append(total)
            put_table(table, c, t, *halves)


def step_table(gathered, table):
    low = lanes() < 64
    for c in range(8):
        for t in range(4):
            a = gathered[(2 * t) * 64 + c * 8:(2 * t) * 64 + c * 8 + 8, :]
            b = gathered[(2 * t + 1) * 64 + c * 8:(2 * t + 1) * 64 + c * 8 + 8, :]
            first = jnp.where(low, a, pltpu.roll(b, 64, 1))
            second = jnp.where(low, pltpu.roll(a, 64, 1), b)
            put_table(table, c, t, first, second)


def first_own_kernel(gathered, coh, vis, pairs, z_ref, w_ref, s_ref, table, near, far):
    start_table(gathered, table)
    model(lambda i: (coh, i * 16), vis, pairs, 0, z_ref, w_ref, s_ref, table, near, far)


def own_kernel(gathered, coh, vis, pairs, z_ref, w_ref, s_ref, table, near, far):
    step_table(gathered, table)
    model(lambda i: (coh, i * 16), vis, pairs, 0, z_ref, w_ref, s_ref, table, near, far)


def other_kernel(table, recv_0, recv_1, recv_2, recv_3, z_ref, w_ref, s_ref, near, far):
    received = (recv_0, recv_1, recv_2, recv_3)
    model(lambda i: (received[i // 2], (i % 2) * 16), None, recv_3, 32, z_ref, w_ref, s_ref, table, near, far)


def other_after_kernel(table, recv_0, recv_1, recv_2, recv_3, after, *rest):
    other_kernel(table, recv_0, recv_1, recv_2, recv_3, *rest)


def first_other_kernel(
    table, recv_0, recv_1, recv_2, recv_3, state_keep, rho_a, z_ref, w_ref, s_ref, gains, duals, target, near, far
):
    received = (recv_0, recv_1, recv_2, recv_3)
    half_rho = 0.5 * rho_a[...]
    for c in range(8):
        at = c * 8
        state = [
            state_keep[which * 64 + at:which * 64 + at + 8, :]
            + received[which][32:40, c * 128:(c + 1) * 128]
            for which in range(3)
        ]
        gains[at:at + 8, :] = state[0]
        duals[at:at + 8, :] = state[1]
        target[at:at + 8, :] = half_rho * state[2] - 0.5 * state[1]
    other_kernel(table, *received, z_ref, w_ref, s_ref, near, far)


def model(coh_at, vis, pairs, first, z_ref, w_ref, s_ref, table, near, far):
    for j in range(ROWS // BLOCK):
        for side, dest in ((0, near), (1, far)):
            both = jnp.dot(table[...], one_hot(pairs, first, side, j), preferred_element_type=F32)
            dest[j % 2] = both[:128] + both[128:]
        for l in range(BLOCK // 128):
            at = j * BLOCK + l * 128

            def coherency(i):
                ref, row = coh_at(i)
                return ref[row:row + 16, at:at + 128]

            gp = matrix(lambda i: near[j % 2, i * 16:(i + 1) * 16, l * 128:(l + 1) * 128])
            gq = matrix(lambda i: far[j % 2, i * 16:(i + 1) * 16, l * 128:(l + 1) * 128])
            cc = matrix(coherency)
            z = product_nh(cc, gq)
            w = product(gp, cc)
            m = product(gp, z)
            for i in range(8):
                z_ref[i * 16:(i + 1) * 16, at:at + 128] = z[i // 4][i % 4]
                w_ref[i * 16:(i + 1) * 16, at:at + 128] = w[i // 4][i % 4]
                total = -jnp.sum(m[i // 4][i % 4], axis=0, keepdims=True)
                if vis is not None:
                    total = total + vis[i:i + 1, at:at + 128]
                s_ref[i:i + 1, at:at + 128] = total


def message_sums_kernel(
    z_ref, w_ref, s_here, s_there, pairs, before, moment, moment_z, out, part_0, part_1, part_2, part_3, left, acc, hot
):
    chan = lax.axis_index("chan")
    near = weigh(basis_at(chan))
    far = weigh(basis_at(chan ^ 4))
    own = comps(moment)
    other = comps(moment_z)
    for d, part in enumerate((part_0, part_1, part_2, part_3)):
        at = basis_at(chan ^ d)
        near_weight = dot_terms(at, near)
        far_weight = dot_terms(at, far)
        put(part, [near_weight * own[c] + far_weight * other[c] for c in range(8)])
    sums_own_kernel(z_ref, w_ref, s_here, s_there, pairs, before, out, left, acc, hot)


def half_sums(z_ref, w_ref, s_here, s_there, pairs, first, before, left, acc, hot):
    steps = ROWS // BLOCK
    for j in range(steps):
        for l in range(BLOCK // 128):
            src = j * BLOCK + l * 128
            r = matrix(lambda i: s_here[i:i + 1, src:src + 128] + s_there[i:i + 1, src:src + 128])
            z = matrix(lambda i: z_ref[i * 16:(i + 1) * 16, src:src + 128])
            w = matrix(lambda i: w_ref[i * 16:(i + 1) * 16, src:src + 128])
            for side, (num, den) in enumerate(
                ((product_nh(r, z), square_nh(z)), (product_hn(r, w), square_hn(w)))
            ):
                at = side * BLOCK + l * 128
                for i, value in enumerate(num[0] + num[1] + den):
                    high, rest = split_parts(value)
                    left[j, i * 16:(i + 1) * 16, at:at + 128] = high
                    left[j, 192 + i * 16:192 + (i + 1) * 16, at:at + 128] = rest
        for side in range(2):
            hot[j, :, side * BLOCK:(side + 1) * BLOCK] = one_hot(pairs, first, side, j)
        total = lax.dot_general(left[j], hot[j], (((1,), (1,)), ((), ())), preferred_element_type=F32)
        if j == 0:
            acc[...] = total if before is None else before[...] + total
        else:
            acc[...] += total


def sums_other_kernel(z_ref, w_ref, s_here, s_there, recv_3, acc, left, hot):
    half_sums(z_ref, w_ref, s_here, s_there, recv_3, 32, None, left, acc, hot)


def sums_own_kernel(z_ref, w_ref, s_here, s_there, pairs, before, out, left, acc, hot):
    half_sums(z_ref, w_ref, s_here, s_there, pairs, 0, before, left, acc, hot)
    low = lanes() < 64
    for c in range(12):
        for t in range(4):
            cols = slice(t * 128, (t + 1) * 128)
            at = c * 16
            v0 = acc[at:at + 8, cols] + acc[192 + at:192 + at + 8, cols]
            v1 = acc[at + 8:at + 16, cols] + acc[192 + at + 8:192 + at + 16, cols]
            out[(2 * t) * 96 + c * 8:(2 * t) * 96 + c * 8 + 8, :] = jnp.where(low, v0, pltpu.roll(v1, 64, 1))
            out[(2 * t + 1) * 96 + c * 8:(2 * t + 1) * 96 + c * 8 + 8, :] = jnp.where(low, pltpu.roll(v0, 64, 1), v1)


def updated(received, gains, target, rho):
    sums = []
    for c in range(12):
        parts = [received[d * 96 + c * 8:d * 96 + c * 8 + 8, :] for d in range(8)]
        while len(parts) > 1:
            parts = [parts[i] + parts[i + 1] for i in range(0, len(parts), 2)]
        sums.append(parts[0])
    half_rho = 0.5 * rho
    a, d, br, bi = sums[8] + half_rho, sums[9] + half_rho, sums[10], sums[11]
    scale = 0.5 / (a * d - br * br - bi * bi)
    n = [sums[i] + target[i] - half_rho * gains[i] for i in range(8)]
    result = [None] * 8
    for i in (0, 1):
        r0, r1, i0, i1 = n[2 * i], n[2 * i + 1], n[4 + 2 * i], n[5 + 2 * i]
        result[2 * i] = gains[2 * i] + scale * (r0 * d - (r1 * br + i1 * bi))
        result[4 + 2 * i] = gains[4 + 2 * i] + scale * (i0 * d - (i1 * br - r1 * bi))
        result[2 * i + 1] = gains[2 * i + 1] + scale * (r1 * a - (r0 * br - i0 * bi))
        result[5 + 2 * i] = gains[5 + 2 * i] + scale * (i1 * a - (i0 * br + r0 * bi))
    return result


def comps(ref):
    return [ref[c * 8:(c + 1) * 8, :] for c in range(8)]


def put(ref, values, base=0):
    for c in range(8):
        ref[base + c * 8:base + (c + 1) * 8, :] = values[c]


def update_kernel(received, gains, target, rho_a, gains_new, spread):
    new = updated(received, comps(gains), comps(target), rho_a[...])
    put(gains_new, new)
    for d in range(8):
        put(spread, new, d * 64)


def update_moment_kernel(received, gains, target, duals, rho_a, gains_new, spread, moment):
    rho = rho_a[...]
    new = updated(received, comps(gains), comps(target), rho)
    put(gains_new, new)
    for d in range(8):
        put(spread, new, d * 64)
    old = comps(duals)
    put(moment, [old[c] + rho * new[c] for c in range(8)])


def update_consensus_kernel(
    received, gains, part_0, part_1, part_2, part_3, duals, rho_a, gains_new, spread, duals_new, target
):
    rho = rho_a[...]
    old_gains = comps(gains)
    old_duals = comps(duals)
    parts = [comps(part) for part in (part_0, part_1, part_2, part_3)]
    fitted = [(parts[0][c] + parts[1][c]) + (parts[2][c] + parts[3][c]) for c in range(8)]
    new_duals = [old_duals[c] + rho * (old_gains[c] - fitted[c]) for c in range(8)]
    aim = [0.5 * (rho * fitted[c] - new_duals[c]) for c in range(8)]
    put(duals_new, new_duals)
    put(target, aim)
    new = updated(received, old_gains, aim, rho)
    put(gains_new, new)
    for d in range(8):
        put(spread, new, d * 64)


def update_last_kernel(received, gains, target, duals, rho_a, keep, send, moment):
    core = lax.axis_index("core")
    rho = rho_a[...]
    new = updated(received, comps(gains), comps(target), rho)
    old = comps(duals)
    lane = lanes()
    quarter = lane // 32
    whole = [old[c] + rho * new[c] for c in range(8)]
    for half in range(2):
        for c in range(4):
            total = jnp.zeros((8, 128), F32)
            for im in range(2):
                for h in range(2):
                    here = jnp.where(quarter == 2 * h + half, whole[im * 4 + c], 0.0)
                    shift = (im * 64 - 32 * h - 32 * half) % 128
                    total = total + (pltpu.roll(here, shift, 1) if shift else here)
            for f in range(CHANNELS):
                at = (2 * f + half) * 32 + c * 8
                moment[at:at + 8, :] = total
    for out, stations in ((keep, core), (send, 1 - core)):
        for base, values in ((0, new), (64, old)):
            for c in range(8):
                total = jnp.zeros((8, 128), F32)
                for h in range(2):
                    here = jnp.where(quarter == 2 * h + stations, values[c], 0.0)
                    total = total + pltpu.roll(here, (64 * core + 96 * stations + 96 * h) % 128, 1)
                out[base + c * 8:base + (c + 1) * 8, :] = total


def finish_kernel(
    moments, keep, recv, rho_f, gains_hbm, duals_hbm, poly_hbm, gains, duals, poly, thin, deep, sems
):
    chan = lax.axis_index("chan")
    rho = rho_f[...]
    low = lanes() < 64

    def place(ref, value, first, stride):
        for q in range(4):
            part = pltpu.roll(value, 128 - 32 * q, 1) if q else value
            ref[pl.ds(q * 8 * stride + first, 8, stride=stride), :] = part

    now = [keep[c * 8:(c + 1) * 8, :] + recv[c * 8:(c + 1) * 8, :] for c in range(16)]
    for c in range(8):
        place(thin, now[c], c, 8)
    gains[...] = thin[0:256, 0:32].reshape(32, 8, 32)
    stores = [pltpu.make_async_copy(gains, gains_hbm, sems.at[0])]
    stores[0].start()
    at = basis_at(chan)
    fitted = [None] * 8
    terms = []
    for t in range(TERMS):
        halves = []
        for half in range(2):
            for c in range(4):
                total = None
                for f in range(CHANNELS):
                    row = f * 64 + half * 32 + c * 8
                    part = float(SOLVE[t, f]) * moments[row:row + 8, :]
                    total = part if total is None else total + part
                halves.append(total)
        real = [jnp.where(low, halves[c], pltpu.roll(halves[4 + c], 64, 1)) for c in range(4)]
        imag = [jnp.where(low, pltpu.roll(halves[c], 64, 1), halves[4 + c]) for c in range(4)]
        terms.append(real + imag)
        for c, value in enumerate(real + imag):
            fitted[c] = value if t == 0 else fitted[c] + at[t] * value
    for c in range(8):
        place(thin, now[8 + c] + rho * (now[c] - fitted[c]), c, 8)
    duals[...] = thin[0:256, 0:32].reshape(32, 8, 32)
    stores.append(pltpu.make_async_copy(duals, duals_hbm, sems.at[1]))
    stores[1].start()
    for q in range(4):
        for t in range(TERMS):
            for c in range(8):
                part = pltpu.roll(terms[t][c], 128 - 32 * q, 1) if q else terms[t][c]
                deep[pl.ds(q * 256 + c * 4 + t, 8, stride=32), :] = part
        dirs = pl.ds(q * 8, 8)
        poly[dirs] = deep[q * 256:(q + 1) * 256, 0:32].reshape(8, 8, TERMS, 32)
        stores.append(pltpu.make_async_copy(poly.at[dirs], poly_hbm.at[dirs], sems.at[2 + q]))
        stores[-1].start()
    for store in stores:
        store.wait()


def local(coherency, visibilities, station_pairs, gains, duals, poly, penalty):
    def swap(x):
        return lax.ppermute(x, "core", CORE_SWAP)

    def exchange(x, axis):
        return lax.all_to_all(x, axis, 0, 0, tiled=True)

    packed = ((64, 128), F32)
    wide = ((512, 128), F32)
    small = ((8, 128), F32)
    state_in = pltpu.VMEM((32, 8, 32), F32)
    thin = pltpu.VMEM((264, 128), F32)
    spread, mark = call(
        spread_kernel, [wide, small], [thin], n_in=1
    )(gains[0])
    gathered = exchange(spread, ("st", "core"))
    coh_keep, state_keep, rho_a, rho_f, *send = call(
        prepare_kernel,
        [((128, ROWS), F32), ((192, 128), F32), small, small] + [((40, ROWS), F32)] * 4,
        [
            pltpu.VMEM((32, 8, ROWS), BF16), state_in, state_in, pltpu.VMEM((32, 8, TERMS, 32), F32),
            pltpu.VMEM((ROWS // 128, 264, 128), F32), thin, pltpu.SemaphoreType.DMA((4,)),
        ],
        hbm=(0, 1, 2, 3, 4), n_in=7,
    )(mark, coherency[0], gains[0], duals[0], poly, station_pairs, jnp.pad(penalty, (0, 96)).reshape(1, 128))
    received = [swap(x) for x in send]
    vis = visibilities[0]

    half_outs = [((128, ROWS), F32), ((128, ROWS), F32), ((8, ROWS), F32)]
    table_out = ((256, STATIONS), BF16)
    pair_scratch = [pltpu.VMEM((2, 128, BLOCK), F32)] * 2
    sums_out = ((768, 128), F32)
    blocks = ROWS // BLOCK
    left = pltpu.VMEM((blocks, 384, 2 * BLOCK), BF16)
    hot = pltpu.VMEM((blocks, STATIONS, 2 * BLOCK), BF16)
    total = pltpu.VMEM((384, STATIONS), F32)

    *own, table = call(first_own_kernel, half_outs + [table_out], pair_scratch, n_in=4)(
        gathered, coh_keep, vis, station_pairs
    )
    *other, gain, dual, target = call(
        first_other_kernel, half_outs + [packed, packed, packed], pair_scratch, n_in=7
    )(table, *received, state_keep, rho_a)

    def step_model(spread, *after):
        *own, table = call(own_kernel, half_outs + [table_out], pair_scratch, n_in=4)(
            exchange(spread, "st"), coh_keep, vis, station_pairs
        )
        kernel = other_after_kernel if after else other_kernel
        other = call(kernel, half_outs, pair_scratch, hbm=(5,), n_in=5 + len(after))(table, *received, *after)
        return own, other

    def step_sums(own, other, kernel=sums_own_kernel, outs=(), extra=()):
        from_own = swap(own[2])
        from_other = swap(other[2])
        (before,) = call(sums_other_kernel, [((384, STATIONS), F32)], [left, hot], n_in=5)(
            *other, from_own, received[3]
        )
        return call(kernel, [sums_out, *outs], [left, total, hot], n_in=6 + len(extra))(
            *own, from_other, station_pairs, before, *extra
        )

    def step(own, other):
        return exchange(step_sums(own, other)[0], "st")

    gain, spread = call(update_kernel, [packed, wide], n_in=4)(step(own, other), gain, target, rho_a)
    gain, spread, moment = call(update_moment_kernel, [packed, wide, packed], n_in=5)(
        step(*step_model(spread)), gain, target, dual, rho_a
    )

    def from_channel(x, distance):
        return lax.ppermute(x, "chan", [(f, f ^ distance) for f in range(CHANNELS)])

    moment_z = from_channel(moment, 4)
    parts, *messages = step_sums(
        *step_model(spread, moment_z), message_sums_kernel, [packed] * 4, (moment, moment_z)
    )
    shares = [messages[0]] + [from_channel(messages[d], d) for d in (1, 2, 3)]
    gain, spread, dual, target = call(update_consensus_kernel, [packed, wide, packed, packed], n_in=8)(
        exchange(parts, "st"), gain, *shares, dual, rho_a
    )
    keep, send, moment = call(update_last_kernel, [((128, 128), F32), ((1024, 128), F32), wide], n_in=5)(
        step(*step_model(spread)), gain, target, dual, rho_a
    )
    moments = exchange(moment, ("chan", "core"))
    gains_out, duals_out, poly_out = call(
        finish_kernel,
        [((32, 8, 32), F32), ((32, 8, 32), F32), ((32, 8, 4, 32), F32)],
        [
            state_in, state_in, pltpu.VMEM((32, 8, TERMS, 32), F32),
            thin, pltpu.VMEM((1056, 128), F32), pltpu.SemaphoreType.DMA((6,)),
        ],
        hbm_out=(0, 1, 2), n_in=4,
    )(moments, keep, swap(send), rho_f)
    return gains_out[None], duals_out[None], poly_out


def solution(mesh):
    chan, bl = mesh.devices.shape
    finer = Mesh(mesh.devices.reshape(chan, bl // 2, 2), ("chan", "st", "core"))
    both = ("st", "core")
    in_specs = (
        P("chan", None, None, both),
        P("chan", None, both),
        P(None, both),
        P("chan", None, None, both),
        P("chan", None, None, both),
        P(None, None, None, both),
        P(),
    )
    out_specs = (
        P("chan", None, None, both),
        P("chan", None, None, both),
        P(None, None, None, both),
    )
    return jax.shard_map(local, mesh=finer, in_specs=in_specs, out_specs=out_specs, check_vma=False)
```

```python
import jax
import jax.numpy as jnp
import numpy as np
from jax import lax
from jax.experimental import pallas as pl
from jax.experimental.pallas import tpu as pltpu
from jax.sharding import Mesh, PartitionSpec as P


CHANNELS = 8
TERMS = 4
ROWS = 1024
BLOCK = 256
STATIONS = 512
F32 = jnp.float32
BF16 = jnp.bfloat16
CORE_SWAP = [(0, 1), (1, 0)]
VMEM_BYTES = 24 * 1024 * 1024


def basis_of(place):
    square = place * place
    return [1.0 + 0.0 * place, place, 1.5 * square - 0.5, (2.5 * square - 1.5) * place]


def consensus_tables():
    basis = np.stack(basis_of((2.0 * np.arange(CHANNELS) + 1.0) / CHANNELS - 1.0), axis=1)
    inverse = np.linalg.inv(basis.T @ basis)
    return inverse, inverse @ basis.T


GRAM_INVERSE, SOLVE = consensus_tables()


def basis_at(channel):
    place = (2.0 * jnp.full((8, 128), channel, jnp.int32).astype(F32) + 1.0) / CHANNELS - 1.0
    return basis_of(place)


def dot_terms(a, b):
    total = a[0] * b[0]
    for t in range(1, TERMS):
        total = total + a[t] * b[t]
    return total


def weigh(values):
    return [
        sum(float(GRAM_INVERSE[t, u]) * values[u] for u in range(t % 2, TERMS, 2)) for t in range(TERMS)
    ]


def call(kernel, out_shapes, scratch=(), hbm=(), hbm_out=(), n_in=0):
    def specs(count, outside):
        return [pl.BlockSpec(memory_space=pl.ANY if i in outside else pltpu.VMEM) for i in range(count)]

    return pl.pallas_call(
        kernel,
        out_shape=[jax.ShapeDtypeStruct(s, d) for s, d in out_shapes],
        in_specs=specs(n_in, hbm),
        out_specs=specs(len(out_shapes), hbm_out),
        scratch_shapes=list(scratch),
        compiler_params=pltpu.CompilerParams(vmem_limit_bytes=VMEM_BYTES),
        cost_estimate=pl.CostEstimate(flops=0, bytes_accessed=1000, transcendentals=0),
    )


def lanes():
    return lax.broadcasted_iota(jnp.int32, (8, 128), 1)


def split_parts(x):
    high = x.astype(BF16)
    return high, (x - high.astype(F32)).astype(BF16)


def matrix(load):
    return [load(i) for i in range(4)], [load(4 + i) for i in range(4)]


def conj_t(m):
    re, im = m
    return [re[0], re[2], re[1], re[3]], [-im[0], -im[2], -im[1], -im[3]]


def product_nh(a, b):
    (ar, ai), (br, bi) = a, b
    re, im = [], []
    for i in (0, 1):
        for j in (0, 1):
            p, q, u, v = 2 * i, 2 * i + 1, 2 * j, 2 * j + 1
            re.append((ar[p] * br[u] + ai[p] * bi[u]) + (ar[q] * br[v] + ai[q] * bi[v]))
            im.append((ai[p] * br[u] - ar[p] * bi[u]) + (ai[q] * br[v] - ar[q] * bi[v]))
    return re, im


def product_hn(a, b):
    (ar, ai), (br, bi) = a, b
    re, im = [], []
    for i in (0, 1):
        for j in (0, 1):
            p, q, u, v = i, 2 + i, j, 2 + j
            re.append((ar[p] * br[u] + ai[p] * bi[u]) + (ar[q] * br[v] + ai[q] * bi[v]))
            im.append((ar[p] * bi[u] - ai[p] * br[u]) + (ar[q] * bi[v] - ai[q] * br[v]))
    return re, im


def product(a, b):
    (ar, ai), (br, bi) = a, b
    re, im = [], []
    for i in (0, 1):
        for j in (0, 1):
            p, q, u, v = 2 * i, 2 * i + 1, j, 2 + j
            re.append((ar[p] * br[u] - ai[p] * bi[u]) + (ar[q] * br[v] - ai[q] * bi[v]))
            im.append((ar[p] * bi[u] + ai[p] * br[u]) + (ar[q] * bi[v] + ai[q] * br[v]))
    return re, im


def square_nh(a):
    r, i = a
    return [
        (r[0] * r[0] + i[0] * i[0]) + (r[1] * r[1] + i[1] * i[1]),
        (r[2] * r[2] + i[2] * i[2]) + (r[3] * r[3] + i[3] * i[3]),
        (r[0] * r[2] + i[0] * i[2]) + (r[1] * r[3] + i[1] * i[3]),
        (i[0] * r[2] - r[0] * i[2]) + (i[1] * r[3] - r[1] * i[3]),
    ]


def square_hn(a):
    r, i = a
    return [
        (r[0] * r[0] + i[0] * i[0]) + (r[2] * r[2] + i[2] * i[2]),
        (r[1] * r[1] + i[1] * i[1]) + (r[3] * r[3] + i[3] * i[3]),
        (r[0] * r[1] + i[0] * i[1]) + (r[2] * r[3] + i[2] * i[3]),
        (r[0] * i[1] - i[0] * r[1]) + (r[2] * i[3] - i[2] * r[3]),
    ]


def spread_kernel(gains, spread, mark, thin):
    thin[...] = jnp.zeros((264, 128), F32)
    mark[...] = jnp.zeros((8, 128), F32)
    thin[0:256, 0:32] = gains[...].reshape(256, 32)
    for half in range(2):
        for c in range(4):
            total = None
            for im in range(2):
                for h in range(2):
                    part = thin[pl.ds((half * 16 + h * 8) * 8 + im * 4 + c, 8, stride=8), :]
                    if im or h:
                        part = pltpu.roll(part, im * 64 + h * 32, 1)
                    total = part if total is None else total + part
            for d in range(8):
                at = (2 * d + half) * 32 + c * 8
                spread[at:at + 8, :] = total


def prepare_kernel(
    mark, coh_hbm, gains_hbm, duals_hbm, poly_hbm, pairs, penalty,
    coh_keep, state_keep, rho_a, rho_f, send_0, send_1, send_2, send_3,
    coh, gains, duals, poly, wide, thin, sems,
):
    send = (send_0, send_1, send_2, send_3)
    copies = [
        pltpu.make_async_copy(src, dst, sems.at[i])
        for i, (src, dst) in enumerate(((gains_hbm, gains), (duals_hbm, duals), (poly_hbm, poly), (coh_hbm, coh)))
    ]
    for copy in copies:
        copy.start()
    core = lax.axis_index("core")
    chan = lax.axis_index("chan")
    row = lax.broadcasted_iota(jnp.int32, (8, 128), 0)
    lane = lanes()
    given = jnp.broadcast_to(penalty[...], (8, 128))
    column = [jnp.sum(jnp.where(lane == q * 8 + row, given, 0.0), axis=1, keepdims=True) for q in range(4)]
    by_dir = jnp.broadcast_to(column[0], (8, 128))
    for q in range(1, 4):
        by_dir = jnp.where(lane // 32 == q, column[q], by_dir)
    mine = jnp.full((8, 128), core, jnp.int32) == 0
    low = jnp.where(mine, column[0], column[2])
    high = jnp.where(mine, column[1], column[3])
    rho_a[...] = jnp.where(lane < 64, low, high)
    rho_f[...] = by_dir
    send_3[32:40, :] = jnp.zeros((8, ROWS), F32)
    send_3[32:34, :] = pairs[...].astype(F32)

    def pack(which):
        for c in range(8):
            for keep, half in ((True, core), (False, 1 - core)):
                total = None
                for h in range(2):
                    part = thin[pl.ds((half * 16 + h * 8) * 8 + c, 8, stride=8), :]
                    part = pltpu.roll(part, h * 64 + core * 32, 1)
                    total = part if total is None else total + part
                if keep:
                    state_keep[which * 64 + c * 8:which * 64 + (c + 1) * 8, :] = total
                else:
                    send[which][32:40, c * 128:(c + 1) * 128] = total

    thin[...] = jnp.zeros((264, 128), F32)
    copies[0].wait()
    thin[0:256, 0:32] = gains[...].reshape(256, 32)
    pack(0)
    copies[1].wait()
    thin[0:256, 0:32] = duals[...].reshape(256, 32)
    pack(1)
    copies[2].wait()
    place = (2.0 * chan.astype(F32) + 1.0) * (1.0 / CHANNELS) - 1.0
    basis = basis_of(place)
    fitted = poly[:, :, 0, :]
    for t in range(1, TERMS):
        fitted = fitted + poly[:, :, t, :] * basis[t]
    thin[0:256, 0:32] = fitted.reshape(256, 32)
    pack(2)
    copies[3].wait()
    for t in range(ROWS // 128):
        cols = slice(t * 128, (t + 1) * 128)
        wide[t, 0:256, :] = coh[:, :, cols].astype(F32).reshape(256, 128)
        for c in range(8):
            coh_keep[c * 16:(c + 1) * 16, cols] = wide[t, pl.ds(core * 128 + c, 16, stride=8), :]
            send[c // 2][(c % 2) * 16:(c % 2) * 16 + 16, cols] = wide[t, pl.ds((1 - core) * 128 + c, 16, stride=8), :]


def one_hot(pairs, first, side, j):
    index = pairs[first + side:first + side + 1, j * BLOCK:(j + 1) * BLOCK].astype(jnp.int32)
    index = jnp.broadcast_to(index, (16, BLOCK)).astype(jnp.int16)
    index = jnp.concatenate([index] * (STATIONS // 16), axis=0)
    here = lax.broadcasted_iota(jnp.int16, (STATIONS, BLOCK), 0) == index
    return jnp.where(here, jnp.ones((STATIONS, BLOCK), BF16), jnp.zeros((STATIONS, BLOCK), BF16))


def put_table(table, c, t, first, second):
    high, rest = split_parts(jnp.concatenate([first, second], axis=0))
    table[c * 16:(c + 1) * 16, t * 128:(t + 1) * 128] = high
    table[128 + c * 16:128 + (c + 1) * 16, t * 128:(t + 1) * 128] = rest


def start_table(gathered, table):
    lane = lanes()
    for c in range(8):
        im, row = divmod(c, 4)
        for t in range(4):
            halves = []
            for h in range(2):
                total = None
                for b in range(4):
                    part = gathered[(4 * t + b) * 32 + row * 8:(4 * t + b) * 32 + row * 8 + 8, :]
                    shift = (b * 32 - im * 64 - h * 32) % 128
                    if shift:
                        part = pltpu.roll(part, shift, 1)
                    total = part if total is None else jnp.where(lane // 32 == b, part, total)
                halves.append(total)
            put_table(table, c, t, *halves)


def step_table(gathered, table):
    low = lanes() < 64
    for c in range(8):
        for t in range(4):
            a = gathered[(2 * t) * 64 + c * 8:(2 * t) * 64 + c * 8 + 8, :]
            b = gathered[(2 * t + 1) * 64 + c * 8:(2 * t + 1) * 64 + c * 8 + 8, :]
            first = jnp.where(low, a, pltpu.roll(b, 64, 1))
            second = jnp.where(low, pltpu.roll(a, 64, 1), b)
            put_table(table, c, t, first, second)


def first_own_kernel(gathered, coh, vis, pairs, z_ref, w_ref, s_ref, table, near, far):
    start_table(gathered, table)
    model(lambda i: (coh, i * 16), vis, pairs, 0, z_ref, w_ref, s_ref, table, near, far)


def own_kernel(gathered, coh, vis, pairs, z_ref, w_ref, s_ref, table, near, far):
    step_table(gathered, table)
    model(lambda i: (coh, i * 16), vis, pairs, 0, z_ref, w_ref, s_ref, table, near, far)


def other_kernel(table, recv_0, recv_1, recv_2, recv_3, z_ref, w_ref, s_ref, near, far):
    received = (recv_0, recv_1, recv_2, recv_3)
    model(lambda i: (received[i // 2], (i % 2) * 16), None, recv_3, 32, z_ref, w_ref, s_ref, table, near, far)


def other_after_kernel(table, recv_0, recv_1, recv_2, recv_3, after, *rest):
    other_kernel(table, recv_0, recv_1, recv_2, recv_3, *rest)


def first_other_kernel(
    table, recv_0, recv_1, recv_2, recv_3, state_keep, rho_a, z_ref, w_ref, s_ref, gains, duals, target, near, far
):
    received = (recv_0, recv_1, recv_2, recv_3)
    half_rho = 0.5 * rho_a[...]
    for c in range(8):
        at = c * 8
        state = [
            state_keep[which * 64 + at:which * 64 + at + 8, :]
            + received[which][32:40, c * 128:(c + 1) * 128]
            for which in range(3)
        ]
        gains[at:at + 8, :] = state[0]
        duals[at:at + 8, :] = state[1]
        target[at:at + 8, :] = half_rho * state[2] - 0.5 * state[1]
    other_kernel(table, *received, z_ref, w_ref, s_ref, near, far)


def model(coh_at, vis, pairs, first, z_ref, w_ref, s_ref, table, near, far):
    for j in range(ROWS // BLOCK):
        for side, dest in ((0, near), (1, far)):
            both = jnp.dot(table[...], one_hot(pairs, first, side, j), preferred_element_type=F32)
            dest[j % 2] = both[:128] + both[128:]
        for l in range(BLOCK // 128):
            at = j * BLOCK + l * 128

            def coherency(i):
                ref, row = coh_at(i)
                return ref[row:row + 16, at:at + 128]

            gp = matrix(lambda i: near[j % 2, i * 16:(i + 1) * 16, l * 128:(l + 1) * 128])
            gq = matrix(lambda i: far[j % 2, i * 16:(i + 1) * 16, l * 128:(l + 1) * 128])
            cc = matrix(coherency)
            z = product_nh(cc, gq)
            w = product(gp, cc)
            m = product(gp, z)
            for i in range(8):
                z_ref[i * 16:(i + 1) * 16, at:at + 128] = z[i // 4][i % 4]
                w_ref[i * 16:(i + 1) * 16, at:at + 128] = w[i // 4][i % 4]
                total = -jnp.sum(m[i // 4][i % 4], axis=0, keepdims=True)
                if vis is not None:
                    total = total + vis[i:i + 1, at:at + 128]
                s_ref[i:i + 1, at:at + 128] = total


def message_sums_kernel(
    z_ref, w_ref, s_here, s_there, pairs, before, moment, moment_z, out, part_0, part_1, part_2, part_3, left, acc, hot
):
    chan = lax.axis_index("chan")
    near = weigh(basis_at(chan))
    far = weigh(basis_at(chan ^ 4))
    own = comps(moment)
    other = comps(moment_z)
    for d, part in enumerate((part_0, part_1, part_2, part_3)):
        at = basis_at(chan ^ d)
        near_weight = dot_terms(at, near)
        far_weight = dot_terms(at, far)
        put(part, [near_weight * own[c] + far_weight * other[c] for c in range(8)])
    sums_own_kernel(z_ref, w_ref, s_here, s_there, pairs, before, out, left, acc, hot)


def half_sums(z_ref, w_ref, s_here, s_there, pairs, first, before, left, acc, hot):
    steps = ROWS // BLOCK
    for j in range(steps):
        for l in range(BLOCK // 128):
            src = j * BLOCK + l * 128
            r = matrix(lambda i: s_here[i:i + 1, src:src + 128] + s_there[i:i + 1, src:src + 128])
            z = matrix(lambda i: z_ref[i * 16:(i + 1) * 16, src:src + 128])
            w = matrix(lambda i: w_ref[i * 16:(i + 1) * 16, src:src + 128])
            for side, (num, den) in enumerate(
                ((product_nh(r, z), square_nh(z)), (product_hn(r, w), square_hn(w)))
            ):
                at = side * BLOCK + l * 128
                for i, value in enumerate(num[0] + num[1] + den):
                    high, rest = split_parts(value)
                    left[j, i * 16:(i + 1) * 16, at:at + 128] = high
                    left[j, 192 + i * 16:192 + (i + 1) * 16, at:at + 128] = rest
        for side in range(2):
            hot[j, :, side * BLOCK:(side + 1) * BLOCK] = one_hot(pairs, first, side, j)
        total = lax.dot_general(left[j], hot[j], (((1,), (1,)), ((), ())), preferred_element_type=F32)
        if j == 0:
            acc[...] = total if before is None else before[...] + total
        else:
            acc[...] += total


def sums_other_kernel(z_ref, w_ref, s_here, s_there, recv_3, acc, left, hot):
    half_sums(z_ref, w_ref, s_here, s_there, recv_3, 32, None, left, acc, hot)


def sums_own_kernel(z_ref, w_ref, s_here, s_there, pairs, before, out, left, acc, hot):
    half_sums(z_ref, w_ref, s_here, s_there, pairs, 0, before, left, acc, hot)
    low = lanes() < 64
    for c in range(12):
        for t in range(4):
            cols = slice(t * 128, (t + 1) * 128)
            at = c * 16
            v0 = acc[at:at + 8, cols] + acc[192 + at:192 + at + 8, cols]
            v1 = acc[at + 8:at + 16, cols] + acc[192 + at + 8:192 + at + 16, cols]
            out[(2 * t) * 96 + c * 8:(2 * t) * 96 + c * 8 + 8, :] = jnp.where(low, v0, pltpu.roll(v1, 64, 1))
            out[(2 * t + 1) * 96 + c * 8:(2 * t + 1) * 96 + c * 8 + 8, :] = jnp.where(low, pltpu.roll(v0, 64, 1), v1)


def updated(received, gains, target, rho):
    sums = []
    for c in range(12):
        parts = [received[d * 96 + c * 8:d * 96 + c * 8 + 8, :] for d in range(8)]
        while len(parts) > 1:
            parts = [parts[i] + parts[i + 1] for i in range(0, len(parts), 2)]
        sums.append(parts[0])
    half_rho = 0.5 * rho
    a, d, br, bi = sums[8] + half_rho, sums[9] + half_rho, sums[10], sums[11]
    scale = 0.5 / (a * d - br * br - bi * bi)
    n = [sums[i] + target[i] - half_rho * gains[i] for i in range(8)]
    result = [None] * 8
    for i in (0, 1):
        r0, r1, i0, i1 = n[2 * i], n[2 * i + 1], n[4 + 2 * i], n[5 + 2 * i]
        result[2 * i] = gains[2 * i] + scale * (r0 * d - (r1 * br + i1 * bi))
        result[4 + 2 * i] = gains[4 + 2 * i] + scale * (i0 * d - (i1 * br - r1 * bi))
        result[2 * i + 1] = gains[2 * i + 1] + scale * (r1 * a - (r0 * br - i0 * bi))
        result[5 + 2 * i] = gains[5 + 2 * i] + scale * (i1 * a - (i0 * br + r0 * bi))
    return result


def comps(ref):
    return [ref[c * 8:(c + 1) * 8, :] for c in range(8)]


def put(ref, values, base=0):
    for c in range(8):
        ref[base + c * 8:base + (c + 1) * 8, :] = values[c]


def update_kernel(received, gains, target, rho_a, gains_new, spread):
    new = updated(received, comps(gains), comps(target), rho_a[...])
    put(gains_new, new)
    for d in range(8):
        put(spread, new, d * 64)


def update_moment_kernel(received, gains, target, duals, rho_a, gains_new, spread, moment):
    rho = rho_a[...]
    new = updated(received, comps(gains), comps(target), rho)
    put(gains_new, new)
    for d in range(8):
        put(spread, new, d * 64)
    old = comps(duals)
    put(moment, [old[c] + rho * new[c] for c in range(8)])


def update_consensus_kernel(
    received, gains, part_0, part_1, part_2, part_3, duals, rho_a, gains_new, spread, duals_new, target
):
    rho = rho_a[...]
    old_gains = comps(gains)
    old_duals = comps(duals)
    parts = [comps(part) for part in (part_0, part_1, part_2, part_3)]
    fitted = [(parts[0][c] + parts[1][c]) + (parts[2][c] + parts[3][c]) for c in range(8)]
    new_duals = [old_duals[c] + rho * (old_gains[c] - fitted[c]) for c in range(8)]
    aim = [0.5 * (rho * fitted[c] - new_duals[c]) for c in range(8)]
    put(duals_new, new_duals)
    put(target, aim)
    new = updated(received, old_gains, aim, rho)
    put(gains_new, new)
    for d in range(8):
        put(spread, new, d * 64)


def update_last_kernel(received, gains, target, duals, rho_a, keep, send, moment):
    core = lax.axis_index("core")
    rho = rho_a[...]
    new = updated(received, comps(gains), comps(target), rho)
    old = comps(duals)
    lane = lanes()
    quarter = lane // 32
    whole = [old[c] + rho * new[c] for c in range(8)]
    for half in range(2):
        for c in range(4):
            total = jnp.zeros((8, 128), F32)
            for im in range(2):
                for h in range(2):
                    here = jnp.where(quarter == 2 * h + half, whole[im * 4 + c], 0.0)
                    shift = (im * 64 - 32 * h - 32 * half) % 128
                    total = total + (pltpu.roll(here, shift, 1) if shift else here)
            for f in range(CHANNELS):
                at = (2 * f + half) * 32 + c * 8
                moment[at:at + 8, :] = total
    for out, stations in ((keep, core), (send, 1 - core)):
        for base, values in ((0, new), (64, old)):
            for c in range(8):
                total = jnp.zeros((8, 128), F32)
                for h in range(2):
                    here = jnp.where(quarter == 2 * h + stations, values[c], 0.0)
                    total = total + pltpu.roll(here, (64 * core + 96 * stations + 96 * h) % 128, 1)
                out[base + c * 8:base + (c + 1) * 8, :] = total


def finish_kernel(
    moments, keep, recv, rho_f, gains_hbm, duals_hbm, poly_hbm, gains, duals, poly, thin, deep, sems
):
    chan = lax.axis_index("chan")
    rho = rho_f[...]
    low = lanes() < 64

    def place(ref, value, first, stride):
        for q in range(4):
            part = pltpu.roll(value, 128 - 32 * q, 1) if q else value
            ref[pl.ds(q * 8 * stride + first, 8, stride=stride), :] = part

    now = [keep[c * 8:(c + 1) * 8, :] + recv[c * 8:(c + 1) * 8, :] for c in range(16)]
    for c in range(8):
        place(thin, now[c], c, 8)
    gains[...] = thin[0:256, 0:32].reshape(32, 8, 32)
    stores = [pltpu.make_async_copy(gains, gains_hbm, sems.at[0])]
    stores[0].start()
    at = basis_at(chan)
    fitted = [None] * 8
    terms = []
    for t in range(TERMS):
        halves = []
        for half in range(2):
            for c in range(4):
                total = None
                for f in range(CHANNELS):
                    row = f * 64 + half * 32 + c * 8
                    part = float(SOLVE[t, f]) * moments[row:row + 8, :]
                    total = part if total is None else total + part
                halves.append(total)
        real = [jnp.where(low, halves[c], pltpu.roll(halves[4 + c], 64, 1)) for c in range(4)]
        imag = [jnp.where(low, pltpu.roll(halves[c], 64, 1), halves[4 + c]) for c in range(4)]
        terms.append(real + imag)
        for c, value in enumerate(real + imag):
            fitted[c] = value if t == 0 else fitted[c] + at[t] * value
    for c in range(8):
        place(thin, now[8 + c] + rho * (now[c] - fitted[c]), c, 8)
    duals[...] = thin[0:256, 0:32].reshape(32, 8, 32)
    stores.append(pltpu.make_async_copy(duals, duals_hbm, sems.at[1]))
    stores[1].start()
    for q in range(4):
        for t in range(TERMS):
            for c in range(8):
                part = pltpu.roll(terms[t][c], 128 - 32 * q, 1) if q else terms[t][c]
                deep[pl.ds(q * 256 + c * 4 + t, 8, stride=32), :] = part
        dirs = pl.ds(q * 8, 8)
        poly[dirs] = deep[q * 256:(q + 1) * 256, 0:32].reshape(8, 8, TERMS, 32)
        stores.append(pltpu.make_async_copy(poly.at[dirs], poly_hbm.at[dirs], sems.at[2 + q]))
        stores[-1].start()
    for store in stores:
        store.wait()


def local(coherency, visibilities, station_pairs, gains, duals, poly, penalty):
    def swap(x):
        return lax.ppermute(x, "core", CORE_SWAP)

    def exchange(x, axis):
        return lax.all_to_all(x, axis, 0, 0, tiled=True)

    packed = ((64, 128), F32)
    wide = ((512, 128), F32)
    small = ((8, 128), F32)
    state_in = pltpu.VMEM((32, 8, 32), F32)
    thin = pltpu.VMEM((264, 128), F32)
    spread, mark = call(
        spread_kernel, [wide, small], [thin], n_in=1
    )(gains[0])
    gathered = exchange(spread, ("st", "core"))
    coh_keep, state_keep, rho_a, rho_f, *send = call(
        prepare_kernel,
        [((128, ROWS), F32), ((192, 128), F32), small, small] + [((40, ROWS), F32)] * 4,
        [
            pltpu.VMEM((32, 8, ROWS), BF16), state_in, state_in, pltpu.VMEM((32, 8, TERMS, 32), F32),
            pltpu.VMEM((ROWS // 128, 264, 128), F32), thin, pltpu.SemaphoreType.DMA((4,)),
        ],
        hbm=(0, 1, 2, 3, 4), n_in=7,
    )(mark, coherency[0], gains[0], duals[0], poly, station_pairs, jnp.pad(penalty, (0, 96)).reshape(1, 128))
    received = [swap(x) for x in send]
    vis = visibilities[0]

    half_outs = [((128, ROWS), F32), ((128, ROWS), F32), ((8, ROWS), F32)]
    table_out = ((256, STATIONS), BF16)
    pair_scratch = [pltpu.VMEM((2, 128, BLOCK), F32)] * 2
    sums_out = ((768, 128), F32)
    blocks = ROWS // BLOCK
    left = pltpu.VMEM((blocks, 384, 2 * BLOCK), BF16)
    hot = pltpu.VMEM((blocks, STATIONS, 2 * BLOCK), BF16)
    total = pltpu.VMEM((384, STATIONS), F32)

    *own, table = call(first_own_kernel, half_outs + [table_out], pair_scratch, n_in=4)(
        gathered, coh_keep, vis, station_pairs
    )
    *other, gain, dual, target = call(
        first_other_kernel, half_outs + [packed, packed, packed], pair_scratch, n_in=7
    )(table, *received, state_keep, rho_a)

    def step_model(spread, *after):
        *own, table = call(own_kernel, half_outs + [table_out], pair_scratch, n_in=4)(
            exchange(spread, "st"), coh_keep, vis, station_pairs
        )
        kernel = other_after_kernel if after else other_kernel
        other = call(kernel, half_outs, pair_scratch, hbm=(5,), n_in=5 + len(after))(table, *received, *after)
        return own, other

    def step_sums(own, other, kernel=sums_own_kernel, outs=(), extra=()):
        from_own = swap(own[2])
        from_other = swap(other[2])
        (before,) = call(sums_other_kernel, [((384, STATIONS), F32)], [left, hot], n_in=5)(
            *other, from_own, received[3]
        )
        return call(kernel, [sums_out, *outs], [left, total, hot], n_in=6 + len(extra))(
            *own, from_other, station_pairs, before, *extra
        )

    def step(own, other):
        return exchange(step_sums(own, other)[0], "st")

    gain, spread = call(update_kernel, [packed, wide], n_in=4)(step(own, other), gain, target, rho_a)
    gain, spread, moment = call(update_moment_kernel, [packed, wide, packed], n_in=5)(
        step(*step_model(spread)), gain, target, dual, rho_a
    )

    def from_channel(x, distance):
        return lax.ppermute(x, "chan", [(f, f ^ distance) for f in range(CHANNELS)])

    moment_z = from_channel(moment, 4)
    parts, *messages = step_sums(
        *step_model(spread, moment_z), message_sums_kernel, [packed] * 4, (moment, moment_z)
    )
    shares = [messages[0]] + [from_channel(messages[d], d) for d in (2, 1, 3)]
    gain, spread, dual, target = call(update_consensus_kernel, [packed, wide, packed, packed], n_in=8)(
        exchange(parts, "st"), gain, *shares, dual, rho_a
    )
    keep, send, moment = call(update_last_kernel, [((128, 128), F32), ((1024, 128), F32), wide], n_in=5)(
        step(*step_model(spread)), gain, target, dual, rho_a
    )
    moments = exchange(moment, ("chan", "core"))
    gains_out, duals_out, poly_out = call(
        finish_kernel,
        [((32, 8, 32), F32), ((32, 8, 32), F32), ((32, 8, 4, 32), F32)],
        [
            state_in, state_in, pltpu.VMEM((32, 8, TERMS, 32), F32),
            thin, pltpu.VMEM((1056, 128), F32), pltpu.SemaphoreType.DMA((6,)),
        ],
        hbm_out=(0, 1, 2), n_in=4,
    )(moments, keep, swap(send), rho_f)
    return gains_out[None], duals_out[None], poly_out


def solution(mesh):
    chan, bl = mesh.devices.shape
    finer = Mesh(mesh.devices.reshape(chan, bl // 2, 2), ("chan", "st", "core"))
    both = ("st", "core")
    in_specs = (
        P("chan", None, None, both),
        P("chan", None, both),
        P(None, both),
        P("chan", None, None, both),
        P("chan", None, None, both),
        P(None, None, None, both),
        P(),
    )
    out_specs = (
        P("chan", None, None, both),
        P("chan", None, None, both),
        P(None, None, None, both),
    )
    return jax.shard_map(local, mesh=finer, in_specs=in_specs, out_specs=out_specs, check_vma=False)
```

```python
import jax
import jax.numpy as jnp
import numpy as np
from jax import lax
from jax.experimental import pallas as pl
from jax.experimental.pallas import tpu as pltpu
from jax.sharding import Mesh, PartitionSpec as P


CHANNELS = 8
TERMS = 4
ROWS = 1024
BLOCK = 256
STATIONS = 512
F32 = jnp.float32
BF16 = jnp.bfloat16
CORE_SWAP = [(0, 1), (1, 0)]
VMEM_BYTES = 24 * 1024 * 1024


def basis_of(place):
    square = place * place
    return [1.0 + 0.0 * place, place, 1.5 * square - 0.5, (2.5 * square - 1.5) * place]


def consensus_tables():
    basis = np.stack(basis_of((2.0 * np.arange(CHANNELS) + 1.0) / CHANNELS - 1.0), axis=1)
    inverse = np.linalg.inv(basis.T @ basis)
    return inverse, inverse @ basis.T


GRAM_INVERSE, SOLVE = consensus_tables()


def basis_at(channel):
    place = (2.0 * jnp.full((8, 128), channel, jnp.int32).astype(F32) + 1.0) / CHANNELS - 1.0
    return basis_of(place)


def dot_terms(a, b):
    total = a[0] * b[0]
    for t in range(1, TERMS):
        total = total + a[t] * b[t]
    return total


def weigh(values):
    return [
        sum(float(GRAM_INVERSE[t, u]) * values[u] for u in range(t % 2, TERMS, 2)) for t in range(TERMS)
    ]


def call(kernel, out_shapes, scratch=(), hbm=(), hbm_out=(), n_in=0):
    def specs(count, outside):
        return [pl.BlockSpec(memory_space=pl.ANY if i in outside else pltpu.VMEM) for i in range(count)]

    return pl.pallas_call(
        kernel,
        out_shape=[jax.ShapeDtypeStruct(s, d) for s, d in out_shapes],
        in_specs=specs(n_in, hbm),
        out_specs=specs(len(out_shapes), hbm_out),
        scratch_shapes=list(scratch),
        compiler_params=pltpu.CompilerParams(vmem_limit_bytes=VMEM_BYTES),
        cost_estimate=pl.CostEstimate(flops=0, bytes_accessed=1000, transcendentals=0),
    )


def lanes():
    return lax.broadcasted_iota(jnp.int32, (8, 128), 1)


def split_parts(x):
    high = x.astype(BF16)
    return high, (x - high.astype(F32)).astype(BF16)


def matrix(load):
    return [load(i) for i in range(4)], [load(4 + i) for i in range(4)]


def conj_t(m):
    re, im = m
    return [re[0], re[2], re[1], re[3]], [-im[0], -im[2], -im[1], -im[3]]


def product_nh(a, b):
    (ar, ai), (br, bi) = a, b
    re, im = [], []
    for i in (0, 1):
        for j in (0, 1):
            p, q, u, v = 2 * i, 2 * i + 1, 2 * j, 2 * j + 1
            re.append((ar[p] * br[u] + ai[p] * bi[u]) + (ar[q] * br[v] + ai[q] * bi[v]))
            im.append((ai[p] * br[u] - ar[p] * bi[u]) + (ai[q] * br[v] - ar[q] * bi[v]))
    return re, im


def product_hn(a, b):
    (ar, ai), (br, bi) = a, b
    re, im = [], []
    for i in (0, 1):
        for j in (0, 1):
            p, q, u, v = i, 2 + i, j, 2 + j
            re.append((ar[p] * br[u] + ai[p] * bi[u]) + (ar[q] * br[v] + ai[q] * bi[v]))
            im.append((ar[p] * bi[u] - ai[p] * br[u]) + (ar[q] * bi[v] - ai[q] * br[v]))
    return re, im


def product(a, b):
    (ar, ai), (br, bi) = a, b
    re, im = [], []
    for i in (0, 1):
        for j in (0, 1):
            p, q, u, v = 2 * i, 2 * i + 1, j, 2 + j
            re.append((ar[p] * br[u] - ai[p] * bi[u]) + (ar[q] * br[v] - ai[q] * bi[v]))
            im.append((ar[p] * bi[u] + ai[p] * br[u]) + (ar[q] * bi[v] + ai[q] * br[v]))
    return re, im


def square_nh(a):
    r, i = a
    return [
        (r[0] * r[0] + i[0] * i[0]) + (r[1] * r[1] + i[1] * i[1]),
        (r[2] * r[2] + i[2] * i[2]) + (r[3] * r[3] + i[3] * i[3]),
        (r[0] * r[2] + i[0] * i[2]) + (r[1] * r[3] + i[1] * i[3]),
        (i[0] * r[2] - r[0] * i[2]) + (i[1] * r[3] - r[1] * i[3]),
    ]


def square_hn(a):
    r, i = a
    return [
        (r[0] * r[0] + i[0] * i[0]) + (r[2] * r[2] + i[2] * i[2]),
        (r[1] * r[1] + i[1] * i[1]) + (r[3] * r[3] + i[3] * i[3]),
        (r[0] * r[1] + i[0] * i[1]) + (r[2] * r[3] + i[2] * i[3]),
        (r[0] * i[1] - i[0] * r[1]) + (r[2] * i[3] - i[2] * r[3]),
    ]


def spread_kernel(gains, spread, mark, thin):
    thin[...] = jnp.zeros((264, 128), F32)
    mark[...] = jnp.zeros((8, 128), F32)
    thin[0:256, 0:32] = gains[...].reshape(256, 32)
    for half in range(2):
        for c in range(4):
            total = None
            for im in range(2):
                for h in range(2):
                    part = thin[pl.ds((half * 16 + h * 8) * 8 + im * 4 + c, 8, stride=8), :]
                    if im or h:
                        part = pltpu.roll(part, im * 64 + h * 32, 1)
                    total = part if total is None else total + part
            for d in range(8):
                at = (2 * d + half) * 32 + c * 8
                spread[at:at + 8, :] = total


def prepare_kernel(
    mark, coh_hbm, gains_hbm, duals_hbm, poly_hbm, pairs, penalty,
    coh_keep, state_keep, rho_a, rho_f, send_0, send_1, send_2, send_3,
    coh, gains, duals, poly, wide, thin, sems,
):
    send = (send_0, send_1, send_2, send_3)
    copies = [
        pltpu.make_async_copy(src, dst, sems.at[i])
        for i, (src, dst) in enumerate(((gains_hbm, gains), (duals_hbm, duals), (poly_hbm, poly), (coh_hbm, coh)))
    ]
    for copy in copies:
        copy.start()
    core = lax.axis_index("core")
    chan = lax.axis_index("chan")
    row = lax.broadcasted_iota(jnp.int32, (8, 128), 0)
    lane = lanes()
    given = jnp.broadcast_to(penalty[...], (8, 128))
    column = [jnp.sum(jnp.where(lane == q * 8 + row, given, 0.0), axis=1, keepdims=True) for q in range(4)]
    by_dir = jnp.broadcast_to(column[0], (8, 128))
    for q in range(1, 4):
        by_dir = jnp.where(lane // 32 == q, column[q], by_dir)
    mine = jnp.full((8, 128), core, jnp.int32) == 0
    low = jnp.where(mine, column[0], column[2])
    high = jnp.where(mine, column[1], column[3])
    rho_a[...] = jnp.where(lane < 64, low, high)
    rho_f[...] = by_dir
    send_3[32:40, :] = jnp.zeros((8, ROWS), F32)
    send_3[32:34, :] = pairs[...].astype(F32)

    def pack(which):
        for c in range(8):
            for keep, half in ((True, core), (False, 1 - core)):
                total = None
                for h in range(2):
                    part = thin[pl.ds((half * 16 + h * 8) * 8 + c, 8, stride=8), :]
                    part = pltpu.roll(part, h * 64 + core * 32, 1)
                    total = part if total is None else total + part
                if keep:
                    state_keep[which * 64 + c * 8:which * 64 + (c + 1) * 8, :] = total
                else:
                    send[which][32:40, c * 128:(c + 1) * 128] = total

    thin[...] = jnp.zeros((264, 128), F32)
    copies[0].wait()
    thin[0:256, 0:32] = gains[...].reshape(256, 32)
    pack(0)
    copies[1].wait()
    thin[0:256, 0:32] = duals[...].reshape(256, 32)
    pack(1)
    copies[2].wait()
    place = (2.0 * chan.astype(F32) + 1.0) * (1.0 / CHANNELS) - 1.0
    basis = basis_of(place)
    fitted = poly[:, :, 0, :]
    for t in range(1, TERMS):
        fitted = fitted + poly[:, :, t, :] * basis[t]
    thin[0:256, 0:32] = fitted.reshape(256, 32)
    pack(2)
    copies[3].wait()
    for t in range(ROWS // 128):
        cols = slice(t * 128, (t + 1) * 128)
        wide[t, 0:256, :] = coh[:, :, cols].astype(F32).reshape(256, 128)
        for c in range(8):
            coh_keep[c * 16:(c + 1) * 16, cols] = wide[t, pl.ds(core * 128 + c, 16, stride=8), :]
            send[c // 2][(c % 2) * 16:(c % 2) * 16 + 16, cols] = wide[t, pl.ds((1 - core) * 128 + c, 16, stride=8), :]


def one_hot(pairs, first, side, j):
    index = pairs[first + side:first + side + 1, j * BLOCK:(j + 1) * BLOCK].astype(jnp.int32)
    index = jnp.broadcast_to(index, (16, BLOCK)).astype(jnp.int16)
    index = jnp.concatenate([index] * (STATIONS // 16), axis=0)
    here = lax.broadcasted_iota(jnp.int16, (STATIONS, BLOCK), 0) == index
    return jnp.where(here, jnp.ones((STATIONS, BLOCK), BF16), jnp.zeros((STATIONS, BLOCK), BF16))


def put_table(table, c, t, first, second):
    high, rest = split_parts(jnp.concatenate([first, second], axis=0))
    table[c * 16:(c + 1) * 16, t * 128:(t + 1) * 128] = high
    table[128 + c * 16:128 + (c + 1) * 16, t * 128:(t + 1) * 128] = rest


def start_table(gathered, table):
    lane = lanes()
    for c in range(8):
        im, row = divmod(c, 4)
        for t in range(4):
            halves = []
            for h in range(2):
                total = None
                for b in range(4):
                    part = gathered[(4 * t + b) * 32 + row * 8:(4 * t + b) * 32 + row * 8 + 8, :]
                    shift = (b * 32 - im * 64 - h * 32) % 128
                    if shift:
                        part = pltpu.roll(part, shift, 1)
                    total = part if total is None else jnp.where(lane // 32 == b, part, total)
                halves.append(total)
            put_table(table, c, t, *halves)


def step_table(gathered, table):
    low = lanes() < 64
    for c in range(8):
        for t in range(4):
            a = gathered[(2 * t) * 64 + c * 8:(2 * t) * 64 + c * 8 + 8, :]
            b = gathered[(2 * t + 1) * 64 + c * 8:(2 * t + 1) * 64 + c * 8 + 8, :]
            first = jnp.where(low, a, pltpu.roll(b, 64, 1))
            second = jnp.where(low, pltpu.roll(a, 64, 1), b)
            put_table(table, c, t, first, second)


def first_own_kernel(gathered, coh, vis, pairs, z_ref, w_ref, s_ref, table, near, far):
    start_table(gathered, table)
    model(lambda i: (coh, i * 16), vis, pairs, 0, z_ref, w_ref, s_ref, table, near, far)


def own_kernel(gathered, coh, vis, pairs, z_ref, w_ref, s_ref, table, near, far):
    step_table(gathered, table)
    model(lambda i: (coh, i * 16), vis, pairs, 0, z_ref, w_ref, s_ref, table, near, far)


def other_kernel(table, recv_0, recv_1, recv_2, recv_3, z_ref, w_ref, s_ref, near, far):
    received = (recv_0, recv_1, recv_2, recv_3)
    model(lambda i: (received[i // 2], (i % 2) * 16), None, recv_3, 32, z_ref, w_ref, s_ref, table, near, far)


def other_after_kernel(table, recv_0, recv_1, recv_2, recv_3, after, *rest):
    other_kernel(table, recv_0, recv_1, recv_2, recv_3, *rest)


def first_other_kernel(
    table, recv_0, recv_1, recv_2, recv_3, state_keep, rho_a, z_ref, w_ref, s_ref, gains, duals, target, near, far
):
    received = (recv_0, recv_1, recv_2, recv_3)
    half_rho = 0.5 * rho_a[...]
    for c in range(8):
        at = c * 8
        state = [
            state_keep[which * 64 + at:which * 64 + at + 8, :]
            + received[which][32:40, c * 128:(c + 1) * 128]
            for which in range(3)
        ]
        gains[at:at + 8, :] = state[0]
        duals[at:at + 8, :] = state[1]
        target[at:at + 8, :] = half_rho * state[2] - 0.5 * state[1]
    other_kernel(table, *received, z_ref, w_ref, s_ref, near, far)


def model(coh_at, vis, pairs, first, z_ref, w_ref, s_ref, table, near, far):
    for j in range(ROWS // BLOCK):
        for side, dest in ((0, near), (1, far)):
            both = jnp.dot(table[...], one_hot(pairs, first, side, j), preferred_element_type=F32)
            dest[j % 2] = both[:128] + both[128:]
        for l in range(BLOCK // 128):
            at = j * BLOCK + l * 128

            def coherency(i):
                ref, row = coh_at(i)
                return ref[row:row + 16, at:at + 128]

            gp = matrix(lambda i: near[j % 2, i * 16:(i + 1) * 16, l * 128:(l + 1) * 128])
            gq = matrix(lambda i: far[j % 2, i * 16:(i + 1) * 16, l * 128:(l + 1) * 128])
            cc = matrix(coherency)
            z = product_nh(cc, gq)
            w = product(gp, cc)
            m = product(gp, z)
            for i in range(8):
                z_ref[i * 16:(i + 1) * 16, at:at + 128] = z[i // 4][i % 4]
                w_ref[i * 16:(i + 1) * 16, at:at + 128] = w[i // 4][i % 4]
                total = -jnp.sum(m[i // 4][i % 4], axis=0, keepdims=True)
                if vis is not None:
                    total = total + vis[i:i + 1, at:at + 128]
                s_ref[i:i + 1, at:at + 128] = total


def message_sums_kernel(
    z_ref, w_ref, s_here, s_there, pairs, before, moment, moment_z, out, part_0, part_1, part_2, part_3, left, acc, hot
):
    chan = lax.axis_index("chan")
    near = weigh(basis_at(chan))
    far = weigh(basis_at(chan ^ 4))
    own = comps(moment)
    other = comps(moment_z)
    for d, part in enumerate((part_0, part_1, part_2, part_3)):
        at = basis_at(chan ^ d)
        near_weight = dot_terms(at, near)
        far_weight = dot_terms(at, far)
        put(part, [near_weight * own[c] + far_weight * other[c] for c in range(8)])
    sums_own_kernel(z_ref, w_ref, s_here, s_there, pairs, before, out, left, acc, hot)


def half_sums(z_ref, w_ref, s_here, s_there, pairs, first, before, left, acc, hot):
    steps = ROWS // BLOCK
    for j in range(steps):
        for l in range(BLOCK // 128):
            src = j * BLOCK + l * 128
            r = matrix(lambda i: s_here[i:i + 1, src:src + 128] + s_there[i:i + 1, src:src + 128])
            z = matrix(lambda i: z_ref[i * 16:(i + 1) * 16, src:src + 128])
            w = matrix(lambda i: w_ref[i * 16:(i + 1) * 16, src:src + 128])
            for side, (num, den) in enumerate(
                ((product_nh(r, z), square_nh(z)), (product_hn(r, w), square_hn(w)))
            ):
                at = side * BLOCK + l * 128
                for i, value in enumerate(num[0] + num[1] + den):
                    high, rest = split_parts(value)
                    left[j, i * 16:(i + 1) * 16, at:at + 128] = high
                    left[j, 192 + i * 16:192 + (i + 1) * 16, at:at + 128] = rest
        for side in range(2):
            hot[j, :, side * BLOCK:(side + 1) * BLOCK] = one_hot(pairs, first, side, j)
        total = lax.dot_general(left[j], hot[j], (((1,), (1,)), ((), ())), preferred_element_type=F32)
        if j == 0:
            acc[...] = total if before is None else before[...] + total
        else:
            acc[...] += total


def sums_other_kernel(z_ref, w_ref, s_here, s_there, recv_3, acc, left, hot):
    half_sums(z_ref, w_ref, s_here, s_there, recv_3, 32, None, left, acc, hot)


def sums_own_kernel(z_ref, w_ref, s_here, s_there, pairs, before, out, left, acc, hot):
    half_sums(z_ref, w_ref, s_here, s_there, pairs, 0, before, left, acc, hot)
    low = lanes() < 64
    for c in range(12):
        for t in range(4):
            cols = slice(t * 128, (t + 1) * 128)
            at = c * 16
            v0 = acc[at:at + 8, cols] + acc[192 + at:192 + at + 8, cols]
            v1 = acc[at + 8:at + 16, cols] + acc[192 + at + 8:192 + at + 16, cols]
            out[(2 * t) * 96 + c * 8:(2 * t) * 96 + c * 8 + 8, :] = jnp.where(low, v0, pltpu.roll(v1, 64, 1))
            out[(2 * t + 1) * 96 + c * 8:(2 * t + 1) * 96 + c * 8 + 8, :] = jnp.where(low, pltpu.roll(v0, 64, 1), v1)


def updated(received, gains, target, rho):
    sums = []
    for c in range(12):
        parts = [received[d * 96 + c * 8:d * 96 + c * 8 + 8, :] for d in range(8)]
        while len(parts) > 1:
            parts = [parts[i] + parts[i + 1] for i in range(0, len(parts), 2)]
        sums.append(parts[0])
    half_rho = 0.5 * rho
    a, d, br, bi = sums[8] + half_rho, sums[9] + half_rho, sums[10], sums[11]
    scale = 0.5 / (a * d - br * br - bi * bi)
    n = [sums[i] + target[i] - half_rho * gains[i] for i in range(8)]
    result = [None] * 8
    for i in (0, 1):
        r0, r1, i0, i1 = n[2 * i], n[2 * i + 1], n[4 + 2 * i], n[5 + 2 * i]
        result[2 * i] = gains[2 * i] + scale * (r0 * d - (r1 * br + i1 * bi))
        result[4 + 2 * i] = gains[4 + 2 * i] + scale * (i0 * d - (i1 * br - r1 * bi))
        result[2 * i + 1] = gains[2 * i + 1] + scale * (r1 * a - (r0 * br - i0 * bi))
        result[5 + 2 * i] = gains[5 + 2 * i] + scale * (i1 * a - (i0 * br + r0 * bi))
    return result


def comps(ref):
    return [ref[c * 8:(c + 1) * 8, :] for c in range(8)]


def put(ref, values, base=0):
    for c in range(8):
        ref[base + c * 8:base + (c + 1) * 8, :] = values[c]


def update_kernel(received, gains, target, rho_a, gains_new, spread):
    new = updated(received, comps(gains), comps(target), rho_a[...])
    put(gains_new, new)
    for d in range(8):
        put(spread, new, d * 64)


def update_moment_kernel(received, gains, target, duals, rho_a, gains_new, spread, moment):
    rho = rho_a[...]
    new = updated(received, comps(gains), comps(target), rho)
    put(gains_new, new)
    for d in range(8):
        put(spread, new, d * 64)
    old = comps(duals)
    put(moment, [old[c] + rho * new[c] for c in range(8)])


def update_consensus_kernel(
    received, gains, part_0, part_1, part_2, part_3, duals, rho_a, gains_new, spread, duals_new, target
):
    rho = rho_a[...]
    old_gains = comps(gains)
    old_duals = comps(duals)
    parts = [comps(part) for part in (part_0, part_1, part_2, part_3)]
    fitted = [(parts[0][c] + parts[1][c]) + (parts[2][c] + parts[3][c]) for c in range(8)]
    new_duals = [old_duals[c] + rho * (old_gains[c] - fitted[c]) for c in range(8)]
    aim = [0.5 * (rho * fitted[c] - new_duals[c]) for c in range(8)]
    put(duals_new, new_duals)
    put(target, aim)
    new = updated(received, old_gains, aim, rho)
    put(gains_new, new)
    for d in range(8):
        put(spread, new, d * 64)


def update_last_kernel(received, gains, target, duals, rho_a, keep, send, moment):
    core = lax.axis_index("core")
    rho = rho_a[...]
    new = updated(received, comps(gains), comps(target), rho)
    old = comps(duals)
    lane = lanes()
    quarter = lane // 32
    whole = [old[c] + rho * new[c] for c in range(8)]
    for half in range(2):
        for c in range(4):
            total = jnp.zeros((8, 128), F32)
            for im in range(2):
                for h in range(2):
                    here = jnp.where(quarter == 2 * h + half, whole[im * 4 + c], 0.0)
                    shift = (im * 64 - 32 * h - 32 * half) % 128
                    total = total + (pltpu.roll(here, shift, 1) if shift else here)
            for f in range(CHANNELS):
                at = (2 * f + half) * 32 + c * 8
                moment[at:at + 8, :] = total
    for out, stations in ((keep, core), (send, 1 - core)):
        for base, values in ((0, new), (64, old)):
            for c in range(8):
                total = jnp.zeros((8, 128), F32)
                for h in range(2):
                    here = jnp.where(quarter == 2 * h + stations, values[c], 0.0)
                    total = total + pltpu.roll(here, (64 * core + 96 * stations + 96 * h) % 128, 1)
                out[base + c * 8:base + (c + 1) * 8, :] = total


def finish_kernel(
    moments, keep, recv, rho_f, gains_hbm, duals_hbm, poly_hbm, gains, duals, poly, thin, deep, sems
):
    chan = lax.axis_index("chan")
    rho = rho_f[...]
    low = lanes() < 64

    def place(ref, value, first, stride):
        for q in range(4):
            part = pltpu.roll(value, 128 - 32 * q, 1) if q else value
            ref[pl.ds(q * 8 * stride + first, 8, stride=stride), :] = part

    now = [keep[c * 8:(c + 1) * 8, :] + recv[c * 8:(c + 1) * 8, :] for c in range(16)]
    for c in range(8):
        place(thin, now[c], c, 8)
    gains[...] = thin[0:256, 0:32].reshape(32, 8, 32)
    stores = [pltpu.make_async_copy(gains, gains_hbm, sems.at[0])]
    stores[0].start()
    at = basis_at(chan)
    fitted = [None] * 8
    terms = []
    for t in range(TERMS):
        halves = []
        for half in range(2):
            for c in range(4):
                total = None
                for f in range(CHANNELS):
                    row = f * 64 + half * 32 + c * 8
                    part = float(SOLVE[t, f]) * moments[row:row + 8, :]
                    total = part if total is None else total + part
                halves.append(total)
        real = [jnp.where(low, halves[c], pltpu.roll(halves[4 + c], 64, 1)) for c in range(4)]
        imag = [jnp.where(low, pltpu.roll(halves[c], 64, 1), halves[4 + c]) for c in range(4)]
        terms.append(real + imag)
        for c, value in enumerate(real + imag):
            fitted[c] = value if t == 0 else fitted[c] + at[t] * value
    for c in range(8):
        place(thin, now[8 + c] + rho * (now[c] - fitted[c]), c, 8)
    duals[...] = thin[0:256, 0:32].reshape(32, 8, 32)
    stores.append(pltpu.make_async_copy(duals, duals_hbm, sems.at[1]))
    stores[1].start()
    for q in range(4):
        for t in range(TERMS):
            for c in range(8):
                part = pltpu.roll(terms[t][c], 128 - 32 * q, 1) if q else terms[t][c]
                deep[pl.ds(q * 256 + c * 4 + t, 8, stride=32), :] = part
        dirs = pl.ds(q * 8, 8)
        poly[dirs] = deep[q * 256:(q + 1) * 256, 0:32].reshape(8, 8, TERMS, 32)
        stores.append(pltpu.make_async_copy(poly.at[dirs], poly_hbm.at[dirs], sems.at[2 + q]))
        stores[-1].start()
    for store in stores:
        store.wait()


def local(coherency, visibilities, station_pairs, gains, duals, poly, penalty):
    def swap(x):
        return lax.ppermute(x, "core", CORE_SWAP)

    def exchange(x, axis):
        return lax.all_to_all(x, axis, 0, 0, tiled=True)

    packed = ((64, 128), F32)
    wide = ((512, 128), F32)
    small = ((8, 128), F32)
    state_in = pltpu.VMEM((32, 8, 32), F32)
    thin = pltpu.VMEM((264, 128), F32)
    spread, mark = call(
        spread_kernel, [wide, small], [thin], n_in=1
    )(gains[0])
    gathered = exchange(spread, ("st", "core"))
    coh_keep, state_keep, rho_a, rho_f, *send = call(
        prepare_kernel,
        [((128, ROWS), F32), ((192, 128), F32), small, small] + [((40, ROWS), F32)] * 4,
        [
            pltpu.VMEM((32, 8, ROWS), BF16), state_in, state_in, pltpu.VMEM((32, 8, TERMS, 32), F32),
            pltpu.VMEM((ROWS // 128, 264, 128), F32), thin, pltpu.SemaphoreType.DMA((4,)),
        ],
        hbm=(0, 1, 2, 3, 4), n_in=7,
    )(mark, coherency[0], gains[0], duals[0], poly, station_pairs, jnp.pad(penalty, (0, 96)).reshape(1, 128))
    received = [swap(x) for x in send]
    vis = visibilities[0]

    half_outs = [((128, ROWS), F32), ((128, ROWS), F32), ((8, ROWS), F32)]
    table_out = ((256, STATIONS), BF16)
    pair_scratch = [pltpu.VMEM((2, 128, BLOCK), F32)] * 2
    sums_out = ((768, 128), F32)
    blocks = ROWS // BLOCK
    left = pltpu.VMEM((blocks, 384, 2 * BLOCK), BF16)
    hot = pltpu.VMEM((blocks, STATIONS, 2 * BLOCK), BF16)
    total = pltpu.VMEM((384, STATIONS), F32)

    *own, table = call(first_own_kernel, half_outs + [table_out], pair_scratch, n_in=4)(
        gathered, coh_keep, vis, station_pairs
    )
    *other, gain, dual, target = call(
        first_other_kernel, half_outs + [packed, packed, packed], pair_scratch, n_in=7
    )(table, *received, state_keep, rho_a)

    def step_model(spread, *after):
        *own, table = call(own_kernel, half_outs + [table_out], pair_scratch, n_in=4)(
            exchange(spread, "st"), coh_keep, vis, station_pairs
        )
        kernel = other_after_kernel if after else other_kernel
        other = call(kernel, half_outs, pair_scratch, hbm=(5,), n_in=5 + len(after))(table, *received, *after)
        return own, other

    def step_sums(own, other, kernel=sums_own_kernel, outs=(), extra=()):
        from_own = swap(own[2])
        from_other = swap(other[2])
        (before,) = call(sums_other_kernel, [((384, STATIONS), F32)], [left, hot], n_in=5)(
            *other, from_own, received[3]
        )
        return call(kernel, [sums_out, *outs], [left, total, hot], n_in=6 + len(extra))(
            *own, from_other, station_pairs, before, *extra
        )

    def step(own, other):
        return exchange(step_sums(own, other)[0], "st")

    gain, spread = call(update_kernel, [packed, wide], n_in=4)(step(own, other), gain, target, rho_a)
    gain, spread, moment = call(update_moment_kernel, [packed, wide, packed], n_in=5)(
        step(*step_model(spread)), gain, target, dual, rho_a
    )

    def from_channel(x, distance):
        return lax.ppermute(x, "chan", [(f, f ^ distance) for f in range(CHANNELS)])

    moment_z = from_channel(moment, 4)
    parts, *messages = step_sums(
        *step_model(spread, moment_z), message_sums_kernel, [packed] * 4, (moment, moment_z)
    )
    shares = [messages[0]] + [from_channel(messages[d], d) for d in (2, 3, 1)]
    gain, spread, dual, target = call(update_consensus_kernel, [packed, wide, packed, packed], n_in=8)(
        exchange(parts, "st"), gain, *shares, dual, rho_a
    )
    keep, send, moment = call(update_last_kernel, [((128, 128), F32), ((1024, 128), F32), wide], n_in=5)(
        step(*step_model(spread)), gain, target, dual, rho_a
    )
    moments = exchange(moment, ("chan", "core"))
    gains_out, duals_out, poly_out = call(
        finish_kernel,
        [((32, 8, 32), F32), ((32, 8, 32), F32), ((32, 8, 4, 32), F32)],
        [
            state_in, state_in, pltpu.VMEM((32, 8, TERMS, 32), F32),
            thin, pltpu.VMEM((1056, 128), F32), pltpu.SemaphoreType.DMA((6,)),
        ],
        hbm_out=(0, 1, 2), n_in=4,
    )(moments, keep, swap(send), rho_f)
    return gains_out[None], duals_out[None], poly_out


def solution(mesh):
    chan, bl = mesh.devices.shape
    finer = Mesh(mesh.devices.reshape(chan, bl // 2, 2), ("chan", "st", "core"))
    both = ("st", "core")
    in_specs = (
        P("chan", None, None, both),
        P("chan", None, both),
        P(None, both),
        P("chan", None, None, both),
        P("chan", None, None, both),
        P(None, None, None, both),
        P(),
    )
    out_specs = (
        P("chan", None, None, both),
        P("chan", None, None, both),
        P(None, None, None, both),
    )
    return jax.shard_map(local, mesh=finer, in_specs=in_specs, out_specs=out_specs, check_vma=False)
```
